256 devices in a mesh: enc: 8 (over z), seq: 16 (over y, x), mp: 2 (over core).
Axes of the slice: x: 4, y: 4, z: 8, core: 2. Of those that a mesh axis runs over, the one named last changes fastest.
Arguments:
- images: bfloat16 [2048, 64, 1280], P(('enc', 'seq', 'mp')), may hold values from -6 to 6
- vit_gain: float32 [1280], replicated, may hold values from 0.5 to 3
- vit_qkv: bfloat16 [1280, 1920], P(('enc', 'mp')), may hold values from -0.15625 to 0.15625
- vit_out: bfloat16 [640, 1280], P(('enc', 'mp')), may hold values from -0.25 to 0.25
- kv_weight: bfloat16 [1280, 1024], P('mp'), may hold values from -0.15625 to 0.15625
- queries: bfloat16 [32768, 4096], P(('enc', 'seq', 'mp')), may hold values from -6 to 6
- q_gain: float32 [128], replicated, may hold values from 0.6 to 3
- k_gain: float32 [128], replicated, may hold values from 0.6 to 3
- out_grad: bfloat16 [32768, 4096], P(('enc', 'seq', 'mp')), may hold values from -6 to 6
- block_image: int32 [2048], P(('enc', 'seq', 'mp')), may hold values from 0 to 7, as said below
- block_dest: int32 [2048], P(('enc', 'seq', 'mp')), may hold values from 0 to 255, as said below
- key_image: int32 [1024, 4], P(('enc', 'seq', 'mp')), may hold values from 0 to 4, as said below
- text_seen: int32 [32768], P(('enc', 'seq', 'mp')), may hold values from 1 to 4, as said below
Outputs:
- attended: bfloat16 [32768, 4096], P(('enc', 'seq', 'mp'))
- kv_grad: bfloat16 [2048, 64, 1024], P(('enc', 'seq', 'mp'))
The draws below stay inside these ranges and needn't reach their ends.
Inputs may be any that keep to these rules, and one draw needn't show every extreme that they name: `block_image`: on each device blocks are numbered by image from 0, rising by one at each new image; an image is one block or the two blocks 2j and 2j+1 of its device. `block_dest`: blocks 2j and 2j+1 of a device go to one device of its seq group; the pairs of a device are spread evenly over the group, so no device sends more than 2 blocks to another and some device sends exactly 2 to some other; every device receives exactly 8 blocks. Every key block receives at most one block; a sequence's blocks fill its first key blocks, 1 to 4 of them, and some sequence holds 4. The blocks of one image go to one sequence, in consecutive key blocks. `key_image`: the image number of a key block within its sequence, counted from 0 in key-block order, or 4 where the key block is empty; it agrees with block_dest and block_image. A text token sees the first text_seen images of its sequence: at least 1, at most the sequence's number of images.
All inputs are finite; a program needn't handle non-finite values.
Results may differ from the reference program's by a relative error of at most 0.034.
The reference program's roundings to bfloat16 on the way count: a program that leaves them out, or rounds other values in their place, can miss the bound.
Values may be sent and summed in bfloat16 or wider, within the bound.
A program may use at most 64 MiB of HBM per device.

```python
import math
import jax
import jax.numpy as jnp
from jax import lax

VIS = 1280
VHEADS = 8
VHEAD = 80
QHEADS = 32
KVHEADS = 4
HEAD = 128
BLK = 64
SEQ_CAP = 4
ENC_BLK = 8
LEN = 32
SEQ_DEV = 4
KSLOTS = 16
KVW = 1024
IMG_BLOCKS = 2048
TEXT = 32768
N_ENC = 8
N_SEQ = 16
N_MP = 2


def arrange_groups(array, tail):
    shaped = array.reshape((N_ENC, N_MP) + array.shape[1:])
    return jnp.swapaxes(shaped, 1, 2).reshape((-1,) + tail)


def routing_tables(key):
    group_count = N_ENC * N_MP
    pair_count = ENC_BLK // 2
    key_slots = pair_count * SEQ_CAP
    group_keys = jax.random.split(jax.random.fold_in(key, 7001), group_count)

    def one_group(group_key):
        subkeys = jax.random.split(group_key, 9)
        perm_rows = jax.random.permutation(subkeys[0], N_SEQ)
        perm_owner = jax.random.permutation(subkeys[1], N_SEQ)
        offsets = jax.random.permutation(subkeys[2], N_SEQ)[jnp.arange(pair_count) % N_SEQ]
        owner_of = perm_owner[(perm_rows[:, None] + offsets[None, :]) % N_SEQ]
        pair_shift = jax.random.randint(subkeys[3], (N_SEQ, pair_count // 2), 0, 2)
        pair_pattern = jnp.stack([pair_shift, -pair_shift], axis=2).reshape(N_SEQ, pair_count)
        heavy_head = jnp.array([2, -1, -1, 0], dtype=jnp.int32)
        heavy_flag = jax.random.randint(subkeys[4], (N_SEQ,), 0, 2)
        forced = jax.random.randint(subkeys[5], (), 0, N_SEQ)
        heavy_flag = jnp.where(jnp.arange(N_SEQ) == forced, 1, heavy_flag)
        leading = jnp.where(heavy_flag[:, None] == 1, heavy_head[None, :], pair_pattern[:, :4])
        pattern = jnp.concatenate([leading, pair_pattern[:, 4:]], axis=1)
        shuffle_score = jax.random.randint(subkeys[6], (N_SEQ, pair_count), 0, 1 << 20) * pair_count + jnp.arange(pair_count)[None, :]
        shuffle = jnp.argsort(shuffle_score, axis=1)
        counts = 2 + jnp.take_along_axis(pattern, shuffle, axis=1)
        seq_end = jnp.cumsum(counts, axis=1)
        seq_begin = seq_end - counts
        position = jnp.arange(ENC_BLK)
        seq_of = jnp.sum(position[None, :, None] >= seq_end[:, None, :], axis=2).astype(jnp.int32)
        begin_of = jnp.take_along_axis(seq_begin, seq_of, axis=1)
        slot_in = position[None, :] - begin_of
        coin_flip = jax.random.randint(subkeys[7], (N_SEQ, pair_count), 0, 2)
        odd_start = jnp.maximum(coin_flip, (slot_in[:, 1::2] == 0).astype(jnp.int32))
        image_start = jnp.stack([jnp.ones_like(odd_start), odd_start], axis=2).reshape(N_SEQ, ENC_BLK)
        running = jnp.cumsum(image_start, axis=1)
        before_image = running - image_start
        image_index = running - jnp.take_along_axis(before_image, begin_of, axis=1) - 1
        image_total = jnp.take_along_axis(running, seq_end - 1, axis=1) - jnp.take_along_axis(before_image, seq_begin, axis=1)
        matches = (seq_of[:, :, None, None] == jnp.arange(pair_count)[None, None, :, None]) & (slot_in[:, :, None, None] == jnp.arange(SEQ_CAP)[None, None, None, :])
        key_image = SEQ_CAP + jnp.sum(jnp.where(matches, image_index[:, :, None, None] - SEQ_CAP, 0), axis=1)
        target = owner_of[:, position // 2]
        destination = target * key_slots + seq_of[target, position[None, :]] * SEQ_CAP + slot_in[target, position[None, :]]
        block_image = jnp.cumsum(image_start[target, position[None, :]], axis=1) - 1
        text_seen = jax.random.randint(subkeys[8], (N_SEQ, pair_count, LEN), 1, image_total[:, :, None] + 1)
        return (block_image, destination, key_image, text_seen)
    block_image, destination, key_image, text_seen = jax.vmap(one_group)(group_keys)
    return (arrange_groups(block_image, ()).astype(jnp.int32), arrange_groups(destination, ()).astype(jnp.int32), arrange_groups(key_image, (SEQ_CAP,)).astype(jnp.int32), arrange_groups(text_seen, ()).astype(jnp.int32))


def draw_block_image(key, part):
    return routing_tables(key)[0]


def draw_block_dest(key, part):
    return routing_tables(key)[1]


def draw_key_image(key, part):
    return routing_tables(key)[2]


def draw_text_seen(key, part):
    return routing_tables(key)[3]


def draw_vit_gain(key, part):
    return jnp.exp(jax.random.uniform(jax.random.fold_in(key, 11), (VIS,), jnp.float32, math.log(0.5), math.log(2.0)))


def draw_q_gain(key, part):
    return jnp.exp(jax.random.uniform(jax.random.fold_in(key, 13), (HEAD,), jnp.float32, math.log(0.6), math.log(1.6)))


def draw_k_gain(key, part):
    return jnp.exp(jax.random.uniform(jax.random.fold_in(key, 17), (HEAD,), jnp.float32, math.log(0.6), math.log(1.6)))


def block_scale(own_key, dims, pieces, smallest, largest):
    gain = 1.0
    for axis_at, shards_of in pieces:
        steps = jax.random.uniform(jax.random.fold_in(jax.random.fold_in(own_key, 6), axis_at), (shards_of,), jnp.float32, smallest / len(pieces), largest / len(pieces))
        gain = gain * jnp.repeat(jnp.exp(steps), dims[axis_at] // shards_of).reshape((-1,) + (1,) * (len(dims) - 1 - axis_at))
    return gain


def scatter_about(rng, shape, width, reach, pieces=(), kind=jnp.bfloat16):
    entries = jax.random.normal(rng, shape, jnp.float32) * width
    if len(pieces) > 0:
        entries = block_scale(rng, shape, pieces, -0.22, 0.18) * entries
    return jnp.clip(entries, min=-reach, max=reach).astype(kind)


def setup_inputs(seed: int = 0) -> dict:
    arg_keys = jax.random.split(jax.random.key(seed), 14)
    return {
        "images": scatter_about(arg_keys[0], (IMG_BLOCKS, BLK, VIS), 1.0, 6.0, ((0, 256),)),
        "vit_gain": draw_vit_gain(jax.random.fold_in(arg_keys[13], 71), 0),
        "vit_qkv": scatter_about(arg_keys[2], (VIS, 3 * VHEADS * VHEAD), VIS ** -0.5, 0.15625, ((0, 16),)),
        "vit_out": scatter_about(arg_keys[3], (VHEADS * VHEAD, VIS), (VHEADS * VHEAD) ** -0.5, 0.25, ((0, 16),)),
        "kv_weight": scatter_about(arg_keys[4], (VIS, KVW), VIS ** -0.5, 0.15625, ((0, 2),)),
        "queries": scatter_about(arg_keys[5], (TEXT, QHEADS * HEAD), 1.0, 6.0, ((0, 256),)),
        "q_gain": draw_q_gain(jax.random.fold_in(arg_keys[13], 71), 0),
        "k_gain": draw_k_gain(jax.random.fold_in(arg_keys[13], 71), 0),
        "out_grad": scatter_about(arg_keys[8], (TEXT, QHEADS * HEAD), 1.0, 6.0, ((0, 256),)),
        "block_image": draw_block_image(jax.random.fold_in(arg_keys[13], 71), 0),
        "block_dest": draw_block_dest(jax.random.fold_in(arg_keys[13], 71), 0),
        "key_image": draw_key_image(jax.random.fold_in(arg_keys[13], 71), 0),
        "text_seen": draw_text_seen(jax.random.fold_in(arg_keys[13], 71), 0),
    }


epsilon = 1e-05

def rounded(values):
    return lax.optimization_barrier(values.astype(jnp.bfloat16)).astype(jnp.float32)

def layer_norm(tokens, gain_vec):
    values = tokens.astype(jnp.float32)
    center = values - lax.optimization_barrier(jnp.mean(values, axis=-1, keepdims=True))
    spread = lax.optimization_barrier(jnp.mean(center * center, axis=-1, keepdims=True))
    return (center * lax.rsqrt(spread + epsilon) * gain_vec).astype(jnp.bfloat16)

def masked_softmax(scores, allowed):
    masked = jnp.where(allowed, scores, -jnp.inf)
    row_max = lax.optimization_barrier(jnp.max(masked, axis=-1, keepdims=True))
    exp_terms = jnp.exp(masked - row_max)
    return exp_terms / lax.optimization_barrier(jnp.sum(exp_terms, axis=-1, keepdims=True))

def encode_device(images_dev, block_image_dev, vit_gain, vit_qkv, vit_out, kv_weight):
    tokens = images_dev.reshape(ENC_BLK * BLK, VIS)
    normed = layer_norm(tokens, vit_gain)
    mixed_qkv = rounded(jnp.dot(normed, vit_qkv, preferred_element_type=jnp.float32))
    heads_view = mixed_qkv.reshape(ENC_BLK * BLK, 3, VHEADS, VHEAD)
    image_of = jnp.repeat(block_image_dev, BLK)
    allowed = (image_of[:, None] == image_of[None, :])[None]
    scores = jnp.einsum('qhd,khd->hqk', heads_view[:, 0], heads_view[:, 1]) * (1.0 / math.sqrt(VHEAD))
    vit_weights = rounded(masked_softmax(scores, allowed))
    vit_attended = jnp.einsum('hqk,khd->qhd', vit_weights, heads_view[:, 2]).astype(jnp.bfloat16)
    vit_attended = vit_attended.reshape(ENC_BLK * BLK, VHEADS * VHEAD)
    residual = tokens.astype(jnp.float32) + jnp.dot(vit_attended, vit_out, preferred_element_type=jnp.float32)
    vit_hidden = residual.astype(jnp.bfloat16)
    token_kv = jnp.dot(vit_hidden, kv_weight, preferred_element_type=jnp.float32).astype(jnp.bfloat16)
    return token_kv.reshape(ENC_BLK, BLK, KVW)

def cross_device(queries_dev, grad_dev, keys_dev, key_image_dev, seen_dev, q_gain, k_gain):
    shared = QHEADS // KVHEADS
    key_rows = SEQ_CAP * BLK
    half_width = KVHEADS * HEAD
    query_f = queries_dev.astype(jnp.float32).reshape(SEQ_DEV, LEN, KVHEADS, shared, HEAD)
    query_inv = lax.rsqrt(lax.optimization_barrier(jnp.mean(query_f * query_f, axis=-1, keepdims=True)) + epsilon)
    query_normed = rounded(query_f * query_inv * q_gain)
    keyval = keys_dev.reshape(SEQ_DEV, key_rows, KVW)
    key_f = keyval[:, :, :half_width].astype(jnp.float32).reshape(SEQ_DEV, key_rows, KVHEADS, HEAD)
    value_f = keyval[:, :, half_width:].astype(jnp.float32).reshape(SEQ_DEV, key_rows, KVHEADS, HEAD)
    inv_key = lax.rsqrt(lax.optimization_barrier(jnp.mean(key_f * key_f, axis=-1, keepdims=True)) + epsilon)
    key_normed = rounded(key_f * inv_key * k_gain)
    scale = 1.0 / math.sqrt(HEAD)
    scores = jnp.einsum('slkgd,smkd->skglm', query_normed, key_normed) * scale
    seen_tok = seen_dev.reshape(SEQ_DEV, LEN)
    key_img = jnp.repeat(key_image_dev, BLK, axis=1)
    allowed = key_img[:, None, None, None, :] < seen_tok[:, None, None, :, None]
    attn_weights = masked_softmax(scores, allowed)
    attn_rounded = rounded(attn_weights)
    attended = jnp.einsum('skglm,smkd->slkgd', attn_rounded, value_f).astype(jnp.bfloat16)
    grad_out = grad_dev.astype(jnp.float32).reshape(SEQ_DEV, LEN, KVHEADS, shared, HEAD)
    grad_values = jnp.einsum('skglm,slkgd->smkd', attn_rounded, grad_out).astype(jnp.bfloat16)
    grad_dot = jnp.einsum('slkgd,smkd->skglm', grad_out, value_f)
    row_delta = lax.optimization_barrier(jnp.sum(attn_weights * grad_dot, axis=-1, keepdims=True))
    grad_scores = rounded(attn_weights * (grad_dot - row_delta) * scale)
    grad_key_normed = jnp.einsum('skglm,slkgd->smkd', grad_scores, query_normed)
    gained = grad_key_normed * k_gain
    grad_keys = inv_key * (gained - key_f * inv_key * inv_key * lax.optimization_barrier(jnp.mean(key_f * gained, axis=-1, keepdims=True)))
    grad_keys = grad_keys.astype(jnp.bfloat16).reshape(SEQ_DEV, key_rows, half_width)
    grad_values = grad_values.reshape(SEQ_DEV, key_rows, half_width)
    grad_kv = jnp.concatenate([grad_keys, grad_values], axis=-1).reshape(KSLOTS, BLK, KVW)
    return (attended.reshape(SEQ_DEV * LEN, QHEADS * HEAD), grad_kv)

def to_groups(array):
    tail = array.shape[1:]
    shaped = array.reshape((N_ENC, N_SEQ, N_MP, -1) + tail)
    return jnp.swapaxes(shaped, 1, 2).reshape((N_ENC * N_MP, N_SEQ, -1) + tail)

def from_groups(array):
    tail = array.shape[3:]
    shaped = array.reshape((N_ENC, N_MP, N_SEQ, array.shape[2]) + tail)
    return jnp.swapaxes(shaped, 1, 2).reshape((-1,) + tail)

def reference(images, vit_gain, vit_qkv, vit_out, kv_weight, queries, q_gain, k_gain, out_grad, block_image, block_dest, key_image, text_seen):

    def encode_one(inputs_dev):
        return encode_device(inputs_dev[0], inputs_dev[1], vit_gain, vit_qkv, vit_out, kv_weight)

    def cross_one(inputs_dev):
        return cross_device(inputs_dev[0], inputs_dev[1], inputs_dev[2], inputs_dev[3], inputs_dev[4], q_gain, k_gain)

    def one_group(inputs_group):
        images_group, image_ids, dest_group, queries_group, grad_group, key_image_group, seen_group = inputs_group
        encoded = lax.map(encode_one, (images_group, image_ids))
        owner_index = dest_group // KSLOTS
        slot_index = dest_group % KSLOTS
        key_blocks = jnp.zeros((N_SEQ, KSLOTS, BLK, KVW), jnp.bfloat16).at[owner_index, slot_index].set(encoded)
        attended_group, grad_kv_group = lax.map(cross_one, (queries_group, grad_group, key_blocks, key_image_group, seen_group))
        return (attended_group, grad_kv_group[owner_index, slot_index])
    attended_all, kv_grad_all = lax.map(one_group, (to_groups(images), to_groups(block_image), to_groups(block_dest), to_groups(queries), to_groups(out_grad), to_groups(key_image), to_groups(text_seen)))
    return (from_groups(attended_all), from_groups(kv_grad_all))
```

```python
import functools
import math

import jax
import jax.numpy as jnp
from jax import lax
from jax.experimental import pallas as pl
from jax.experimental.pallas import tpu as pltpu
from jax.sharding import PartitionSpec as P

VHEADS = 8
VHEAD = 80
HEAD = 128
KVHEADS = 4
SHARED = 8
BLK = 64
LEN = 32
CAP = 4
PEERS = 16
PAIRS = 4
PIECES = 2
PER = KVHEADS // PIECES
WIDE = PER * 2 * HEAD
EPS = 1e-05
MESH = pl.DeviceIdType.MESH
f32 = jnp.float32
bf16 = jnp.bfloat16


def dot_nn(left, right):
    return jnp.dot(left, right, preferred_element_type=f32)


def dot_nt(left, right):
    return lax.dot_general(left, right, (((1,), (1,)), ((), ())), preferred_element_type=f32)


def dot_tn(left, right):
    return lax.dot_general(left, right, (((0,), (0,)), ((), ())), preferred_element_type=f32)


def greet(axis, count, me):
    barrier = pltpu.get_barrier_semaphore()

    def body(step, carry):
        peer = lax.rem(me + step, count)
        pl.semaphore_signal(barrier, inc=1, device_id={axis: peer}, device_id_type=MESH)
        return carry

    lax.fori_loop(1, count, body, 0)
    pl.semaphore_wait(barrier, count - 1)


def exchange(source, target, me, send_sem, recv_sem):
    def body(step, carry):
        peer = lax.rem(me + step, PEERS)
        pltpu.make_async_remote_copy(
            src_ref=source.at[peer],
            dst_ref=target.at[me],
            send_sem=send_sem,
            recv_sem=recv_sem,
            device_id={"seq": peer},
            device_id_type=MESH,
        ).start()
        return carry

    lax.fori_loop(1, PEERS, body, 0)
    target[me] = source[me]


def wait_all(buffer, sem):
    view = buffer.at[pl.ds(0, PEERS - 1)]
    pltpu.make_async_copy(view, view, sem).wait()


def reach_all(step_map, doublings):
    total = None
    power = step_map
    for index in range(doublings):
        if total is None:
            n = step_map.shape[0]
            eye = lax.broadcasted_iota(jnp.int32, (n, n), 0) == lax.broadcasted_iota(
                jnp.int32, (n, n), 1
            )
            total = jnp.where(eye, 1.0, 0.0) + power
        else:
            total = total + dot_nn(total.astype(bf16), power.astype(bf16))
        if index < doublings - 1:
            power = dot_nn(power.astype(bf16), power.astype(bf16))
    return total


def split_colors(src_partner, dst_partner, doublings):
    n = src_partner.shape[0]
    row = lax.broadcasted_iota(jnp.int32, (n, n), 0)
    col = lax.broadcasted_iota(jnp.int32, (n, n), 1)
    src_f = jnp.where(src_partner, 1.0, 0.0)
    dst_f = jnp.where(dst_partner, 1.0, 0.0)
    orbit = reach_all(dot_nn(src_f.astype(bf16), dst_f.astype(bf16)), doublings) > 0.5
    lead_c = jnp.min(jnp.where(orbit, col, n), axis=1, keepdims=True)
    lead_r = jnp.min(jnp.where(orbit, row, n), axis=0, keepdims=True)
    other_c = jnp.sum(jnp.where(src_partner, lead_r, 0), axis=1, keepdims=True)
    other_r = jnp.sum(jnp.where(src_partner, lead_c, 0), axis=0, keepdims=True)
    return (lead_c < other_c).astype(jnp.int32), (lead_r < other_r).astype(jnp.int32)


def color_tables(dest, me):
    n = dest.shape[0]
    row = lax.broadcasted_iota(jnp.int32, (n, n), 0)
    col = lax.broadcasted_iota(jnp.int32, (n, n), 1)
    dest_t = jnp.transpose(dest.astype(f32)).astype(jnp.int32)
    owner_c, owner_r = dest >> 4, dest_t >> 4
    parity_same = (row & 1) == (col & 1)
    src_same = ((row >> 3) == (col >> 3)) & parity_same
    dst_same = (owner_c == owner_r) & parity_same
    rank_c = jnp.sum(jnp.where(dst_same & (col < row), 1, 0), axis=1, keepdims=True)
    rank_r = jnp.sum(jnp.where(dst_same & (row < col), 1, 0), axis=0, keepdims=True)
    src_partner = col == (row ^ 2)
    dst_partner = dst_same & (rank_r == (rank_c ^ 1))
    one_c, one_r = split_colors(src_partner, dst_partner, 5)
    alike = (one_c == one_r) & (row != col)
    two_c, _ = split_colors(src_same & alike, dst_same & alike, 4)
    color = jnp.broadcast_to(2 * one_c + two_c, (n, n))
    src = row >> 3
    pair = (row & 7) >> 1
    half = row & 1
    even = half == 0
    mine = src == me
    turn = me >> 2

    def pick(mask, value):
        return jnp.sum(jnp.where(mask, value, 0), axis=0, keepdims=True)

    rows = [
        pick(mine & even & (color == col), pair),
        pick(mine & even & (pair == col), color),
        pick(even & (color == turn) & (owner_c == col), src),
        pick(even & (color == turn) & (src == col), owner_c),
        pick((owner_c == me) & ((dest & 15) == col), 2 * color + half + 1) - 1,
        pick((owner_c == me) & (2 * color + half == col), dest & 15),
    ]
    rows += [jnp.zeros_like(rows[0])] * 2
    return jnp.concatenate(rows, axis=0)


def tables_kernel(dest_ref, tab_ref, every, send_sem, recv_sem):
    me = lax.axis_index("seq")
    greet("seq", PEERS, me)

    def body(step, carry):
        peer = lax.rem(me + step, PEERS)
        pltpu.make_async_remote_copy(
            src_ref=dest_ref,
            dst_ref=every.at[me],
            send_sem=send_sem,
            recv_sem=recv_sem,
            device_id={"seq": peer},
            device_id_type=MESH,
        ).start()
        return carry

    lax.fori_loop(1, PEERS, body, 0)
    every[me] = dest_ref[...]
    wait_all(every, recv_sem)
    wait_all(every, send_sem)
    tab_ref[...] = color_tables(every[...].reshape(PEERS * 8, 128), me)


def encoder_kernel(
    tab_ref, image_ref, x_ref, gain_ref, qkv_ref, out_ref, kv_ref, pay_ref, normed, mixed, att, hidden
):
    tokens, vis = x_ref.shape
    span = 2 * BLK

    def norm_rows(t, carry):
        rows = pl.ds(pl.multiple_of(t * 64, 64), 64)
        values = x_ref[rows, :].astype(f32)
        center = values - jnp.mean(values, axis=-1, keepdims=True)
        spread = jnp.mean(center * center, axis=-1, keepdims=True)
        normed[rows, :] = (center * lax.rsqrt(spread + EPS) * gain_ref[...]).astype(bf16)
        return carry

    lax.fori_loop(0, tokens // 64, norm_rows, 0)

    def mix_columns(t, carry):
        cols = pl.ds(pl.multiple_of(t * 384, 128), 384)
        mixed[:, cols] = dot_nn(normed[...], qkv_ref[:, cols]).astype(bf16)
        return carry

    lax.fori_loop(0, mixed.shape[1] // 384, mix_columns, 0)

    width = VHEADS * VHEAD
    scale = 1.0 / math.sqrt(VHEAD)
    row = lax.broadcasted_iota(jnp.int32, (span, span), 0)
    col = lax.broadcasted_iota(jnp.int32, (span, span), 1)
    near = (row // BLK) == (col // BLK)

    def attend(j, carry):
        rows = pl.ds(pl.multiple_of(j * span, span), span)
        joined = image_ref[2 * j] == image_ref[2 * j + 1]
        allowed = near | joined
        tiles = [None] * (width // 128)
        for head in range(VHEADS):
            first, last = head * VHEAD // 128, ((head + 1) * VHEAD - 1) // 128
            cut = (last - first + 1) * 128
            base = first * 128
            lane = lax.broadcasted_iota(jnp.int32, (span, cut), 1) + base
            inside = (lane >= head * VHEAD) & (lane < (head + 1) * VHEAD)
            q = jnp.where(inside, mixed[rows, base : base + cut], jnp.zeros((), bf16))
            k = mixed[rows, width + base : width + base + cut]
            v = mixed[rows, 2 * width + base : 2 * width + base + cut]
            scores = jnp.where(allowed, dot_nt(k, q) * scale, -jnp.inf)
            terms = jnp.exp(scores - jnp.max(scores, axis=0, keepdims=True))
            weights = (terms / jnp.sum(terms, axis=0, keepdims=True)).astype(bf16)
            result = dot_tn(weights, v)
            for tile in range(first, last + 1):
                at = (tile - first) * 128
                part = result[:, at : at + 128]
                if tiles[tile] is None:
                    tiles[tile] = part
                else:
                    tiles[tile] = jnp.where(inside[:, at : at + 128], part, tiles[tile])
        att[rows, :] = jnp.concatenate(tiles, axis=1).astype(bf16)
        return carry

    lax.fori_loop(0, tokens // span, attend, 0)

    def project(t, carry):
        cols = pl.ds(pl.multiple_of(t * 256, 256), 256)
        part = x_ref[:, cols].astype(f32) + dot_nn(att[...], out_ref[:, cols])
        hidden[:, :, cols] = part.astype(bf16).reshape(PAIRS, span, 256)
        return carry

    lax.fori_loop(0, vis // 256, project, 0)

    half = KVHEADS * HEAD
    for piece in range(PIECES):

        def make_pay(t, carry):
            source = jnp.concatenate([hidden[tab_ref[0, c]] for c in range(PAIRS)], axis=0)
            at = pl.multiple_of((piece * PER + t) * HEAD, HEAD)
            weight = jnp.concatenate(
                [kv_ref[:, pl.ds(at, HEAD)], kv_ref[:, pl.ds(half + at, HEAD)]], axis=1
            )
            got = dot_nn(source, weight).astype(bf16).reshape(PEERS, span // 4, 2 * HEAD)
            pay_ref[piece, :, :, pl.ds(pl.multiple_of(t * 2 * HEAD, 2 * HEAD), 2 * HEAD)] = got
            return carry

        lax.fori_loop(0, PER, make_pay, 0)


def cross_kernel(
    tab_ref,
    kimg_ref,
    seen_ref,
    pay_ref,
    q_ref,
    og_ref,
    qg_ref,
    kg_ref,
    att_ref,
    kvg_ref,
    qn,
    got1,
    out2,
    got2,
    gkv,
    out3,
    got3,
    out4,
    got4,
    send_sem,
    recv_sem,
):
    me = lax.axis_index("seq")
    scale = 1.0 / math.sqrt(HEAD)
    greet("seq", PEERS, me)
    for h in range(PIECES):
        exchange(pay_ref.at[h], got1[h], me, send_sem.at[0, h], recv_sem.at[0, h])

    def norm_queries(g, carry):
        block = q_ref[:, pl.ds(pl.multiple_of(g * SHARED * HEAD, HEAD), SHARED * HEAD)]
        for hh in range(SHARED):
            x = block[:, hh * HEAD : (hh + 1) * HEAD].astype(f32)
            inv = lax.rsqrt(jnp.mean(x * x, axis=-1, keepdims=True) + EPS)
            y = (x * inv * qg_ref[...]).astype(bf16)
            for s in range(CAP):
                qn[g, s, hh * LEN : (hh + 1) * LEN, :] = y[s * LEN : (s + 1) * LEN, :]
        return carry

    lax.fori_loop(0, KVHEADS, norm_queries, 0)

    def relay(h, got, out, row, target, phase):
        wait_all(got[h], recv_sem.at[phase - 1, h])

        def body(d, carry):
            out[h][d] = got[h][tab_ref[row, d]]
            return carry

        lax.fori_loop(0, PEERS, body, 0)
        exchange(out[h], target[h], me, send_sem.at[phase, h], recv_sem.at[phase, h])

    def one(h, gi, s):
        g = h * PER + gi
        at = pl.multiple_of(gi * 2 * HEAD, 2 * HEAD)
        blocks, masks = [], []
        seen = seen_ref[pl.ds(s, 1), :]
        for kb in range(CAP):
            index = tab_ref[4, s * CAP + kb]
            block = got2[h][pl.ds(2 * jnp.maximum(index, 0), 2), :, pl.ds(at, 2 * HEAD)]
            blocks.append(
                jnp.where(index >= 0, block, jnp.zeros((), bf16)).reshape(BLK, 2 * HEAD)
            )
            visible = kimg_ref[s, kb] < seen
            masks.append(jnp.broadcast_to(visible, (BLK, SHARED * LEN)))
        keyval = jnp.concatenate(blocks, axis=0)
        allowed = jnp.concatenate(masks, axis=0)
        keys = keyval[:, :HEAD].astype(f32)
        values = keyval[:, HEAD:]
        inv = lax.rsqrt(jnp.mean(keys * keys, axis=-1, keepdims=True) + EPS)
        kn = (keys * inv * kg_ref[...]).astype(bf16)
        queries = qn[g, s]
        rows = pl.ds(pl.multiple_of(s * LEN, LEN), LEN)
        col0 = pl.multiple_of(g * SHARED * HEAD, SHARED * HEAD)
        grad_row = og_ref[rows, pl.ds(col0, SHARED * HEAD)]
        grads = jnp.concatenate(
            [grad_row[:, hh * HEAD : (hh + 1) * HEAD] for hh in range(SHARED)], axis=0
        )
        scores = jnp.where(allowed, dot_nt(kn, queries) * scale, -jnp.inf)
        terms = jnp.exp(scores - jnp.max(scores, axis=0, keepdims=True))
        weights = terms / jnp.sum(terms, axis=0, keepdims=True)
        rounded = weights.astype(bf16)
        attended = dot_tn(rounded, values).astype(bf16)
        att_ref[rows, pl.ds(col0, SHARED * HEAD)] = jnp.concatenate(
            [attended[hh * LEN : (hh + 1) * LEN, :] for hh in range(SHARED)], axis=1
        )
        grad_values = dot_nn(rounded, grads)
        grad_dot = dot_nt(values, grads)
        delta = jnp.sum(weights * grad_dot, axis=0, keepdims=True)
        grad_scores = (weights * (grad_dot - delta) * scale).astype(bf16)
        gained = dot_nn(grad_scores, queries) * kg_ref[...]
        mean = jnp.mean(keys * gained, axis=-1, keepdims=True)
        grad_keys = inv * (gained - keys * inv * inv * mean)
        result = jnp.concatenate([grad_keys, grad_values], axis=1).astype(bf16)
        gkv[pl.ds(s * CAP, CAP), :, pl.ds(at, 2 * HEAD)] = result.reshape(CAP, BLK, 2 * HEAD)

    def attend(h):
        wait_all(got2[h], recv_sem.at[1, h])

        def body(step, carry):
            gi, s = step // (CAP // 2), lax.rem(step, CAP // 2) * 2
            one(h, gi, s)
            one(h, gi, s + 1)
            return carry

        lax.fori_loop(0, PER * CAP // 2, body, 0)

        def pack(cb, carry):
            block = gkv[tab_ref[5, cb]]
            out3[h][pl.ds(2 * cb, 2)] = block.reshape(2, BLK // 2, WIDE)
            return carry

        lax.fori_loop(0, 2 * PAIRS, pack, 0)
        exchange(out3[h], got3[h], me, send_sem.at[2, h], recv_sem.at[2, h])

    for h in range(PIECES):
        relay(h, got1, out2, 2, got2, 1)
    for h in range(PIECES):
        attend(h)
        if h > 0:
            relay(h - 1, got3, out4, 3, got4, 3)
    relay(PIECES - 1, got3, out4, 3, got4, 3)
    half = KVHEADS * HEAD
    for h in range(PIECES):
        wait_all(got4[h], recv_sem.at[3, h])
        for j in range(PAIRS):
            color = tab_ref[1, j]
            block = got4[h][pl.ds(4 * color, 4)].reshape(2, BLK, WIDE)
            for gi in range(PER):
                at = (h * PER + gi) * HEAD
                kvg_ref[2 * j : 2 * j + 2, :, at : at + HEAD] = block[
                    :, :, gi * 2 * HEAD : gi * 2 * HEAD + HEAD
                ]
                kvg_ref[2 * j : 2 * j + 2, :, half + at : half + at + HEAD] = block[
                    :, :, gi * 2 * HEAD + HEAD : (gi + 1) * 2 * HEAD
                ]
    for phase in range(4):
        for h in range(PIECES):
            wait_all(got1[h], send_sem.at[phase, h])


VMEM = pl.BlockSpec(memory_space=pltpu.VMEM)
SMEM = pl.BlockSpec(memory_space=pltpu.SMEM)
LIMIT = 48 * 1024 * 1024


def local(
    images,
    vit_gain,
    vit_qkv,
    vit_out,
    kv_weight,
    queries,
    q_gain,
    k_gain,
    out_grad,
    block_image,
    block_dest,
    key_image,
    text_seen,
):
    enc_blocks, block_len, vis = images.shape
    tokens = enc_blocks * block_len
    full_qkv = lax.all_gather(vit_qkv, ("enc", "mp"), axis=0, tiled=True)
    full_out = lax.all_gather(vit_out, ("enc", "mp"), axis=0, tiled=True)
    full_kv = lax.all_gather(kv_weight, "mp", axis=0, tiled=True)
    tables = pl.pallas_call(
        tables_kernel,
        out_shape=jax.ShapeDtypeStruct((8, 128), jnp.int32),
        in_specs=[VMEM],
        out_specs=VMEM,
        scratch_shapes=[
            pltpu.VMEM((PEERS, 8, 128), jnp.int32),
            pltpu.SemaphoreType.DMA,
            pltpu.SemaphoreType.DMA,
        ],
        compiler_params=pltpu.CompilerParams(collective_id=0, has_side_effects=True),
    )(jnp.broadcast_to(block_dest[:, None], (8, 128)))
    slots = (PIECES, PEERS, BLK // 2, WIDE)
    payload = pl.pallas_call(
        encoder_kernel,
        out_shape=jax.ShapeDtypeStruct(slots, bf16),
        in_specs=[SMEM, SMEM] + [VMEM] * 5,
        out_specs=VMEM,
        scratch_shapes=[
            pltpu.VMEM((tokens, vis), bf16),
            pltpu.VMEM((tokens, 3 * VHEADS * VHEAD), bf16),
            pltpu.VMEM((tokens, VHEADS * VHEAD), bf16),
            pltpu.VMEM((PAIRS, 2 * BLK, vis), bf16),
        ],
        compiler_params=pltpu.CompilerParams(vmem_limit_bytes=LIMIT),
    )(
        tables,
        block_image,
        images.reshape(tokens, vis),
        vit_gain.reshape(1, vis),
        full_qkv,
        full_out,
        full_kv,
    )
    seen = jnp.tile(text_seen.reshape(CAP, 1, LEN), (1, SHARED, 1)).reshape(CAP, SHARED * LEN)
    attended, kv_grad = pl.pallas_call(
        cross_kernel,
        out_shape=(
            jax.ShapeDtypeStruct(queries.shape, bf16),
            jax.ShapeDtypeStruct((enc_blocks, block_len, 2 * KVHEADS * HEAD), bf16),
        ),
        in_specs=[SMEM, SMEM] + [VMEM] * 6,
        out_specs=(VMEM, VMEM),
        scratch_shapes=[pltpu.VMEM((KVHEADS, CAP, SHARED * LEN, HEAD), bf16)]
        + [[pltpu.VMEM(slots[1:], bf16)] * PIECES] * 3
        + [pltpu.VMEM((CAP * CAP, BLK, WIDE), bf16)]
        + [[pltpu.VMEM(slots[1:], bf16)] * PIECES] * 4
        + [pltpu.SemaphoreType.DMA((4, PIECES))] * 2,
        compiler_params=pltpu.CompilerParams(
            collective_id=1, has_side_effects=True, vmem_limit_bytes=LIMIT
        ),
    )(
        tables,
        key_image,
        seen,
        payload,
        queries,
        out_grad,
        q_gain.reshape(1, HEAD),
        k_gain.reshape(1, HEAD),
    )
    return attended, kv_grad


def solution(mesh):
    everywhere = ("enc", "seq", "mp")
    placed = (
        P(everywhere, None, None),
        P(),
        P(("enc", "mp"), None),
        P(("enc", "mp"), None),
        P("mp", None),
        P(everywhere, None),
        P(),
        P(),
        P(everywhere, None),
        P(everywhere),
        P(everywhere),
        P(everywhere, None),
        P(everywhere),
    )
    return jax.shard_map(
        local,
        mesh=mesh,
        in_specs=placed,
        out_specs=(P(everywhere, None), P(everywhere, None, None)),
        check_vma=False,
    )
```

```python
import functools
import math

import jax
import jax.numpy as jnp
from jax import lax
from jax.experimental import pallas as pl
from jax.experimental.pallas import tpu as pltpu
from jax.sharding import PartitionSpec as P

VHEADS = 8
VHEAD = 80
HEAD = 128
KVHEADS = 4
SHARED = 8
BLK = 64
LEN = 32
CAP = 4
PEERS = 16
PAIRS = 4
PIECES = 2
PER = KVHEADS // PIECES
WIDE = PER * 2 * HEAD
EPS = 1e-05
MESH = pl.DeviceIdType.MESH
f32 = jnp.float32
bf16 = jnp.bfloat16


def dot_nn(left, right):
    return jnp.dot(left, right, preferred_element_type=f32)


def dot_nt(left, right):
    return lax.dot_general(left, right, (((1,), (1,)), ((), ())), preferred_element_type=f32)


def dot_tn(left, right):
    return lax.dot_general(left, right, (((0,), (0,)), ((), ())), preferred_element_type=f32)


def greet(axis, count, me):
    barrier = pltpu.get_barrier_semaphore()

    def body(step, carry):
        peer = lax.rem(me + step, count)
        pl.semaphore_signal(barrier, inc=1, device_id={axis: peer}, device_id_type=MESH)
        return carry

    lax.fori_loop(1, count, body, 0)
    pl.semaphore_wait(barrier, count - 1)


def exchange(source, target, me, send_sem, recv_sem):
    def body(step, carry):
        peer = lax.rem(me + step, PEERS)
        pltpu.make_async_remote_copy(
            src_ref=source.at[peer],
            dst_ref=target.at[me],
            send_sem=send_sem,
            recv_sem=recv_sem,
            device_id={"seq": peer},
            device_id_type=MESH,
        ).start()
        return carry

    lax.fori_loop(1, PEERS, body, 0)
    target[me] = source[me]


def wait_all(buffer, sem):
    view = buffer.at[pl.ds(0, PEERS - 1)]
    pltpu.make_async_copy(view, view, sem).wait()


def split_colors(src_partner, dst_partner, doublings):
    n = src_partner.shape[0]
    row = lax.broadcasted_iota(jnp.int32, (n, n), 0)
    col = lax.broadcasted_iota(jnp.int32, (n, n), 1)
    src_b = jnp.where(src_partner, 1.0, 0.0).astype(bf16)
    dst_b = jnp.where(dst_partner, 1.0, 0.0).astype(bf16)
    power = dot_nn(src_b, dst_b).astype(bf16)
    total = jnp.where(row == col, 1.0, 0.0) + power.astype(f32)
    yield
    for _ in range(doublings - 1):
        power = dot_nn(power, power).astype(bf16)
        total = total + dot_nn(total.astype(bf16), power)
        yield
    orbit = total > 0.5
    lead_c = jnp.min(jnp.where(orbit, col, n), axis=1, keepdims=True)
    lead_r = jnp.min(jnp.where(orbit, row, n), axis=0, keepdims=True)
    other_c = jnp.sum(jnp.where(src_partner, lead_r, 0), axis=1, keepdims=True)
    other_r = jnp.sum(jnp.where(src_partner, lead_c, 0), axis=0, keepdims=True)
    return (lead_c < other_c).astype(jnp.int32), (lead_r < other_r).astype(jnp.int32)


def color_tables(dest, me):
    n = dest.shape[0]
    row = lax.broadcasted_iota(jnp.int32, (n, n), 0)
    col = lax.broadcasted_iota(jnp.int32, (n, n), 1)
    dest_t = jnp.transpose(dest.astype(f32)).astype(jnp.int32)
    owner_c, owner_r = dest >> 4, dest_t >> 4
    parity_same = (row & 1) == (col & 1)
    src_same = ((row >> 3) == (col >> 3)) & parity_same
    dst_same = (owner_c == owner_r) & parity_same
    rank_c = jnp.sum(jnp.where(dst_same & (col < row), 1, 0), axis=1, keepdims=True)
    rank_r = jnp.sum(jnp.where(dst_same & (row < col), 1, 0), axis=0, keepdims=True)
    src_partner = col == (row ^ 2)
    dst_partner = dst_same & (rank_r == (rank_c ^ 1))
    yield
    one_c, one_r = yield from split_colors(src_partner, dst_partner, 5)
    yield
    alike = (one_c == one_r) & (row != col)
    two_c, _ = yield from split_colors(src_same & alike, dst_same & alike, 4)
    yield
    color = jnp.broadcast_to(2 * one_c + two_c, (n, n))
    src = row >> 3
    pair = (row & 7) >> 1
    half = row & 1
    even = half == 0
    mine = src == me
    turn = me // 4

    def pick(mask, value):
        return jnp.sum(jnp.where(mask, value, 0), axis=0, keepdims=True)

    rows = [
        pick(mine & even & (color == col), pair),
        pick(mine & even & (pair == col), color),
        pick(even & (color == turn) & (owner_c == col), src),
        pick(even & (color == turn) & (src == col), owner_c),
        pick((owner_c == me) & ((dest & 15) == col), 2 * color + half + 1) - 1,
        pick((owner_c == me) & (2 * color + half == col), dest & 15),
    ]
    rows += [jnp.zeros_like(rows[0])] * 2
    return jnp.concatenate(rows, axis=0)


PLANES = 8
ROWS = 160
PIECE = 256
COLS = 4 * PIECE
ARRIVALS = PLANES - 1


def encoder_kernel(
    image_ref,
    dest_ref,
    x_hbm,
    gain_ref,
    qkv_hbm,
    own_out_ref,
    kv_hbm,
    pay_ref,
    tab_out_ref,
    x_ref,
    every,
    tab_ref,
    weight,
    out_parts,
    out_ref,
    kv_ref,
    normed,
    mixed,
    att,
    hidden,
    local_sem,
    dest_sem,
    own_sem,
    kv_sem,
    z_send,
    z_recv,
    o_send,
    o_recv,
    r_send,
    r_recv,
    m_send,
    m_recv,
    om_sem,
):
    tokens, vis = x_ref.shape
    span = 2 * BLK
    e, q, m = lax.axis_index("enc"), lax.axis_index("seq"), lax.axis_index("mp")
    other = 1 - m
    d = 1 - 2 * m
    stride = 1 + 3 * m
    pos = lax.rem(q // stride, 4)
    ring = q - pos * stride
    left, right = lax.rem(pos + 3, 4), lax.rem(pos + 1, 4)
    ahead, behind = lax.rem(e + d + PLANES, PLANES), lax.rem(e - d + PLANES, PLANES)
    to_left, to_right = {"seq": ring + left * stride}, {"seq": ring + right * stride}
    to_ahead, to_behind, to_mate = {"enc": ahead}, {"enc": behind}, {"mp": other}

    def plane_rows(plane):
        return pl.ds(pl.multiple_of(plane * ROWS, ROWS), ROWS)

    def columns(at, count):
        return pl.ds(pl.multiple_of(at, HEAD), count)

    def remote(source, target, send, recv, device):
        copy = pltpu.make_async_remote_copy(
            src_ref=source,
            dst_ref=target,
            send_sem=send,
            recv_sem=recv,
            device_id=device,
            device_id_type=MESH,
        )
        copy.start()

    def done(view, sem):
        pltpu.make_async_copy(view, view, sem).wait()

    own_rows = pl.ds(pl.multiple_of(e * ROWS + m * (ROWS // 2), ROWS // 2), ROWS // 2)
    kv_half = kv_hbm.shape[0]
    kv_rows = pl.ds(pl.multiple_of(m * kv_half, kv_half), kv_half)
    qkv_copy = pltpu.make_async_copy(
        qkv_hbm, weight.at[own_rows, pl.ds(0, qkv_hbm.shape[1])], local_sem.at[0]
    )
    x_copy = pltpu.make_async_copy(x_hbm, x_ref, local_sem.at[1])
    kv_copy = pltpu.make_async_copy(kv_hbm, kv_ref.at[kv_rows], local_sem.at[2])
    qkv_copy.start()
    x_copy.start()
    kv_copy.start()
    out_parts[m, e, 0 : own_out_ref.shape[0], :] = own_out_ref[...]

    barrier = pltpu.get_barrier_semaphore()

    def hello(step, carry):
        pl.semaphore_signal(
            barrier, inc=1, device_id={"seq": lax.rem(q + step, PEERS)}, device_id_type=MESH
        )
        return carry

    lax.fori_loop(1, PEERS, hello, 0)
    for device in (to_ahead, to_behind, to_mate):
        pl.semaphore_signal(barrier, inc=1, device_id=device, device_id_type=MESH)
    pl.semaphore_wait(barrier, PEERS + 2)

    qkv_copy.wait()
    for which, start in ((0, other), (1, m)):
        view = weight.at[own_rows, columns(start * COLS, COLS)]
        remote(view, view, own_sem.at[0, which], own_sem.at[1, which], to_mate)

    def send_dest(step, carry):
        peer = lax.rem(q + step, PEERS)
        remote(dest_ref, every.at[q], dest_sem.at[0], dest_sem.at[1], {"seq": peer})
        return carry

    lax.fori_loop(1, PEERS, send_dest, 0)
    every[q] = dest_ref[...]

    mate_rows = pl.ds(
        pl.multiple_of(e * ROWS + other * (ROWS // 2), ROWS // 2), ROWS // 2
    )
    done(weight.at[mate_rows, columns(m * COLS, COLS)], own_sem.at[1, 0])

    my_cols = columns(m * COLS + pos * PIECE, PIECE)

    def send_z(plane, arrival, device):
        view = weight.at[plane_rows(plane), my_cols]
        remote(view, view, z_send.at[arrival], z_recv.at[arrival], device)

    def send_out(plane, arrival, device):
        view = out_parts.at[m, plane]
        remote(view, view, o_send.at[arrival], o_recv.at[arrival], device)

    for send in (send_z, send_out):
        send(e, 0, to_ahead)
        send(e, 1, to_behind)
    kv_there = kv_ref.at[kv_rows]
    remote(kv_hbm, kv_there, kv_sem.at[0], kv_sem.at[1], to_mate)
    x_copy.wait()

    def norm_rows(t):
        rows = slice(t * 64, t * 64 + 64)
        values = x_ref[rows, :].astype(f32)
        center = values - jnp.mean(values, axis=-1, keepdims=True)
        spread = jnp.mean(center * center, axis=-1, keepdims=True)
        normed[rows, :] = (center * lax.rsqrt(spread + EPS) * gain_ref[...]).astype(bf16)

    def jobs():
        for t in range(2):
            norm_rows(t)
            yield
        wait_all(every, dest_sem.at[1])
        tab_out_ref[...] = yield from color_tables(every[...].reshape(PEERS * 8, 128), q)
        yield
        for t in range(2, tokens // 64):
            norm_rows(t)
            yield

    work = jobs()

    def plane_of(arrival):
        hops = arrival // 2 + 1
        if arrival % 2 == 0:
            return lax.rem(e - d * hops + PLANES, PLANES)
        return lax.rem(e + d * hops + PLANES, PLANES)

    def piece(k, place):
        return weight.at[plane_rows(plane_of(k)), columns(m * COLS + place * PIECE, PIECE)]

    def part(k, place, which):
        return weight.at[
            plane_rows(plane_of(k)),
            columns(m * COLS + place * PIECE + which * (PIECE // 2), PIECE // 2),
        ]

    far = lax.rem(pos + 2, 4)
    for k in range(ARRIVALS + 2):
        if k < ARRIVALS:
            device = to_ahead if k % 2 == 0 else to_behind
            plane = plane_of(k)
            done(piece(k, pos), z_recv.at[k])
            if k + 2 < ARRIVALS:
                send_z(plane, k + 2, device)
            remote(piece(k, pos), piece(k, pos), r_send.at[k, 0], r_recv.at[k, 0], to_right)
            remote(piece(k, pos), piece(k, pos), r_send.at[k, 1], r_recv.at[k, 1], to_left)
            done(out_parts.at[m, plane], o_recv.at[k])
            if k + 2 < ARRIVALS:
                send_out(plane, k + 2, device)
        j = k - 1
        if 0 <= j < ARRIVALS:
            done(piece(j, left), r_recv.at[j, 0])
            remote(part(j, left, 0), part(j, left, 0), r_send.at[j, 2], r_recv.at[j, 2], to_right)
            done(piece(j, right), r_recv.at[j, 1])
            remote(part(j, right, 1), part(j, right, 1), r_send.at[j, 3], r_recv.at[j, 3], to_left)
        j = k - 2
        if 0 <= j < ARRIVALS:
            done(part(j, far, 0), r_recv.at[j, 2])
            done(part(j, far, 1), r_recv.at[j, 3])
            view = weight.at[plane_rows(plane_of(j)), columns(m * COLS, COLS)]
            remote(view, view, m_send.at[j], m_recv.at[j], to_mate)
        if k == ARRIVALS - 1:
            remote(out_parts.at[m], out_parts.at[m], om_sem.at[0], om_sem.at[1], to_mate)
        for _ in range(3):
            next(work, None)
    for _ in work:
        pass
    tab_copy = pltpu.make_async_copy(tab_out_ref, tab_ref, local_sem.at[3])
    tab_copy.start()

    done(weight.at[mate_rows, columns(other * COLS, COLS)], own_sem.at[1, 1])
    for k in range(ARRIVALS):
        done(weight.at[plane_rows(e), columns(0, COLS)], m_recv.at[k])

    def mix_columns(t, carry):
        cols = pl.ds(pl.multiple_of(t * 384, 128), 384)
        mixed[:, cols] = dot_nn(normed[...], weight[:, cols]).astype(bf16)
        return carry

    lax.fori_loop(0, mixed.shape[1] // 384, mix_columns, 0)

    width = VHEADS * VHEAD
    scale = 1.0 / math.sqrt(VHEAD)
    row = lax.broadcasted_iota(jnp.int32, (span, span), 0)
    col = lax.broadcasted_iota(jnp.int32, (span, span), 1)
    near = (row // BLK) == (col // BLK)

    def attend(j, carry):
        rows = pl.ds(pl.multiple_of(j * span, span), span)
        joined = image_ref[2 * j] == image_ref[2 * j + 1]
        allowed = near | joined
        tiles = [None] * (width // 128)
        for head in range(VHEADS):
            first, last = head * VHEAD // 128, ((head + 1) * VHEAD - 1) // 128
            cut = (last - first + 1) * 128
            base = first * 128
            lane = lax.broadcasted_iota(jnp.int32, (span, cut), 1) + base
            inside = (lane >= head * VHEAD) & (lane < (head + 1) * VHEAD)
            query = jnp.where(inside, mixed[rows, base : base + cut], jnp.zeros((), bf16))
            key = mixed[rows, width + base : width + base + cut]
            value = mixed[rows, 2 * width + base : 2 * width + base + cut]
            scores = jnp.where(allowed, dot_nt(key, query) * scale, -jnp.inf)
            terms = jnp.exp(scores - jnp.max(scores, axis=0, keepdims=True))
            weights = (terms / jnp.sum(terms, axis=0, keepdims=True)).astype(bf16)
            result = dot_tn(weights, value)
            for tile in range(first, last + 1):
                at = (tile - first) * 128
                found = result[:, at : at + 128]
                if tiles[tile] is None:
                    tiles[tile] = found
                else:
                    tiles[tile] = jnp.where(inside[:, at : at + 128], found, tiles[tile])
        att[rows, :] = jnp.concatenate(tiles, axis=1).astype(bf16)
        return carry

    lax.fori_loop(0, tokens // span, attend, 0)

    done(out_parts.at[other], om_sem.at[1])
    have = own_out_ref.shape[0]
    for plane in range(PLANES):
        both = [out_parts[core, plane, 0:have, :].astype(f32) for core in range(2)]
        out_ref[2 * have * plane : 2 * have * (plane + 1), :] = jnp.concatenate(
            both, axis=0
        ).astype(bf16)

    def project(t, carry):
        cols = pl.ds(pl.multiple_of(t * 256, 256), 256)
        total = x_ref[:, cols].astype(f32) + dot_nn(att[...], out_ref[:, cols])
        hidden[:, :, cols] = total.astype(bf16).reshape(PAIRS, span, 256)
        return carry

    lax.fori_loop(0, vis // 256, project, 0)

    tab_copy.wait()
    kv_copy.wait()
    done(kv_there, kv_sem.at[1])
    half = KVHEADS * HEAD
    for h in range(PIECES):

        def make_pay(t, carry):
            source = jnp.concatenate([hidden[tab_ref[0, c] & 3] for c in range(PAIRS)], axis=0)
            at = pl.multiple_of((h * PER + t) * HEAD, HEAD)
            both = jnp.concatenate(
                [kv_ref[:, pl.ds(at, HEAD)], kv_ref[:, pl.ds(half + at, HEAD)]], axis=1
            )
            got = dot_nn(source, both).astype(bf16).reshape(PEERS, span // 4, 2 * HEAD)
            pay_ref[h, :, :, pl.ds(pl.multiple_of(t * 2 * HEAD, 2 * HEAD), 2 * HEAD)] = got
            return carry

        lax.fori_loop(0, PER, make_pay, 0)

    wait_all(every, dest_sem.at[0])
    for which, start in ((0, other), (1, m)):
        done(weight.at[own_rows, columns(start * COLS, COLS)], own_sem.at[0, which])
    done(kv_there, kv_sem.at[0])
    done(out_parts.at[m], om_sem.at[0])
    for k in range(ARRIVALS):
        done(piece(k, pos), z_send.at[k])
        done(out_parts.at[m, e], o_send.at[k])
        for way in range(4):
            done(piece(k, pos) if way < 2 else part(k, pos, 0), r_send.at[k, way])
        done(weight.at[plane_rows(e), columns(0, COLS)], m_send.at[k])


def cross_kernel(
    tab_ref,
    kimg_ref,
    seen_ref,
    pay_ref,
    q_ref,
    og_ref,
    qg_ref,
    kg_ref,
    att_ref,
    kvg_ref,
    qn,
    got1,
    out2,
    got2,
    gkv,
    out3,
    got3,
    out4,
    got4,
    send_sem,
    recv_sem,
):
    me = lax.axis_index("seq")
    scale = 1.0 / math.sqrt(HEAD)
    greet("seq", PEERS, me)
    for h in range(PIECES):
        exchange(pay_ref.at[h], got1[h], me, send_sem.at[0, h], recv_sem.at[0, h])

    def norm_queries(g, carry):
        block = q_ref[:, pl.ds(pl.multiple_of(g * SHARED * HEAD, HEAD), SHARED * HEAD)]
        for hh in range(SHARED):
            x = block[:, hh * HEAD : (hh + 1) * HEAD].astype(f32)
            inv = lax.rsqrt(jnp.mean(x * x, axis=-1, keepdims=True) + EPS)
            y = (x * inv * qg_ref[...]).astype(bf16)
            for s in range(CAP):
                qn[g, s, hh * LEN : (hh + 1) * LEN, :] = y[s * LEN : (s + 1) * LEN, :]
        return carry

    lax.fori_loop(0, KVHEADS, norm_queries, 0)

    def relay(h, got, out, row, target, phase):
        wait_all(got[h], recv_sem.at[phase - 1, h])

        def body(d, carry):
            out[h][d] = got[h][tab_ref[row, d] & 15]
            return carry

        lax.fori_loop(0, PEERS, body, 0)
        exchange(out[h], target[h], me, send_sem.at[phase, h], recv_sem.at[phase, h])

    def one(h, gi, s):
        g = h * PER + gi
        at = pl.multiple_of(gi * 2 * HEAD, 2 * HEAD)
        blocks, masks = [], []
        seen = seen_ref[pl.ds(s, 1), :]
        for kb in range(CAP):
            index = tab_ref[4, s * CAP + kb]
            block = got2[h][pl.ds(2 * (jnp.maximum(index, 0) & 7), 2), :, pl.ds(at, 2 * HEAD)]
            blocks.append(
                jnp.where(index >= 0, block, jnp.zeros((), bf16)).reshape(BLK, 2 * HEAD)
            )
            visible = kimg_ref[s, kb] < seen
            masks.append(jnp.broadcast_to(visible, (BLK, SHARED * LEN)))
        keyval = jnp.concatenate(blocks, axis=0)
        allowed = jnp.concatenate(masks, axis=0)
        keys = keyval[:, :HEAD].astype(f32)
        values = keyval[:, HEAD:]
        inv = lax.rsqrt(jnp.mean(keys * keys, axis=-1, keepdims=True) + EPS)
        kn = (keys * inv * kg_ref[...]).astype(bf16)
        queries = qn[g, s]
        rows = pl.ds(pl.multiple_of(s * LEN, LEN), LEN)
        col0 = pl.multiple_of(g * SHARED * HEAD, SHARED * HEAD)
        grad_row = og_ref[rows, pl.ds(col0, SHARED * HEAD)]
        grads = jnp.concatenate(
            [grad_row[:, hh * HEAD : (hh + 1) * HEAD] for hh in range(SHARED)], axis=0
        )
        scores = jnp.where(allowed, dot_nt(kn, queries) * scale, -jnp.inf)
        terms = jnp.exp(scores - jnp.max(scores, axis=0, keepdims=True))
        weights = terms / jnp.sum(terms, axis=0, keepdims=True)
        rounded = weights.astype(bf16)
        attended = dot_tn(rounded, values).astype(bf16)
        att_ref[rows, pl.ds(col0, SHARED * HEAD)] = jnp.concatenate(
            [attended[hh * LEN : (hh + 1) * LEN, :] for hh in range(SHARED)], axis=1
        )
        grad_values = dot_nn(rounded, grads)
        grad_dot = dot_nt(values, grads)
        delta = jnp.sum(weights * grad_dot, axis=0, keepdims=True)
        grad_scores = (weights * (grad_dot - delta) * scale).astype(bf16)
        gained = dot_nn(grad_scores, queries) * kg_ref[...]
        mean = jnp.mean(keys * gained, axis=-1, keepdims=True)
        grad_keys = inv * (gained - keys * inv * inv * mean)
        result = jnp.concatenate([grad_keys, grad_values], axis=1).astype(bf16)
        gkv[pl.ds(s * CAP, CAP), :, pl.ds(at, 2 * HEAD)] = result.reshape(CAP, BLK, 2 * HEAD)

    def attend(h):
        wait_all(got2[h], recv_sem.at[1, h])

        def body(step, carry):
            gi, s = step // (CAP // 2), lax.rem(step, CAP // 2) * 2
            one(h, gi, s)
            one(h, gi, s + 1)
            return carry

        lax.fori_loop(0, PER * CAP // 2, body, 0)

        def pack(cb, carry):
            block = gkv[tab_ref[5, cb] & 15]
            out3[h][pl.ds(2 * cb, 2)] = block.reshape(2, BLK // 2, WIDE)
            return carry

        lax.fori_loop(0, 2 * PAIRS, pack, 0)
        exchange(out3[h], got3[h], me, send_sem.at[2, h], recv_sem.at[2, h])

    for h in range(PIECES):
        relay(h, got1, out2, 2, got2, 1)
    for h in range(PIECES):
        attend(h)
        if h > 0:
            relay(h - 1, got3, out4, 3, got4, 3)
    relay(PIECES - 1, got3, out4, 3, got4, 3)
    half = KVHEADS * HEAD
    for h in range(PIECES):
        wait_all(got4[h], recv_sem.at[3, h])
        for j in range(PAIRS):
            color = tab_ref[1, j] & 3
            block = got4[h][pl.ds(4 * color, 4)].reshape(2, BLK, WIDE)
            for gi in range(PER):
                at = (h * PER + gi) * HEAD
                kvg_ref[2 * j : 2 * j + 2, :, at : at + HEAD] = block[
                    :, :, gi * 2 * HEAD : gi * 2 * HEAD + HEAD
                ]
                kvg_ref[2 * j : 2 * j + 2, :, half + at : half + at + HEAD] = block[
                    :, :, gi * 2 * HEAD + HEAD : (gi + 1) * 2 * HEAD
                ]
    for phase in range(4):
        for h in range(PIECES):
            wait_all(got1[h], send_sem.at[phase, h])


VMEM = pl.BlockSpec(memory_space=pltpu.VMEM)
SMEM = pl.BlockSpec(memory_space=pltpu.SMEM)
ANY = pl.BlockSpec(memory_space=pl.ANY)
LIMIT = 48 * 1024 * 1024


def local(
    images,
    vit_gain,
    vit_qkv,
    vit_out,
    kv_weight,
    queries,
    q_gain,
    k_gain,
    out_grad,
    block_image,
    block_dest,
    key_image,
    text_seen,
):
    enc_blocks, block_len, vis = images.shape
    tokens = enc_blocks * block_len
    slots = (PIECES, PEERS, BLK // 2, WIDE)
    payload, tables = pl.pallas_call(
        encoder_kernel,
        out_shape=(
            jax.ShapeDtypeStruct(slots, bf16),
            jax.ShapeDtypeStruct((8, 128), jnp.int32),
        ),
        in_specs=[SMEM, VMEM, ANY, VMEM, ANY, VMEM, ANY],
        out_specs=(VMEM, VMEM),
        scratch_shapes=[
            pltpu.VMEM((tokens, vis), bf16),
            pltpu.VMEM((PEERS, 8, 128), jnp.int32),
            pltpu.SMEM((8, 128), jnp.int32),
            pltpu.VMEM((vis, 2 * COLS), bf16),
            pltpu.VMEM((2, PLANES, 48, vis), bf16),
            pltpu.VMEM((VHEADS * VHEAD, vis), bf16),
            pltpu.VMEM((vis, 2 * KVHEADS * HEAD), bf16),
            pltpu.VMEM((tokens, vis), bf16),
            pltpu.VMEM((tokens, 3 * VHEADS * VHEAD), bf16),
            pltpu.VMEM((tokens, VHEADS * VHEAD), bf16),
            pltpu.VMEM((PAIRS, 2 * BLK, vis), bf16),
            pltpu.SemaphoreType.DMA((4,)),
            pltpu.SemaphoreType.DMA((2,)),
            pltpu.SemaphoreType.DMA((2, 2)),
            pltpu.SemaphoreType.DMA((2,)),
        ]
        + [pltpu.SemaphoreType.DMA((ARRIVALS,))] * 4
        + [pltpu.SemaphoreType.DMA((ARRIVALS, 4))] * 2
        + [pltpu.SemaphoreType.DMA((ARRIVALS,))] * 2
        + [pltpu.SemaphoreType.DMA((2,))],
        compiler_params=pltpu.CompilerParams(
            collective_id=0, has_side_effects=True, vmem_limit_bytes=LIMIT
        ),
    )(
        block_image,
        jnp.broadcast_to(block_dest[:, None], (8, 128)),
        images.reshape(tokens, vis),
        vit_gain.reshape(1, vis),
        vit_qkv,
        vit_out,
        kv_weight,
    )
    seen = jnp.tile(text_seen.reshape(CAP, 1, LEN), (1, SHARED, 1)).reshape(CAP, SHARED * LEN)
    attended, kv_grad = pl.pallas_call(
        cross_kernel,
        out_shape=(
            jax.ShapeDtypeStruct(queries.shape, bf16),
            jax.ShapeDtypeStruct((enc_blocks, block_len, 2 * KVHEADS * HEAD), bf16),
        ),
        in_specs=[SMEM, SMEM] + [VMEM] * 6,
        out_specs=(VMEM, VMEM),
        scratch_shapes=[pltpu.VMEM((KVHEADS, CAP, SHARED * LEN, HEAD), bf16)]
        + [[pltpu.VMEM(slots[1:], bf16)] * PIECES] * 3
        + [pltpu.VMEM((CAP * CAP, BLK, WIDE), bf16)]
        + [[pltpu.VMEM(slots[1:], bf16)] * PIECES] * 4
        + [pltpu.SemaphoreType.DMA((4, PIECES))] * 2,
        compiler_params=pltpu.CompilerParams(
            collective_id=1, has_side_effects=True, vmem_limit_bytes=LIMIT
        ),
    )(
        tables,
        key_image,
        seen,
        payload,
        queries,
        out_grad,
        q_gain.reshape(1, HEAD),
        k_gain.reshape(1, HEAD),
    )
    return attended, kv_grad


def solution(mesh):
    everywhere = ("enc", "seq", "mp")
    placed = (
        P(everywhere, None, None),
        P(),
        P(("enc", "mp"), None),
        P(("enc", "mp"), None),
        P("mp", None),
        P(everywhere, None),
        P(),
        P(),
        P(everywhere, None),
        P(everywhere),
        P(everywhere),
        P(everywhere, None),
        P(everywhere),
    )
    return jax.shard_map(
        local,
        mesh=mesh,
        in_specs=placed,
        out_specs=(P(everywhere, None), P(everywhere, None, None)),
        check_vma=False,
    )
```

```python
import math

import jax
import jax.numpy as jnp
from jax import lax
from jax.experimental import pallas as pl
from jax.experimental.pallas import tpu as pltpu
from jax.sharding import PartitionSpec as P

VHEADS = 8
VHEAD = 80
HEAD = 128
KVHEADS = 4
SHARED = 8
BLK = 64
LEN = 32
CAP = 4
PEERS = 16
PAIRS = 4
PIECES = 4
PER = KVHEADS // PIECES
WIDE = PER * 2 * HEAD
EPS = 1e-05
MESH = pl.DeviceIdType.MESH
f32 = jnp.float32
bf16 = jnp.bfloat16


def dot_nn(left, right):
    return jnp.dot(left, right, preferred_element_type=f32)


def dot_nt(left, right):
    return lax.dot_general(left, right, (((1,), (1,)), ((), ())), preferred_element_type=f32)


def dot_tn(left, right):
    return lax.dot_general(left, right, (((0,), (0,)), ((), ())), preferred_element_type=f32)


def exchange(source, target, me, send_sem, recv_sem):
    def body(step, carry):
        peer = lax.rem(me + step, PEERS)
        pltpu.make_async_remote_copy(
            src_ref=source.at[peer],
            dst_ref=target.at[me],
            send_sem=send_sem,
            recv_sem=recv_sem,
            device_id={"seq": peer},
            device_id_type=MESH,
        ).start()
        return carry

    lax.fori_loop(1, PEERS, body, 0)
    target[me] = source[me]


def wait_all(buffer, sem):
    view = buffer.at[pl.ds(0, PEERS - 1)]
    pltpu.make_async_copy(view, view, sem).wait()


def split_colors(src_partner, dst_partner, doublings):
    n = src_partner.shape[0]
    row = lax.broadcasted_iota(jnp.int32, (n, n), 0)
    col = lax.broadcasted_iota(jnp.int32, (n, n), 1)
    src_b = jnp.where(src_partner, 1.0, 0.0).astype(bf16)
    dst_b = jnp.where(dst_partner, 1.0, 0.0).astype(bf16)
    power = dot_nn(src_b, dst_b).astype(bf16)
    total = jnp.where(row == col, 1.0, 0.0) + power.astype(f32)
    yield
    for _ in range(doublings - 1):
        power = dot_nn(power, power).astype(bf16)
        total = total + dot_nn(total.astype(bf16), power)
        yield
    orbit = total > 0.5
    lead_c = jnp.min(jnp.where(orbit, col, n), axis=1, keepdims=True)
    lead_r = jnp.min(jnp.where(orbit, row, n), axis=0, keepdims=True)
    other_c = jnp.sum(jnp.where(src_partner, lead_r, 0), axis=1, keepdims=True)
    other_r = jnp.sum(jnp.where(src_partner, lead_c, 0), axis=0, keepdims=True)
    return (lead_c < other_c).astype(jnp.int32), (lead_r < other_r).astype(jnp.int32)


def color_tables(dest, me):
    n = dest.shape[0]
    row = lax.broadcasted_iota(jnp.int32, (n, n), 0)
    col = lax.broadcasted_iota(jnp.int32, (n, n), 1)
    dest_t = jnp.transpose(dest.astype(f32)).astype(jnp.int32)
    owner_c, owner_r = dest >> 4, dest_t >> 4
    parity_same = (row & 1) == (col & 1)
    src_same = ((row >> 3) == (col >> 3)) & parity_same
    dst_same = (owner_c == owner_r) & parity_same
    rank_c = jnp.sum(jnp.where(dst_same & (col < row), 1, 0), axis=1, keepdims=True)
    rank_r = jnp.sum(jnp.where(dst_same & (row < col), 1, 0), axis=0, keepdims=True)
    src_partner = col == (row ^ 2)
    dst_partner = dst_same & (rank_r == (rank_c ^ 1))
    yield
    one_c, one_r = yield from split_colors(src_partner, dst_partner, 5)
    yield
    alike = (one_c == one_r) & (row != col)
    two_c, _ = yield from split_colors(src_same & alike, dst_same & alike, 4)
    yield
    color = jnp.broadcast_to(2 * one_c + two_c, (n, n))
    src = row >> 3
    pair = (row & 7) >> 1
    half = row & 1
    even = half == 0
    mine = src == me
    turn = me // 4

    def pick(mask, value):
        return jnp.sum(jnp.where(mask, value, 0), axis=0, keepdims=True)

    rows = [
        pick(mine & even & (color == col), pair),
        pick(mine & even & (pair == col), color),
        pick(even & (color == turn) & (owner_c == col), src),
        pick(even & (color == turn) & (src == col), owner_c),
        pick((owner_c == me) & ((dest & 15) == col), 2 * color + half + 1) - 1,
        pick((owner_c == me) & (2 * color + half == col), dest & 15),
    ]
    rows += [jnp.zeros_like(rows[0])] * 2
    return jnp.concatenate(rows, axis=0)


PLANES = 8
ROWS = 160
PIECE = 256
COLS = 4 * PIECE
ARRIVALS = PLANES - 1
CHUNK = 384
LOG2E = 1.4426950408889634


def softmax_over_rows(scores, allowed, scale):
    masked = jnp.where(allowed, scores, -jnp.inf)
    top = jnp.max(masked, axis=0, keepdims=True)
    terms = jnp.exp2((masked - top) * (scale * LOG2E))
    return terms * (1.0 / jnp.sum(terms, axis=0, keepdims=True))


def kernel(
    image_ref,
    dest_ref,
    kimg_ref,
    seen_ref,
    gain_ref,
    qg_ref,
    kg_ref,
    x_hbm,
    qkv_hbm,
    out_hbm,
    kv_hbm,
    q_hbm,
    og_hbm,
    att_ref,
    kvg_ref,
    x_ref,
    own_out,
    q_ref,
    og_ref,
    dest_tile,
    every,
    tab_tile,
    tab_ref,
    seen_rows,
    weight,
    out_parts,
    out_ref,
    kv_ref,
    normed,
    summed,
    mixed,
    att,
    hidden,
    pay,
    qn,
    gkv,
    got1,
    out2,
    got2,
    out3,
    got3,
    out4,
    got4,
    local_sem,
    dest_sem,
    own_sem,
    kv_sem,
    z_send,
    z_recv,
    o_send,
    o_recv,
    r_send,
    r_recv,
    m_send,
    m_recv,
    om_sem,
    send_sem,
    recv_sem,
):
    tokens, vis = x_ref.shape
    span = 2 * BLK
    e, q, m = lax.axis_index("enc"), lax.axis_index("seq"), lax.axis_index("mp")
    other = 1 - m
    d = 1 - 2 * m
    stride = 1 + 3 * m
    pos = lax.rem(q // stride, 4)
    ring = q - pos * stride
    left, right, far = lax.rem(pos + 3, 4), lax.rem(pos + 1, 4), lax.rem(pos + 2, 4)
    ahead, behind = lax.rem(e + d + PLANES, PLANES), lax.rem(e - d + PLANES, PLANES)
    to_left, to_right = {"seq": ring + left * stride}, {"seq": ring + right * stride}
    to_ahead, to_behind, to_mate = {"enc": ahead}, {"enc": behind}, {"mp": other}

    def plane_rows(plane):
        return pl.ds(pl.multiple_of(plane * ROWS, ROWS), ROWS)

    def columns(at, count):
        return pl.ds(pl.multiple_of(at, HEAD), count)

    def remote(source, target, send, recv, device):
        pltpu.make_async_remote_copy(
            src_ref=source,
            dst_ref=target,
            send_sem=send,
            recv_sem=recv,
            device_id=device,
            device_id_type=MESH,
        ).start()

    def done(view, sem):
        pltpu.make_async_copy(view, view, sem).wait()

    half_rows = ROWS // 2
    own_rows = pl.ds(pl.multiple_of(e * ROWS + m * half_rows, half_rows), half_rows)
    mate_rows = pl.ds(pl.multiple_of(e * ROWS + other * half_rows, half_rows), half_rows)
    kv_half = kv_hbm.shape[0]
    kv_rows = pl.ds(pl.multiple_of(m * kv_half, kv_half), kv_half)
    copies = [
        pltpu.make_async_copy(source, target, local_sem.at[index])
        for index, (source, target) in enumerate(
            (
                (qkv_hbm, weight.at[own_rows, pl.ds(0, qkv_hbm.shape[1])]),
                (x_hbm, x_ref),
                (out_hbm, own_out),
                (kv_hbm, kv_ref.at[kv_rows]),
                (q_hbm, q_ref),
                (og_hbm, og_ref),
                (tab_tile, tab_ref),
            )
        )
    ]
    qkv_copy, x_copy, out_copy, kv_copy, q_copy, og_copy, tab_copy = copies
    for copy in copies[:-1]:
        copy.start()

    barrier = pltpu.get_barrier_semaphore()

    def hello(step, carry):
        pl.semaphore_signal(
            barrier, inc=1, device_id={"seq": lax.rem(q + step, PEERS)}, device_id_type=MESH
        )
        return carry

    lax.fori_loop(1, PEERS, hello, 0)
    for device in (to_ahead, to_behind, to_mate):
        pl.semaphore_signal(barrier, inc=1, device_id=device, device_id_type=MESH)

    sub = lax.broadcasted_iota(jnp.int32, (8, 128), 0)
    lane = lax.broadcasted_iota(jnp.int32, (8, 128), 1)
    tile = jnp.zeros((8, 128), jnp.int32)
    for block in range(8):
        tile = jnp.where(sub == block, dest_ref[block], tile)
    dest_tile[...] = tile
    every[q] = tile
    spread = jnp.where(lane // LEN == sub, seen_ref[...].astype(f32), 0.0).astype(bf16)
    wide = (128, SHARED * LEN)
    place = lax.rem(lax.broadcasted_iota(jnp.int32, wide, 0), LEN) == lax.rem(
        lax.broadcasted_iota(jnp.int32, wide, 1), LEN
    )
    seen_rows[...] = dot_nn(spread, jnp.where(place, 1.0, 0.0).astype(bf16)).astype(jnp.int32)
    gain = jnp.concatenate([gain_ref[t : t + 1, :] for t in range(vis // 128)], axis=1)
    out_copy.wait()
    out_parts[m, e, 0 : own_out.shape[0], :] = own_out[...]
    qkv_copy.wait()
    pl.semaphore_wait(barrier, PEERS + 2)

    my_cols = columns(m * COLS + pos * PIECE, PIECE)
    for which, start in ((0, other), (1, m)):
        view = weight.at[own_rows, columns(start * COLS, COLS)]
        remote(view, view, own_sem.at[0, which], own_sem.at[1, which], to_mate)
    view = weight.at[own_rows, my_cols]
    remote(view, view, z_send.at[0], z_recv.at[0], to_ahead)
    remote(view, view, z_send.at[1], z_recv.at[1], to_behind)

    def send_dest(step, carry):
        peer = lax.rem(q + step, PEERS)
        remote(dest_tile, every.at[q], dest_sem.at[0], dest_sem.at[1], {"seq": peer})
        return carry

    lax.fori_loop(1, PEERS, send_dest, 0)
    done(weight.at[mate_rows, columns(m * COLS, COLS)], own_sem.at[1, 0])
    view = weight.at[mate_rows, my_cols]
    remote(view, view, z_send.at[0], z_recv.at[0], to_ahead)
    remote(view, view, z_send.at[1], z_recv.at[1], to_behind)
    kv_there = kv_ref.at[kv_rows]
    remote(kv_hbm, kv_there, kv_sem.at[0], kv_sem.at[1], to_mate)

    def send_z(plane, arrival, device):
        view = weight.at[plane_rows(plane), my_cols]
        remote(view, view, z_send.at[arrival], z_recv.at[arrival], device)

    def send_out(plane, arrival, device):
        view = out_parts.at[m, plane]
        remote(view, view, o_send.at[arrival], o_recv.at[arrival], device)

    def plane_of(arrival):
        hops = arrival // 2 + 1
        if arrival % 2 == 0:
            return lax.rem(e - d * hops + PLANES, PLANES)
        return lax.rem(e + d * hops + PLANES, PLANES)

    def piece(k, place):
        return weight.at[plane_rows(plane_of(k)), columns(m * COLS + place * PIECE, PIECE)]

    def part(k, place, which):
        return weight.at[
            plane_rows(plane_of(k)),
            columns(m * COLS + place * PIECE + which * (PIECE // 2), PIECE // 2),
        ]

    def pass_out(arrivals):
        for k in arrivals:
            done(out_parts.at[m, plane_of(k)], o_recv.at[k])
            if k + 2 < ARRIVALS:
                send_out(plane_of(k), k + 2, to_ahead if k % 2 == 0 else to_behind)

    chunks = 3 * VHEADS * VHEAD // CHUNK

    def norm_jobs():
        x_copy.wait()
        for t in range(tokens // 64):
            rows = slice(t * 64, t * 64 + 64)
            values = x_ref[rows, :].astype(f32)
            center = values - jnp.mean(values, axis=-1, keepdims=True)
            spread = jnp.mean(center * center, axis=-1, keepdims=True)
            result = (center * lax.rsqrt(spread + EPS) * gain).astype(bf16)
            for plane in range(PLANES):
                normed[plane, rows, :] = result[:, plane * ROWS : (plane + 1) * ROWS]
            yield

    def table_jobs():
        wait_all(every, dest_sem.at[1])
        tab_tile[...] = yield from color_tables(every[...].reshape(PEERS * 8, 128), q)
        tab_copy.start()

    def add_plane(plane, mode, begin, end):
        def body(t, carry):
            cols = pl.ds(pl.multiple_of(t * CHUNK, 128), CHUNK)
            found = dot_nn(normed[plane], weight[plane_rows(plane), cols])
            if mode == 0:
                summed[:, cols] = found
            elif mode == 1:
                summed[:, cols] += found
            else:
                mixed[:, cols] = (summed[:, cols] + found).astype(bf16)
            return carry

        lax.fori_loop(begin, end, body, 0)

    def plane_jobs(k):
        if k < 0:
            done(weight.at[mate_rows, columns(other * COLS, COLS)], own_sem.at[1, 1])
            plane = e
        else:
            same = k ^ 1 if k < ARRIVALS - 1 else k
            done(weight.at[plane_rows(e), columns(0, COLS)], m_recv.at[same])
            plane = plane_of(k)
        mode = 0 if k < 0 else 1 if k < ARRIVALS - 1 else 2
        add_plane(plane, mode, 0, 2)
        yield
        add_plane(plane, mode, 2, chunks)
        yield

    queue = [norm_jobs(), table_jobs(), plane_jobs(-1)]

    def pump(steps):
        while queue and steps > 0:
            try:
                next(queue[0])
                steps -= 1
            except StopIteration:
                queue.pop(0)

    pump(2)
    for k in range(ARRIVALS + 2):
        if k < ARRIVALS:
            done(piece(k, pos), z_recv.at[k])
            if k + 2 < ARRIVALS:
                send_z(plane_of(k), k + 2, to_ahead if k % 2 == 0 else to_behind)
            view = piece(k, pos)
            remote(view, view, r_send.at[k, 0], r_recv.at[k, 0], to_right)
            remote(view, view, r_send.at[k, 1], r_recv.at[k, 1], to_left)
        pump(2)
        j = k - 1
        if 0 <= j < ARRIVALS:
            view = part(j, left, 0)
            done(piece(j, left), r_recv.at[j, 0])
            remote(view, view, r_send.at[j, 2], r_recv.at[j, 2], to_right)
            view = part(j, right, 1)
            done(piece(j, right), r_recv.at[j, 1])
            remote(view, view, r_send.at[j, 3], r_recv.at[j, 3], to_left)
        pump(1)
        j = k - 2
        if 0 <= j < ARRIVALS:
            done(part(j, far, 0), r_recv.at[j, 2])
            done(part(j, far, 1), r_recv.at[j, 3])
            view = weight.at[plane_rows(plane_of(j)), columns(m * COLS, COLS)]
            remote(view, view, m_send.at[j], m_recv.at[j], to_mate)
        if k == 1:
            send_out(e, 0, to_ahead)
            send_out(e, 1, to_behind)
        if k == 4:
            pass_out((0, 1))
        if k == 6:
            pass_out((2, 3))
        pump(1)
        if k >= 3:
            queue.append(plane_jobs(k - 3))
    pump(1000)
    pass_out((4, 5))
    queue.append(plane_jobs(ARRIVALS - 1))
    pump(1000)

    width = VHEADS * VHEAD
    row = lax.broadcasted_iota(jnp.int32, (span, span), 0)
    col = lax.broadcasted_iota(jnp.int32, (span, span), 1)
    near = (row // BLK) == (col // BLK)

    def window(head):
        first, last = head * VHEAD // 128, ((head + 1) * VHEAD - 1) // 128
        return first, last, first * 128, (last - first + 1) * 128

    def attend_pair(j, carry):
        rows = pl.ds(pl.multiple_of(j * span, span), span)
        allowed = near | (image_ref[2 * j] == image_ref[2 * j + 1])
        insides, scores = [], []
        for head in range(VHEADS):
            _, _, base, cut = window(head)
            lanes = lax.broadcasted_iota(jnp.int32, (span, cut), 1) + base
            inside = (lanes >= head * VHEAD) & (lanes < (head + 1) * VHEAD)
            query = jnp.where(inside, mixed[rows, base : base + cut], jnp.zeros((), bf16))
            key = mixed[rows, width + base : width + base + cut]
            insides.append(inside)
            scores.append(dot_nt(key, query))
        weights = [
            softmax_over_rows(found, allowed, 1.0 / math.sqrt(VHEAD)).astype(bf16)
            for found in scores
        ]
        tiles = [None] * (width // 128)
        for head in range(VHEADS):
            first, last, base, cut = window(head)
            value = mixed[rows, 2 * width + base : 2 * width + base + cut]
            result = dot_tn(weights[head], value)
            for t in range(first, last + 1):
                at = (t - first) * 128
                found = result[:, at : at + 128]
                if tiles[t] is not None:
                    found = jnp.where(insides[head][:, at : at + 128], found, tiles[t])
                tiles[t] = found
        att[rows, :] = jnp.concatenate(tiles, axis=1).astype(bf16)
        return carry

    lax.fori_loop(0, PAIRS // 2, attend_pair, 0)
    pass_out((6,))
    remote(out_parts.at[m], out_parts.at[m], om_sem.at[0], om_sem.at[1], to_mate)
    lax.fori_loop(PAIRS // 2, PAIRS, attend_pair, 0)

    done(out_parts.at[other], om_sem.at[1])
    have = own_out.shape[0]
    for plane in range(PLANES):
        both = [out_parts[core, plane, 0:have, :].astype(f32) for core in range(2)]
        out_ref[2 * have * plane : 2 * have * (plane + 1), :] = jnp.concatenate(
            both, axis=0
        ).astype(bf16)

    def project(t, carry):
        cols = pl.ds(pl.multiple_of(t * 256, 256), 256)
        total = x_ref[:, cols].astype(f32) + dot_nn(att[...], out_ref[:, cols])
        hidden[:, :, cols] = total.astype(bf16).reshape(PAIRS, span, 256)
        return carry

    lax.fori_loop(0, vis // 256, project, 0)

    tab_copy.wait()
    kv_copy.wait()
    done(kv_there, kv_sem.at[1])
    half = KVHEADS * HEAD
    for h in range(PIECES):
        source = jnp.concatenate([hidden[tab_ref[0, c] & 3] for c in range(PAIRS)], axis=0)
        for t in range(PER):
            at = (h * PER + t) * HEAD
            both = jnp.concatenate(
                [kv_ref[:, at : at + HEAD], kv_ref[:, half + at : half + at + HEAD]], axis=1
            )
            pay[h][:, :, t * 2 * HEAD : (t + 1) * 2 * HEAD] = (
                dot_nn(source, both).astype(bf16).reshape(PEERS, span // 4, 2 * HEAD)
            )
        exchange(pay[h], got1[h], q, send_sem.at[0, h], recv_sem.at[0, h])

    q_copy.wait()

    def norm_queries(g, carry):
        block = q_ref[:, pl.ds(pl.multiple_of(g * SHARED * HEAD, HEAD), SHARED * HEAD)]
        for hh in range(SHARED):
            x = block[:, hh * HEAD : (hh + 1) * HEAD].astype(f32)
            inv = lax.rsqrt(jnp.mean(x * x, axis=-1, keepdims=True) + EPS)
            y = (x * inv * qg_ref[...]).astype(bf16)
            for s in range(CAP):
                qn[g, s, hh * LEN : (hh + 1) * LEN, :] = y[s * LEN : (s + 1) * LEN, :]
        return carry

    lax.fori_loop(0, KVHEADS, norm_queries, 0)
    og_copy.wait()

    def relay(h, got, out, table, target, phase):
        wait_all(got[h], recv_sem.at[phase - 1, h])

        def body(index, carry):
            out[h][index] = got[h][tab_ref[table, index] & 15]
            return carry

        lax.fori_loop(0, PEERS, body, 0)
        exchange(out[h], target[h], q, send_sem.at[phase, h], recv_sem.at[phase, h])

    def one(h, gi, s):
        g = h * PER + gi
        at = pl.multiple_of(gi * 2 * HEAD, 2 * HEAD)
        blocks, masks = [], []
        seen = seen_rows[pl.ds(s, 1), :]
        for kb in range(CAP):
            index = tab_ref[4, s * CAP + kb]
            block = got2[h][pl.ds(2 * (jnp.maximum(index, 0) & 7), 2), :, pl.ds(at, 2 * HEAD)]
            blocks.append(
                jnp.where(index >= 0, block, jnp.zeros((), bf16)).reshape(BLK, 2 * HEAD)
            )
            masks.append(jnp.broadcast_to(kimg_ref[s, kb] < seen, (BLK, SHARED * LEN)))
        keyval = jnp.concatenate(blocks, axis=0)
        allowed = jnp.concatenate(masks, axis=0)
        keys = keyval[:, :HEAD].astype(f32)
        values = keyval[:, HEAD:]
        inv = lax.rsqrt(jnp.mean(keys * keys, axis=-1, keepdims=True) + EPS)
        kn = (keys * inv * kg_ref[...]).astype(bf16)
        queries = qn[g, s]
        rows = pl.ds(pl.multiple_of(s * LEN, LEN), LEN)
        cols = pl.ds(pl.multiple_of(g * SHARED * HEAD, SHARED * HEAD), SHARED * HEAD)
        grad_row = og_ref[rows, cols]
        grads = jnp.concatenate(
            [grad_row[:, hh * HEAD : (hh + 1) * HEAD] for hh in range(SHARED)], axis=0
        )
        scale = 1.0 / math.sqrt(HEAD)
        weights = softmax_over_rows(dot_nt(kn, queries), allowed, scale)
        rounded = weights.astype(bf16)
        attended = dot_tn(rounded, values).astype(bf16)
        att_ref[rows, cols] = jnp.concatenate(
            [attended[hh * LEN : (hh + 1) * LEN, :] for hh in range(SHARED)], axis=1
        )
        grad_values = dot_nn(rounded, grads)
        grad_dot = dot_nt(values, grads)
        delta = jnp.sum(weights * grad_dot, axis=0, keepdims=True)
        grad_scores = (weights * (grad_dot - delta) * scale).astype(bf16)
        gained = dot_nn(grad_scores, queries) * kg_ref[...]
        mean = jnp.mean(keys * gained, axis=-1, keepdims=True)
        grad_keys = inv * (gained - keys * inv * inv * mean)
        result = jnp.concatenate([grad_keys, grad_values], axis=1).astype(bf16)
        gkv[pl.ds(s * CAP, CAP), :, pl.ds(at, 2 * HEAD)] = result.reshape(CAP, BLK, 2 * HEAD)

    def attend(h):
        wait_all(got2[h], recv_sem.at[1, h])

        def body(step, carry):
            gi, s = step // (CAP // 2), lax.rem(step, CAP // 2) * 2
            one(h, gi, s)
            one(h, gi, s + 1)
            return carry

        lax.fori_loop(0, PER * CAP // 2, body, 0)

        def pack(cb, carry):
            block = gkv[tab_ref[5, cb] & 15]
            out3[h][pl.ds(2 * cb, 2)] = block.reshape(2, BLK // 2, WIDE)
            return carry

        lax.fori_loop(0, 2 * PAIRS, pack, 0)
        exchange(out3[h], got3[h], q, send_sem.at[2, h], recv_sem.at[2, h])

    for h in range(PIECES):
        relay(h, got1, out2, 2, got2, 1)
    for h in range(PIECES):
        attend(h)
        if h > 0:
            relay(h - 1, got3, out4, 3, got4, 3)
    relay(PIECES - 1, got3, out4, 3, got4, 3)
    for h in range(PIECES):
        wait_all(got4[h], recv_sem.at[3, h])
        for j in range(PAIRS):
            color = tab_ref[1, j] & 3
            block = got4[h][pl.ds(4 * color, 4)].reshape(2, BLK, WIDE)
            for gi in range(PER):
                at = (h * PER + gi) * HEAD
                kvg_ref[2 * j : 2 * j + 2, :, at : at + HEAD] = block[
                    :, :, gi * 2 * HEAD : gi * 2 * HEAD + HEAD
                ]
                kvg_ref[2 * j : 2 * j + 2, :, half + at : half + at + HEAD] = block[
                    :, :, gi * 2 * HEAD + HEAD : (gi + 1) * 2 * HEAD
                ]

    for phase in range(4):
        for h in range(PIECES):
            wait_all(got1[h], send_sem.at[phase, h])
    wait_all(every, dest_sem.at[0])
    for which, start in ((0, other), (1, m)):
        done(weight.at[own_rows, columns(start * COLS, COLS)], own_sem.at[0, which])
    done(kv_there, kv_sem.at[0])
    done(out_parts.at[m], om_sem.at[0])
    for k in range(ARRIVALS):
        done(piece(k, pos), z_send.at[k])
        done(out_parts.at[m, e], o_send.at[k])
        for way in range(4):
            done(piece(k, pos) if way < 2 else part(k, pos, 0), r_send.at[k, way])
        done(weight.at[plane_rows(e), columns(0, COLS)], m_send.at[k])


VMEM = pl.BlockSpec(memory_space=pltpu.VMEM)
SMEM = pl.BlockSpec(memory_space=pltpu.SMEM)
HBM = pl.BlockSpec(memory_space=pltpu.HBM)
LIMIT = 62 * 1024 * 1024


def local(
    images,
    vit_gain,
    vit_qkv,
    vit_out,
    kv_weight,
    queries,
    q_gain,
    k_gain,
    out_grad,
    block_image,
    block_dest,
    key_image,
    text_seen,
):
    enc_blocks, block_len, vis = images.shape
    tokens = enc_blocks * block_len
    buffers = [pltpu.VMEM((PEERS, BLK // 2, WIDE), bf16)] * PIECES
    dma = pltpu.SemaphoreType.DMA
    return pl.pallas_call(
        kernel,
        out_shape=(
            jax.ShapeDtypeStruct(queries.shape, bf16),
            jax.ShapeDtypeStruct((enc_blocks, block_len, 2 * KVHEADS * HEAD), bf16),
        ),
        in_specs=[SMEM] * 3 + [VMEM] * 4 + [HBM] * 6,
        out_specs=(VMEM, VMEM),
        scratch_shapes=[
            pltpu.VMEM((tokens, vis), bf16),
            pltpu.VMEM(vit_out.shape, bf16),
            pltpu.VMEM(queries.shape, bf16),
            pltpu.VMEM(queries.shape, bf16),
            pltpu.VMEM((8, 128), jnp.int32),
            pltpu.VMEM((PEERS, 8, 128), jnp.int32),
            pltpu.VMEM((8, 128), jnp.int32),
            pltpu.SMEM((8, 128), jnp.int32),
            pltpu.VMEM((8, SHARED * LEN), jnp.int32),
            pltpu.VMEM((vis, 2 * COLS), bf16),
            pltpu.VMEM((2, PLANES, 48, vis), bf16),
            pltpu.VMEM((VHEADS * VHEAD, vis), bf16),
            pltpu.VMEM((vis, 2 * KVHEADS * HEAD), bf16),
            pltpu.VMEM((PLANES, tokens, ROWS), bf16),
            pltpu.VMEM((tokens, 3 * VHEADS * VHEAD), f32),
            pltpu.VMEM((tokens, 3 * VHEADS * VHEAD), bf16),
            pltpu.VMEM((tokens, VHEADS * VHEAD), bf16),
            pltpu.VMEM((PAIRS, 2 * BLK, vis), bf16),
            buffers,
            pltpu.VMEM((KVHEADS, CAP, SHARED * LEN, HEAD), bf16),
            pltpu.VMEM((CAP * CAP, BLK, WIDE), bf16),
        ]
        + [buffers] * 7
        + [dma((7,)), dma((2,)), dma((2, 2)), dma((2,))]
        + [dma((ARRIVALS,))] * 4
        + [dma((ARRIVALS, 4))] * 2
        + [dma((ARRIVALS,))] * 2
        + [dma((2,))]
        + [dma((4, PIECES))] * 2,
        compiler_params=pltpu.CompilerParams(
            collective_id=0, has_side_effects=True, vmem_limit_bytes=LIMIT
        ),
    )(
        block_image,
        block_dest,
        key_image,
        text_seen.reshape(1, -1),
        vit_gain.reshape(-1, 128),
        q_gain.reshape(1, HEAD),
        k_gain.reshape(1, HEAD),
        images.reshape(tokens, vis),
        vit_qkv,
        vit_out,
        kv_weight,
        queries,
        out_grad,
    )


def solution(mesh):
    everywhere = ("enc", "seq", "mp")
    placed = (
        P(everywhere, None, None),
        P(),
        P(("enc", "mp"), None),
        P(("enc", "mp"), None),
        P("mp", None),
        P(everywhere, None),
        P(),
        P(),
        P(everywhere, None),
        P(everywhere),
        P(everywhere),
        P(everywhere, None),
        P(everywhere),
    )
    return jax.shard_map(
        local,
        mesh=mesh,
        in_specs=placed,
        out_specs=(P(everywhere, None), P(everywhere, None, None)),
        check_vma=False,
    )
```

```python
import math

import jax
import jax.numpy as jnp
from jax import lax
from jax.experimental import pallas as pl
from jax.experimental.pallas import tpu as pltpu
from jax.sharding import PartitionSpec as P

VHEADS = 8
VHEAD = 80
HEAD = 128
KVHEADS = 4
SHARED = 8
BLK = 64
LEN = 32
CAP = 4
PEERS = 16
PAIRS = 4
PIECES = 4
PER = KVHEADS // PIECES
WIDE = PER * 2 * HEAD
GROUPS = 2
GROUP = KVHEADS // GROUPS
GWIDE = GROUP * 2 * HEAD
EPS = 1e-05
MESH = pl.DeviceIdType.MESH
f32 = jnp.float32
bf16 = jnp.bfloat16


def dot_nn(left, right):
    return jnp.dot(left, right, preferred_element_type=f32)


def dot_nt(left, right):
    return lax.dot_general(left, right, (((1,), (1,)), ((), ())), preferred_element_type=f32)


def dot_tn(left, right):
    return lax.dot_general(left, right, (((0,), (0,)), ((), ())), preferred_element_type=f32)


def exchange(source, target, me, send_sem, recv_sem, own_sem=None):
    def body(step, carry):
        peer = lax.rem(me + step, PEERS)
        pltpu.make_async_remote_copy(
            src_ref=source.at[peer],
            dst_ref=target.at[me],
            send_sem=send_sem,
            recv_sem=recv_sem,
            device_id={"seq": peer},
            device_id_type=MESH,
        ).start()
        return carry

    lax.fori_loop(1, PEERS, body, 0)
    if own_sem is None:
        target[me] = source[me]
    else:
        pltpu.make_async_copy(source.at[me], target.at[me], own_sem).start()


def wait_all(buffer, sem):
    view = buffer.at[pl.ds(0, PEERS - 1)]
    pltpu.make_async_copy(view, view, sem).wait()


def split_colors(src_partner, dst_partner, doublings):
    n = src_partner.shape[0]
    row = lax.broadcasted_iota(jnp.int32, (n, n), 0)
    col = lax.broadcasted_iota(jnp.int32, (n, n), 1)
    src_b = jnp.where(src_partner, 1.0, 0.0).astype(bf16)
    dst_b = jnp.where(dst_partner, 1.0, 0.0).astype(bf16)
    power = dot_nn(src_b, dst_b).astype(bf16)
    total = jnp.where(row == col, 1.0, 0.0) + power.astype(f32)
    yield
    for _ in range(doublings - 1):
        power = dot_nn(power, power).astype(bf16)
        total = total + dot_nn(total.astype(bf16), power)
        yield
    orbit = total > 0.5
    lead_c = jnp.min(jnp.where(orbit, col, n), axis=1, keepdims=True)
    lead_r = jnp.min(jnp.where(orbit, row, n), axis=0, keepdims=True)
    other_c = jnp.sum(jnp.where(src_partner, lead_r, 0), axis=1, keepdims=True)
    other_r = jnp.sum(jnp.where(src_partner, lead_c, 0), axis=0, keepdims=True)
    return (lead_c < other_c).astype(jnp.int32), (lead_r < other_r).astype(jnp.int32)


def color_tables(dest, me):
    n = dest.shape[0]
    row = lax.broadcasted_iota(jnp.int32, (n, n), 0)
    col = lax.broadcasted_iota(jnp.int32, (n, n), 1)
    dest_t = jnp.transpose(dest.astype(f32)).astype(jnp.int32)
    owner_c, owner_r = dest >> 4, dest_t >> 4
    parity_same = (row & 1) == (col & 1)
    src_same = ((row >> 3) == (col >> 3)) & parity_same
    dst_same = (owner_c == owner_r) & parity_same
    rank_c = jnp.sum(jnp.where(dst_same & (col < row), 1, 0), axis=1, keepdims=True)
    rank_r = jnp.sum(jnp.where(dst_same & (row < col), 1, 0), axis=0, keepdims=True)
    src_partner = col == (row ^ 2)
    dst_partner = dst_same & (rank_r == (rank_c ^ 1))
    yield
    one_c, one_r = yield from split_colors(src_partner, dst_partner, 5)
    yield
    alike = (one_c == one_r) & (row != col)
    two_c, _ = yield from split_colors(src_same & alike, dst_same & alike, 4)
    yield
    color = jnp.broadcast_to(2 * one_c + two_c, (n, n))
    src = row >> 3
    pair = (row & 7) >> 1
    half = row & 1
    even = half == 0
    mine = src == me
    turn, turn2 = me // 4, me // 8

    def pick(mask, value):
        return jnp.sum(jnp.where(mask, value, 0), axis=0, keepdims=True)

    rows = [
        pick(mine & even & (color == col), pair),
        pick(mine & even & (pair == col), color),
        pick(even & (color == turn2) & (owner_c == col), src),
        pick(even & (color == turn) & (src == col), owner_c),
        pick((owner_c == me) & ((dest & 15) == col), 2 * color + half + 1) - 1,
        pick((owner_c == me) & (2 * color + half == col), dest & 15),
        pick(even & (color == 2 + turn2) & (owner_c == col), src),
    ]
    rows += [jnp.zeros_like(rows[0])]
    return jnp.concatenate(rows, axis=0)


PLANES = 8
ROWS = 160
PIECE = 256
ARRIVALS = PLANES - 1
WINDOW = 384
LOG2E = 1.4426950408889634


def softmax_over_rows(scores, allowed, scale):
    masked = jnp.where(allowed, scores, -jnp.inf)
    top = jnp.max(masked, axis=0, keepdims=True)
    terms = jnp.exp2((masked - top) * (scale * LOG2E))
    return terms * (1.0 / jnp.sum(terms, axis=0, keepdims=True))


def kernel(
    image_ref,
    dest_ref,
    kimg_ref,
    seen_ref,
    gain_ref,
    qg_ref,
    kg_ref,
    x_hbm,
    qkv_hbm,
    out_hbm,
    kv_hbm,
    q_hbm,
    og_hbm,
    att_hbm,
    back_hbm,
    tab_hbm,
    x_ref,
    own_out,
    own_qkv,
    q_ref,
    og_ref,
    att_ref,
    dest_tile,
    every,
    tab_tile,
    tab_ref,
    seen_rows,
    weight,
    out_parts,
    out_ref,
    kv_ref,
    normed,
    summed,
    mixed,
    att,
    hidden,
    pay,
    qn,
    gkv,
    got1,
    out2,
    got2,
    out3,
    got3,
    out4,
    local_sem,
    dest_sem,
    own_sem,
    kv_sem,
    z_send,
    z_recv,
    o_send,
    o_recv,
    r_send,
    r_recv,
    m_send,
    m_recv,
    ro_send,
    ro_recv,
    mo_send,
    mo_recv,
    oo_sem,
    att_sem,
    own_back,
    f_send,
    f_recv,
    send_sem,
    recv_sem,
):
    pairs_here, span, vis = x_ref.shape
    tokens = pairs_here * span
    e, q, m = lax.axis_index("enc"), lax.axis_index("seq"), lax.axis_index("mp")
    other = 1 - m
    d = 1 - 2 * m
    stride = 1 + 3 * m
    pos = lax.rem(q // stride, 4)
    ring = q - pos * stride
    left, right, far = lax.rem(pos + 3, 4), lax.rem(pos + 1, 4), lax.rem(pos + 2, 4)
    ahead, behind = lax.rem(e + d + PLANES, PLANES), lax.rem(e - d + PLANES, PLANES)
    to_left, to_right = {"seq": ring + left * stride}, {"seq": ring + right * stride}
    to_ahead, to_behind, to_mate = {"enc": ahead}, {"enc": behind}, {"mp": other}

    def remote(source, target, send, recv, device):
        pltpu.make_async_remote_copy(
            src_ref=source,
            dst_ref=target,
            send_sem=send,
            recv_sem=recv,
            device_id=device,
            device_id_type=MESH,
        ).start()

    def done(view, sem):
        pltpu.make_async_copy(view, view, sem).wait()

    half_rows = ROWS // 2
    own_rows = pl.ds(pl.multiple_of(m * half_rows, half_rows), half_rows)
    mate_rows = pl.ds(pl.multiple_of(other * half_rows, half_rows), half_rows)
    kv_half = kv_hbm.shape[0]
    kv_rows = pl.ds(pl.multiple_of(m * kv_half, kv_half), kv_half)
    copies = [
        pltpu.make_async_copy(source, target, local_sem.at[index])
        for index, (source, target) in enumerate(
            (
                (qkv_hbm, own_qkv),
                (x_hbm, x_ref),
                (out_hbm, own_out),
                (kv_hbm, kv_ref.at[kv_rows]),
                (q_hbm, q_ref),
                (og_hbm, og_ref),
                (tab_tile, tab_ref),
                (tab_tile, tab_hbm),
            )
        )
    ]
    qkv_copy, x_copy, out_copy, kv_copy, q_copy, og_copy, tab_copy, tab_out = copies
    for copy in copies[:-2]:
        copy.start()

    barrier = pltpu.get_barrier_semaphore()

    def hello(step, carry):
        pl.semaphore_signal(
            barrier, inc=1, device_id={"seq": lax.rem(q + step, PEERS)}, device_id_type=MESH
        )
        return carry

    lax.fori_loop(1, PEERS, hello, 0)
    for device in (to_ahead, to_behind, to_mate):
        pl.semaphore_signal(barrier, inc=1, device_id=device, device_id_type=MESH)

    sub = lax.broadcasted_iota(jnp.int32, (8, 128), 0)
    lane = lax.broadcasted_iota(jnp.int32, (8, 128), 1)
    tile = jnp.zeros((8, 128), jnp.int32)
    for block in range(8):
        tile = jnp.where(sub == block, dest_ref[block], tile)
    dest_tile[...] = tile
    every[q] = tile
    spread = jnp.where(lane // LEN == sub, seen_ref[...].astype(f32), 0.0).astype(bf16)
    wide = (128, SHARED * LEN)
    place = lax.rem(lax.broadcasted_iota(jnp.int32, wide, 0), LEN) == lax.rem(
        lax.broadcasted_iota(jnp.int32, wide, 1), LEN
    )
    seen_rows[...] = dot_nn(spread, jnp.where(place, 1.0, 0.0).astype(bf16)).astype(jnp.int32)
    gain = jnp.concatenate([gain_ref[t : t + 1, :] for t in range(vis // 128)], axis=1)
    out_copy.wait()
    have = own_out.shape[0]
    for place in range(4):
        at = min(place * WINDOW, vis - WINDOW)
        out_parts[m, e, place, 0:have, :] = own_out[:, at : at + WINDOW]
    qkv_copy.wait()
    for p in range(8):
        count = min(PIECE, own_qkv.shape[1] - p * PIECE)
        weight[p, e, own_rows, 0:count] = own_qkv[:, p * PIECE : p * PIECE + count]
    pl.semaphore_wait(barrier, PEERS + 2)

    mine = 4 * m + pos

    def side(core):
        return pl.ds(4 * core, 4)

    for which, core in ((0, other), (1, m)):
        view = weight.at[side(core), e, own_rows]
        remote(view, view, own_sem.at[0, which], own_sem.at[1, which], to_mate)

    def send_z(plane, which, arrival):
        view = weight.at[mine, plane, mate_rows if which else own_rows]
        device = to_behind if arrival % 2 else to_ahead
        remote(view, view, z_send.at[arrival, which], z_recv.at[arrival, which], device)

    send_z(e, 0, 0)
    send_z(e, 0, 1)
    view = out_parts.at[m, e]
    remote(view, view, oo_sem.at[0], oo_sem.at[1], to_mate)

    def send_dest(step, carry):
        peer = lax.rem(q + step, PEERS)
        remote(dest_tile, every.at[q], dest_sem.at[0], dest_sem.at[1], {"seq": peer})
        return carry

    lax.fori_loop(1, PEERS, send_dest, 0)
    done(weight.at[side(m), e, mate_rows], own_sem.at[1, 0])
    send_z(e, 1, 0)
    send_z(e, 1, 1)
    kv_there = kv_ref.at[kv_rows]

    def send_out(plane, arrival):
        view = out_parts.at[m, plane, pos]
        device = to_behind if arrival % 2 else to_ahead
        remote(view, view, o_send.at[arrival], o_recv.at[arrival], device)

    def plane_of(arrival):
        hops = arrival // 2 + 1
        if arrival % 2 == 0:
            return lax.rem(e - d * hops + PLANES, PLANES)
        return lax.rem(e + d * hops + PLANES, PLANES)

    def piece(k, place):
        return weight.at[4 * m + place, plane_of(k)]

    def part(k, place, which):
        return weight.at[4 * m + place, plane_of(k), pl.ds(which * half_rows, half_rows)]

    width = VHEADS * VHEAD

    def norm_jobs():
        x_copy.wait()
        for t in range(tokens // 64):
            rows = slice(t * 64, t * 64 + 64)
            values = x_ref[t // 2, t % 2 * 64 : t % 2 * 64 + 64, :].astype(f32)
            center = values - jnp.mean(values, axis=-1, keepdims=True)
            spread = jnp.mean(center * center, axis=-1, keepdims=True)
            result = (center * lax.rsqrt(spread + EPS) * gain).astype(bf16)
            for plane in range(PLANES):
                normed[plane, rows, :] = result[:, plane * ROWS : (plane + 1) * ROWS]
            yield

    def table_jobs():
        wait_all(every, dest_sem.at[1])
        tab_tile[...] = yield from color_tables(every[...].reshape(PEERS * 8, 128), q)
        tab_copy.start()
        tab_out.start()

    def add_plane(plane, mode, p):
        count = min(PIECE, 3 * width - p * PIECE)
        cols = slice(p * PIECE, p * PIECE + count)
        found = dot_nn(normed[plane], weight[p, plane, :, 0:count])
        if mode == 0:
            summed[:, cols] = found
        elif mode == 1:
            summed[:, cols] += found
        else:
            total = (summed[:, cols] + found).astype(bf16)
            mixed[:, :, cols] = total.reshape(PAIRS, span, count)

    def plane_jobs(k):
        if k < 0:
            done(weight.at[side(other), e, mate_rows], own_sem.at[1, 1])
            plane = e
        else:
            same = k ^ 1 if k < ARRIVALS - 1 else k
            done(weight.at[side(m), e], m_recv.at[same])
            plane = plane_of(k)
        mode = 0 if k < 0 else 1 if k < ARRIVALS - 1 else 2
        for p in range(8):
            add_plane(plane, mode, p)
            if p % 3 == 2:
                yield
        yield

    def out_jobs(k):
        if k < 0:
            plane = e
            done(out_parts.at[m, e], oo_sem.at[1])
        else:
            plane = plane_of(k)
            done(out_parts.at[m, e], mo_recv.at[k ^ 1 if k < ARRIVALS - 1 else k])
        both = []
        for core in range(2):
            parts = [out_parts[core, plane, place, 0:have, :] for place in range(4)]
            parts[3] = parts[3][:, 4 * WINDOW - vis :]
            both.append(jnp.concatenate(parts, axis=1).astype(f32))
        rows = pl.ds(pl.multiple_of(2 * have * plane, 2 * have), 2 * have)
        out_ref[rows, :] = jnp.concatenate(both, axis=0).astype(bf16)
        yield

    queue = [norm_jobs(), table_jobs(), plane_jobs(-1)]

    def pump(steps):
        while queue and steps > 0:
            try:
                next(queue[0])
                steps -= 1
            except StopIteration:
                queue.pop(0)

    send_out(e, 0)
    send_out(e, 1)
    remote(kv_hbm, kv_there, kv_sem.at[0], kv_sem.at[1], to_mate)
    pump(2)
    hops = ((0, 1), (2, 3), (4, 5), (6,))
    for t in range(len(hops) + 2):
        if t < len(hops):
            for which in range(2):
                for k in hops[t]:
                    rows = mate_rows if which else own_rows
                    done(weight.at[mine, plane_of(k), rows], z_recv.at[k, which])
                    if k + 2 < ARRIVALS:
                        send_z(plane_of(k), which, k + 2)
            for k in hops[t]:
                view = piece(k, pos)
                remote(view, view, r_send.at[k, 0], r_recv.at[k, 0], to_right)
                remote(view, view, r_send.at[k, 1], r_recv.at[k, 1], to_left)
            for k in hops[t]:
                view = out_parts.at[m, plane_of(k), pos]
                done(view, o_recv.at[k])
                if k + 2 < ARRIVALS:
                    send_out(plane_of(k), k + 2)
                remote(view, view, ro_send.at[k, 0], ro_recv.at[k, 0], to_right)
                remote(view, view, ro_send.at[k, 1], ro_recv.at[k, 1], to_left)
        pump(2)
        if 0 <= t - 1 < len(hops):
            for k in hops[t - 1]:
                view = part(k, left, 0)
                done(piece(k, left), r_recv.at[k, 0])
                remote(view, view, r_send.at[k, 2], r_recv.at[k, 2], to_right)
                view = part(k, right, 1)
                done(piece(k, right), r_recv.at[k, 1])
                remote(view, view, r_send.at[k, 3], r_recv.at[k, 3], to_left)
            for k in hops[t - 1]:
                from_left = out_parts.at[m, plane_of(k), left]
                from_right = out_parts.at[m, plane_of(k), right]
                done(from_left, ro_recv.at[k, 0])
                done(from_right, ro_recv.at[k, 1])
                if k % 2 == 0:
                    remote(from_left, from_left, ro_send.at[k, 2], ro_recv.at[k, 2], to_right)
                else:
                    remote(from_right, from_right, ro_send.at[k, 2], ro_recv.at[k, 2], to_left)
        pump(2)
        if 0 <= t - 2 < len(hops):
            for k in hops[t - 2]:
                done(part(k, far, 0), r_recv.at[k, 2])
                done(part(k, far, 1), r_recv.at[k, 3])
                view = weight.at[side(m), plane_of(k)]
                remote(view, view, m_send.at[k], m_recv.at[k], to_mate)
            for k in hops[t - 2]:
                done(out_parts.at[m, plane_of(k), far], ro_recv.at[k, 2])
                view = out_parts.at[m, plane_of(k)]
                remote(view, view, mo_send.at[k], mo_recv.at[k], to_mate)
        pump(2)
        if t == 1:
            queue.append(out_jobs(-1))
        if 0 <= t - 2 < len(hops):
            queue.extend(plane_jobs(k) for k in hops[t - 2])
        if 0 <= t - 3 < len(hops):
            queue.extend(out_jobs(k) for k in hops[t - 3])
    pump(1000)
    queue.append(out_jobs(ARRIVALS - 1))

    row = lax.broadcasted_iota(jnp.int32, (span, span), 0)
    col = lax.broadcasted_iota(jnp.int32, (span, span), 1)
    near = (row // BLK) == (col // BLK)

    def window(head):
        first, last = head * VHEAD // 128, ((head + 1) * VHEAD - 1) // 128
        return first, last, first * 128, (last - first + 1) * 128

    def attend_pair(c):
        pair = tab_ref[0, c] & 3
        allowed = near | (image_ref[2 * pair] == image_ref[2 * pair + 1])
        insides, scores = [], []
        for head in range(VHEADS):
            _, _, base, cut = window(head)
            lanes = lax.broadcasted_iota(jnp.int32, (span, cut), 1) + base
            inside = (lanes >= head * VHEAD) & (lanes < (head + 1) * VHEAD)
            query = jnp.where(inside, mixed[pair, :, base : base + cut], jnp.zeros((), bf16))
            key = mixed[pair, :, width + base : width + base + cut]
            insides.append(inside)
            scores.append(dot_nt(key, query))
        weights = [
            softmax_over_rows(found, allowed, 1.0 / math.sqrt(VHEAD)).astype(bf16)
            for found in scores
        ]
        tiles = [None] * (width // 128)
        for head in range(VHEADS):
            first, last, base, cut = window(head)
            value = mixed[pair, :, 2 * width + base : 2 * width + base + cut]
            result = dot_tn(weights[head], value)
            for t in range(first, last + 1):
                at = (t - first) * 128
                found = result[:, at : at + 128]
                if tiles[t] is not None:
                    found = jnp.where(insides[head][:, at : at + 128], found, tiles[t])
                tiles[t] = found
        att[c] = jnp.concatenate(tiles, axis=1).astype(bf16)

    half = KVHEADS * HEAD
    tab_copy.wait()
    for a in range(2):
        pairs = (2 * a, 2 * a + 1)

        def attend_pairs(c, carry):
            attend_pair(c)
            return carry

        lax.fori_loop(pairs[0], pairs[1] + 1, attend_pairs, 0)
        if a == 0:
            pump(1000)
        attended = jnp.concatenate([att[c] for c in pairs], axis=0)

        def project(t, carry):
            cols = pl.ds(pl.multiple_of(t * 256, 256), 256)
            tokens_in = jnp.concatenate(
                [x_ref[tab_ref[0, c] & 3, :, cols] for c in pairs], axis=0
            )
            total = tokens_in.astype(f32) + dot_nn(attended, out_ref[:, cols])
            hidden[a, :, cols] = total.astype(bf16)
            return carry

        lax.fori_loop(0, vis // 256, project, 0)
        if a == 0:
            kv_copy.wait()
            done(kv_there, kv_sem.at[1])
        for b in range(GROUPS):
            for t in range(GROUP):
                at = (b * GROUP + t) * HEAD
                both = jnp.concatenate(
                    [kv_ref[:, at : at + HEAD], kv_ref[:, half + at : half + at + HEAD]], axis=1
                )
                pay[a][b][:, :, t * 2 * HEAD : (t + 1) * 2 * HEAD] = (
                    dot_nn(hidden[a], both).astype(bf16).reshape(PEERS, BLK // 4, 2 * HEAD)
                )
            exchange(pay[a][b], got1[a][b], q, f_send.at[0, a, b], f_recv.at[0, a, b])

    q_copy.wait()

    def norm_queries(g, carry):
        block = q_ref[:, pl.ds(pl.multiple_of(g * SHARED * HEAD, HEAD), SHARED * HEAD)]
        for hh in range(SHARED):
            x = block[:, hh * HEAD : (hh + 1) * HEAD].astype(f32)
            inv = lax.rsqrt(jnp.mean(x * x, axis=-1, keepdims=True) + EPS)
            y = (x * inv * qg_ref[...]).astype(bf16)
            for s in range(CAP):
                qn[g, s, hh * LEN : (hh + 1) * LEN, :] = y[s * LEN : (s + 1) * LEN, :]
        return carry

    lax.fori_loop(0, KVHEADS, norm_queries, 0)
    og_copy.wait()

    def shuffle(got, out, table):
        def body(index, carry):
            out[index] = got[tab_ref[table, index] & 15]
            return carry

        lax.fori_loop(0, PEERS, body, 0)

    def relay(a, b):
        wait_all(got1[a][b], f_recv.at[0, a, b])
        shuffle(got1[a][b], out2[a][b], 6 if a else 2)
        exchange(out2[a][b], got2[b].at[pl.ds(a * PEERS, PEERS)], q, f_send.at[1, a, b], f_recv.at[1, a, b])

    def give_back(h):
        wait_all(got3[h], recv_sem.at[0, h])
        shuffle(got3[h], out4[h], 3)
        exchange(out4[h], back_hbm.at[h], q, send_sem.at[1, h], recv_sem.at[1, h], own_back.at[h])

    def one(h, gi, s):
        g = h * PER + gi
        at = pl.multiple_of(gi * 2 * HEAD, 2 * HEAD)
        group = h * PER // GROUP
        from_col = pl.multiple_of((h * PER % GROUP + gi) * 2 * HEAD, 2 * HEAD)
        blocks, masks = [], []
        seen = seen_rows[pl.ds(s, 1), :]
        for kb in range(CAP):
            index = tab_ref[4, s * CAP + kb]
            start = 4 * (jnp.maximum(index, 0) & 7)
            block = got2[group][pl.ds(start, 4), :, pl.ds(from_col, 2 * HEAD)]
            blocks.append(
                jnp.where(index >= 0, block, jnp.zeros((), bf16)).reshape(BLK, 2 * HEAD)
            )
            masks.append(jnp.broadcast_to(kimg_ref[s, kb] < seen, (BLK, SHARED * LEN)))
        keyval = jnp.concatenate(blocks, axis=0)
        allowed = jnp.concatenate(masks, axis=0)
        keys = keyval[:, :HEAD].astype(f32)
        values = keyval[:, HEAD:]
        inv = lax.rsqrt(jnp.mean(keys * keys, axis=-1, keepdims=True) + EPS)
        kn = (keys * inv * kg_ref[...]).astype(bf16)
        queries = qn[g, s]
        rows = pl.ds(pl.multiple_of(s * LEN, LEN), LEN)
        cols = pl.ds(pl.multiple_of(g * SHARED * HEAD, SHARED * HEAD), SHARED * HEAD)
        grad_row = og_ref[rows, cols]
        grads = jnp.concatenate(
            [grad_row[:, hh * HEAD : (hh + 1) * HEAD] for hh in range(SHARED)], axis=0
        )
        scale = 1.0 / math.sqrt(HEAD)
        weights = softmax_over_rows(dot_nt(kn, queries), allowed, scale)
        rounded = weights.astype(bf16)
        attended = dot_tn(rounded, values).astype(bf16)
        att_ref[rows, cols] = jnp.concatenate(
            [attended[hh * LEN : (hh + 1) * LEN, :] for hh in range(SHARED)], axis=1
        )
        grad_values = dot_nn(rounded, grads)
        grad_dot = dot_nt(values, grads)
        delta = jnp.sum(weights * grad_dot, axis=0, keepdims=True)
        grad_scores = (weights * (grad_dot - delta) * scale).astype(bf16)
        gained = dot_nn(grad_scores, queries) * kg_ref[...]
        mean = jnp.mean(keys * gained, axis=-1, keepdims=True)
        grad_keys = inv * (gained - keys * inv * inv * mean)
        result = jnp.concatenate([grad_keys, grad_values], axis=1).astype(bf16)
        gkv[pl.ds(s * CAP, CAP), :, pl.ds(at, 2 * HEAD)] = result.reshape(CAP, BLK, 2 * HEAD)

    def attend(h):
        if h * PER % GROUP == 0:
            for a in range(2):
                wait_all(got2[h * PER // GROUP], f_recv.at[1, a, h * PER // GROUP])

        def body(step, carry):
            gi, s = step // (CAP // 2), lax.rem(step, CAP // 2) * 2
            one(h, gi, s)
            one(h, gi, s + 1)
            return carry

        lax.fori_loop(0, PER * CAP // 2, body, 0)

        def pack(cb, carry):
            block = gkv[tab_ref[5, cb] & 15]
            out3[h][pl.ds(2 * cb, 2)] = block.reshape(2, BLK // 2, WIDE)
            return carry

        lax.fori_loop(0, 2 * PAIRS, pack, 0)
        exchange(out3[h], got3[h], q, send_sem.at[0, h], recv_sem.at[0, h])
        cols = slice(h * PER * SHARED * HEAD, (h + 1) * PER * SHARED * HEAD)
        pltpu.make_async_copy(att_ref.at[:, cols], att_hbm.at[:, cols], att_sem.at[h]).start()

    for a in range(2):
        for b in range(GROUPS):
            relay(a, b)
    for h in range(PIECES):
        attend(h)
        if h > 0:
            give_back(h - 1)
    give_back(PIECES - 1)
    for h in range(PIECES):
        wait_all(back_hbm.at[h], recv_sem.at[1, h])

    tab_out.wait()
    for h in range(PIECES):
        cols = slice(h * PER * SHARED * HEAD, (h + 1) * PER * SHARED * HEAD)
        pltpu.make_async_copy(att_ref.at[:, cols], att_hbm.at[:, cols], att_sem.at[h]).wait()
        pltpu.make_async_copy(out4[h].at[q], back_hbm.at[h, q], own_back.at[h]).wait()
        for phase in range(2):
            wait_all(got3[h], send_sem.at[phase, h])
    for a in range(2):
        for b in range(GROUPS):
            for phase in range(2):
                wait_all(got1[a][b], f_send.at[phase, a, b])
    wait_all(every, dest_sem.at[0])
    for which in range(2):
        done(weight.at[side(m), e, own_rows], own_sem.at[0, which])
    done(kv_there, kv_sem.at[0])
    done(out_parts.at[m, e], oo_sem.at[0])
    for k in range(ARRIVALS):
        for which in range(2):
            done(weight.at[mine, e, own_rows], z_send.at[k, which])
        done(out_parts.at[m, e, pos], o_send.at[k])
        done(out_parts.at[m, e], mo_send.at[k])
        for way in range(3):
            done(out_parts.at[m, e, pos], ro_send.at[k, way])
        for way in range(4):
            done(piece(k, pos) if way < 2 else part(k, pos, 0), r_send.at[k, way])
        done(weight.at[side(m), e], m_send.at[k])


def place_kernel(tab_ref, att_hbm, back_hbm, att_out, kvg_out, att, back, kvg, sems):
    parts = 4
    rows = att.shape[0] // parts
    att_in, back_in, att_back, kvg_back = [], [], [], []
    for t in range(parts):
        view = pl.ds(t * rows, rows)
        att_in.append(pltpu.make_async_copy(att_hbm.at[view], att.at[view], sems.at[0, t]))
        att_back.append(pltpu.make_async_copy(att.at[view], att_out.at[view], sems.at[1, t]))
    for h in range(PIECES):
        back_in.append(pltpu.make_async_copy(back_hbm.at[h], back.at[h], sems.at[2, h]))
    for j in range(PAIRS):
        view = pl.ds(2 * j, 2)
        kvg_back.append(pltpu.make_async_copy(kvg.at[view], kvg_out.at[view], sems.at[3, j]))
    for copy in back_in + att_in:
        copy.start()
    for copy in back_in:
        copy.wait()
    half = KVHEADS * HEAD
    for j in range(PAIRS):
        color = tab_ref[1, j] & 3
        for g in range(KVHEADS):
            at = g % PER * 2 * HEAD
            block = back[g // PER, pl.ds(4 * color, 4), :, at : at + 2 * HEAD]
            block = block.reshape(2, BLK, 2 * HEAD)
            kvg[2 * j : 2 * j + 2, :, g * HEAD : (g + 1) * HEAD] = block[:, :, :HEAD]
            kvg[2 * j : 2 * j + 2, :, half + g * HEAD : half + (g + 1) * HEAD] = block[:, :, HEAD:]
        kvg_back[j].start()
    for coming, going in zip(att_in, att_back):
        coming.wait()
        going.start()
    for copy in kvg_back + att_back:
        copy.wait()


VMEM = pl.BlockSpec(memory_space=pltpu.VMEM)
SMEM = pl.BlockSpec(memory_space=pltpu.SMEM)
HBM = pl.BlockSpec(memory_space=pltpu.HBM)
LIMIT = 62 * 1024 * 1024


def local(
    images,
    vit_gain,
    vit_qkv,
    vit_out,
    kv_weight,
    queries,
    q_gain,
    k_gain,
    out_grad,
    block_image,
    block_dest,
    key_image,
    text_seen,
):
    enc_blocks, block_len, vis = images.shape
    tokens = enc_blocks * block_len
    buffers = [pltpu.VMEM((PEERS, BLK // 2, WIDE), bf16)] * PIECES
    chunks = [[pltpu.VMEM((PEERS, BLK // 4, GWIDE), bf16)] * GROUPS] * 2
    dma = pltpu.SemaphoreType.DMA
    attended, back, tables = pl.pallas_call(
        kernel,
        out_shape=(
            jax.ShapeDtypeStruct(queries.shape, bf16),
            jax.ShapeDtypeStruct((PIECES, PEERS, BLK // 2, WIDE), bf16),
            jax.ShapeDtypeStruct((8, 128), jnp.int32),
        ),
        in_specs=[SMEM] * 3 + [VMEM] * 4 + [HBM] * 6,
        out_specs=(HBM, HBM, HBM),
        scratch_shapes=[
            pltpu.VMEM((PAIRS, 2 * BLK, vis), bf16),
            pltpu.VMEM(vit_out.shape, bf16),
            pltpu.VMEM(vit_qkv.shape, bf16),
            pltpu.VMEM(queries.shape, bf16),
            pltpu.VMEM(queries.shape, bf16),
            pltpu.VMEM(queries.shape, bf16),
            pltpu.VMEM((8, 128), jnp.int32),
            pltpu.VMEM((PEERS, 8, 128), jnp.int32),
            pltpu.VMEM((8, 128), jnp.int32),
            pltpu.SMEM((8, 128), jnp.int32),
            pltpu.VMEM((8, SHARED * LEN), jnp.int32),
            pltpu.VMEM((8, PLANES, ROWS, PIECE), bf16),
            pltpu.VMEM((2, PLANES, 4, 48, WINDOW), bf16),
            pltpu.VMEM((VHEADS * VHEAD, vis), bf16),
            pltpu.VMEM((vis, 2 * KVHEADS * HEAD), bf16),
            pltpu.VMEM((PLANES, tokens, ROWS), bf16),
            pltpu.VMEM((tokens, 3 * VHEADS * VHEAD), f32),
            pltpu.VMEM((PAIRS, 2 * BLK, 3 * VHEADS * VHEAD), bf16),
            pltpu.VMEM((PAIRS, 2 * BLK, VHEADS * VHEAD), bf16),
            pltpu.VMEM((2, 4 * BLK, vis), bf16),
            chunks,
            pltpu.VMEM((KVHEADS, CAP, SHARED * LEN, HEAD), bf16),
            pltpu.VMEM((CAP * CAP, BLK, WIDE), bf16),
            chunks,
            chunks,
            [pltpu.VMEM((2 * PEERS, BLK // 4, GWIDE), bf16)] * GROUPS,
            buffers,
            buffers,
            buffers,
            dma((8,)),
            dma((2,)),
            dma((2, 2)),
            dma((2,)),
        ]
        + [dma((ARRIVALS, 2))] * 2
        + [dma((ARRIVALS,))] * 2
        + [dma((ARRIVALS, 4))] * 2
        + [dma((ARRIVALS,))] * 2
        + [dma((ARRIVALS, 3))] * 2
        + [dma((ARRIVALS,))] * 2
        + [dma((2,)), dma((PIECES,)), dma((PIECES,))]
        + [dma((2, 2, GROUPS))] * 2
        + [dma((2, PIECES))] * 2,
        compiler_params=pltpu.CompilerParams(
            collective_id=0, has_side_effects=True, vmem_limit_bytes=LIMIT
        ),
    )(
        block_image,
        block_dest,
        key_image,
        text_seen.reshape(1, -1),
        vit_gain.reshape(-1, 128),
        q_gain.reshape(1, HEAD),
        k_gain.reshape(1, HEAD),
        images.reshape(PAIRS, 2 * BLK, vis),
        vit_qkv,
        vit_out,
        kv_weight,
        queries,
        out_grad,
    )
    attended, kv_grad = pl.pallas_call(
        place_kernel,
        out_shape=(
            jax.ShapeDtypeStruct(queries.shape, bf16),
            jax.ShapeDtypeStruct((enc_blocks, block_len, 2 * KVHEADS * HEAD), bf16),
        ),
        in_specs=[SMEM, HBM, HBM],
        out_specs=(HBM, HBM),
        scratch_shapes=[
            pltpu.VMEM(queries.shape, bf16),
            pltpu.VMEM((PIECES, PEERS, BLK // 2, WIDE), bf16),
            pltpu.VMEM((enc_blocks, block_len, 2 * KVHEADS * HEAD), bf16),
            dma((4, 4)),
        ],
        compiler_params=pltpu.CompilerParams(vmem_limit_bytes=LIMIT),
    )(tables, attended, back)
    return attended, kv_grad


def solution(mesh):
    everywhere = ("enc", "seq", "mp")
    placed = (
        P(everywhere, None, None),
        P(),
        P(("enc", "mp"), None),
        P(("enc", "mp"), None),
        P("mp", None),
        P(everywhere, None),
        P(),
        P(),
        P(everywhere, None),
        P(everywhere),
        P(everywhere),
        P(everywhere, None),
        P(everywhere),
    )
    return jax.shard_map(
        local,
        mesh=mesh,
        in_specs=placed,
        out_specs=(P(everywhere, None), P(everywhere, None, None)),
        check_vma=False,
    )
```

```python
import math

import jax
import jax.numpy as jnp
from jax import lax
from jax.experimental import pallas as pl
from jax.experimental.pallas import tpu as pltpu
from jax.sharding import PartitionSpec as P

VHEADS = 8
VHEAD = 80
HEAD = 128
KVHEADS = 4
SHARED = 8
BLK = 64
LEN = 32
CAP = 4
PEERS = 16
PAIRS = 4
PIECES = 2
PER = KVHEADS // PIECES
WIDE = PER * 2 * HEAD
GROUPS = 2
GROUP = KVHEADS // GROUPS
GWIDE = GROUP * 2 * HEAD
EPS = 1e-05
MESH = pl.DeviceIdType.MESH
f32 = jnp.float32
bf16 = jnp.bfloat16


def dot_nn(left, right):
    return jnp.dot(left, right, preferred_element_type=f32)


def dot_nt(left, right):
    return lax.dot_general(left, right, (((1,), (1,)), ((), ())), preferred_element_type=f32)


def dot_tn(left, right):
    return lax.dot_general(left, right, (((0,), (0,)), ((), ())), preferred_element_type=f32)


def exchange(source, target, me, send_sem, recv_sem, own_sem=None):
    def body(step, carry):
        peer = lax.rem(me + step, PEERS)
        pltpu.make_async_remote_copy(
            src_ref=source.at[peer],
            dst_ref=target.at[me],
            send_sem=send_sem,
            recv_sem=recv_sem,
            device_id={"seq": peer},
            device_id_type=MESH,
        ).start()
        return carry

    lax.fori_loop(1, PEERS, body, 0)
    if own_sem is None:
        target[me] = source[me]
    else:
        pltpu.make_async_copy(source.at[me], target.at[me], own_sem).start()


def wait_all(buffer, sem):
    view = buffer.at[pl.ds(0, PEERS - 1)]
    pltpu.make_async_copy(view, view, sem).wait()


def split_colors(src_partner, dst_partner, doublings):
    n = src_partner.shape[0]
    row = lax.broadcasted_iota(jnp.int32, (n, n), 0)
    col = lax.broadcasted_iota(jnp.int32, (n, n), 1)
    src_b = jnp.where(src_partner, 1.0, 0.0).astype(bf16)
    dst_b = jnp.where(dst_partner, 1.0, 0.0).astype(bf16)
    power = dot_nn(src_b, dst_b).astype(bf16)
    total = jnp.where(row == col, 1.0, 0.0) + power.astype(f32)
    yield
    for _ in range(doublings - 1):
        power = dot_nn(power, power).astype(bf16)
        total = total + dot_nn(total.astype(bf16), power)
        yield
    orbit = total > 0.5
    lead_c = jnp.min(jnp.where(orbit, col, n), axis=1, keepdims=True)
    lead_r = jnp.min(jnp.where(orbit, row, n), axis=0, keepdims=True)
    other_c = jnp.sum(jnp.where(src_partner, lead_r, 0), axis=1, keepdims=True)
    other_r = jnp.sum(jnp.where(src_partner, lead_c, 0), axis=0, keepdims=True)
    return (lead_c < other_c).astype(jnp.int32), (lead_r < other_r).astype(jnp.int32)


def color_tables(dest, me):
    n = dest.shape[0]
    row = lax.broadcasted_iota(jnp.int32, (n, n), 0)
    col = lax.broadcasted_iota(jnp.int32, (n, n), 1)
    dest_t = jnp.transpose(dest.astype(f32)).astype(jnp.int32)
    owner_c, owner_r = dest >> 4, dest_t >> 4
    parity_same = (row & 1) == (col & 1)
    src_same = ((row >> 3) == (col >> 3)) & parity_same
    dst_same = (owner_c == owner_r) & parity_same
    rank_c = jnp.sum(jnp.where(dst_same & (col < row), 1, 0), axis=1, keepdims=True)
    rank_r = jnp.sum(jnp.where(dst_same & (row < col), 1, 0), axis=0, keepdims=True)
    src_partner = col == (row ^ 2)
    dst_partner = dst_same & (rank_r == (rank_c ^ 1))
    yield
    one_c, one_r = yield from split_colors(src_partner, dst_partner, 5)
    yield
    alike = (one_c == one_r) & (row != col)
    two_c, _ = yield from split_colors(src_same & alike, dst_same & alike, 4)
    yield
    color = jnp.broadcast_to(2 * one_c + two_c, (n, n))
    src = row >> 3
    pair = (row & 7) >> 1
    half = row & 1
    even = half == 0
    mine = src == me
    turn, turn2 = me // 4, me // 8

    def pick(mask, value):
        return jnp.sum(jnp.where(mask, value, 0), axis=0, keepdims=True)

    rows = [
        pick(mine & even & (color == col), pair),
        pick(mine & even & (pair == col), color),
        pick(even & (color == turn2) & (owner_c == col), src),
        pick(even & (color == turn) & (src == col), owner_c),
        pick((owner_c == me) & ((dest & 15) == col), 2 * color + half + 1) - 1,
        pick((owner_c == me) & (2 * color + half == col), dest & 15),
        pick(even & (color == 2 + turn2) & (owner_c == col), src),
    ]
    rows += [jnp.zeros_like(rows[0])]
    return jnp.concatenate(rows, axis=0)


PLANES = 8
ROWS = 160
PIECE = 256
ARRIVALS = PLANES - 1
WINDOW = 384
LOG2E = 1.4426950408889634


def softmax_over_rows(scores, allowed, scale):
    masked = jnp.where(allowed, scores, -jnp.inf)
    top = jnp.max(masked, axis=0, keepdims=True)
    terms = jnp.exp2((masked - top) * (scale * LOG2E))
    return terms * (1.0 / jnp.sum(terms, axis=0, keepdims=True))


def kernel(
    image_hbm,
    dest_hbm,
    kimg_hbm,
    seen_hbm,
    gain_hbm,
    qg_hbm,
    kg_hbm,
    x_hbm,
    qkv_hbm,
    out_hbm,
    kv_hbm,
    q_hbm,
    og_hbm,
    att_hbm,
    back_hbm,
    tab_hbm,
    image_ref,
    dest_ref,
    kimg_ref,
    seen_ref,
    gain_ref,
    qg_ref,
    kg_ref,
    x_ref,
    own_out,
    own_qkv,
    q_ref,
    og_ref,
    att_ref,
    dest_tile,
    every,
    tab_tile,
    tab_ref,
    seen_rows,
    weight,
    out_parts,
    out_ref,
    kv_ref,
    normed,
    summed,
    mixed,
    att,
    hidden,
    pay,
    qn,
    gkv,
    got1,
    out2,
    got2,
    out3,
    got3,
    out4,
    local_sem,
    dest_sem,
    own_sem,
    kv_sem,
    z_send,
    z_recv,
    o_send,
    o_recv,
    r_send,
    r_recv,
    m_send,
    m_recv,
    ro_send,
    ro_recv,
    mo_send,
    mo_recv,
    oo_sem,
    att_sem,
    own_back,
    f_send,
    f_recv,
    send_sem,
    recv_sem,
):
    pairs_here, span, vis = x_ref.shape
    tokens = pairs_here * span
    e, q, m = lax.axis_index("enc"), lax.axis_index("seq"), lax.axis_index("mp")
    other = 1 - m
    d = 1 - 2 * m
    stride = 1 + 3 * m
    pos = lax.rem(q // stride, 4)
    ring = q - pos * stride
    left, right, far = lax.rem(pos + 3, 4), lax.rem(pos + 1, 4), lax.rem(pos + 2, 4)
    ahead, behind = lax.rem(e + d + PLANES, PLANES), lax.rem(e - d + PLANES, PLANES)
    to_left, to_right = {"seq": ring + left * stride}, {"seq": ring + right * stride}
    to_ahead, to_behind, to_mate = {"enc": ahead}, {"enc": behind}, {"mp": other}

    def remote(source, target, send, recv, device):
        pltpu.make_async_remote_copy(
            src_ref=source,
            dst_ref=target,
            send_sem=send,
            recv_sem=recv,
            device_id=device,
            device_id_type=MESH,
        ).start()

    def done(view, sem):
        pltpu.make_async_copy(view, view, sem).wait()

    half_rows = ROWS // 2
    own_rows = pl.ds(pl.multiple_of(m * half_rows, half_rows), half_rows)
    mate_rows = pl.ds(pl.multiple_of(other * half_rows, half_rows), half_rows)
    kv_half = kv_hbm.shape[0]
    kv_rows = pl.ds(pl.multiple_of(m * kv_half, kv_half), kv_half)
    copies = [
        pltpu.make_async_copy(source, target, local_sem.at[index])
        for index, (source, target) in enumerate(
            (
                (qkv_hbm, own_qkv),
                (x_hbm, x_ref),
                (out_hbm, own_out),
                (kv_hbm, kv_ref.at[kv_rows]),
                (q_hbm, q_ref),
                (og_hbm, og_ref),
                (tab_tile, tab_ref),
                (tab_tile, tab_hbm),
                (dest_hbm, dest_ref),
                (seen_hbm, seen_ref),
                (gain_hbm, gain_ref),
                (image_hbm, image_ref),
                (kimg_hbm, kimg_ref),
                (qg_hbm, qg_ref),
                (kg_hbm, kg_ref),
            )
        )
    ]
    qkv_copy, x_copy, out_copy, kv_copy, q_copy, og_copy, tab_copy, tab_out = copies[:8]
    dest_copy, seen_copy, gain_copy = copies[8:11]
    late = copies[11:]
    for copy in [qkv_copy] + copies[8:] + copies[1:6]:
        copy.start()

    barrier = pltpu.get_barrier_semaphore()

    def hello(step, carry):
        pl.semaphore_signal(
            barrier, inc=1, device_id={"seq": lax.rem(q + step, PEERS)}, device_id_type=MESH
        )
        return carry

    lax.fori_loop(1, PEERS, hello, 0)
    for device in (to_ahead, to_behind, to_mate):
        pl.semaphore_signal(barrier, inc=1, device_id=device, device_id_type=MESH)

    sub = lax.broadcasted_iota(jnp.int32, (8, 128), 0)
    lane = lax.broadcasted_iota(jnp.int32, (8, 128), 1)
    tile = jnp.zeros((8, 128), jnp.int32)
    for copy in (dest_copy, seen_copy, gain_copy):
        copy.wait()
    for block in range(8):
        tile = jnp.where(sub == block, dest_ref[block], tile)
    dest_tile[...] = tile
    every[q] = tile
    spread = jnp.where(lane // LEN == sub, seen_ref[...].astype(f32), 0.0).astype(bf16)
    wide = (128, SHARED * LEN)
    place = lax.rem(lax.broadcasted_iota(jnp.int32, wide, 0), LEN) == lax.rem(
        lax.broadcasted_iota(jnp.int32, wide, 1), LEN
    )
    seen_rows[...] = dot_nn(spread, jnp.where(place, 1.0, 0.0).astype(bf16)).astype(jnp.int32)
    gain = jnp.concatenate([gain_ref[t : t + 1, :] for t in range(vis // 128)], axis=1)
    out_copy.wait()
    have = own_out.shape[0]
    for place in range(4):
        at = min(place * WINDOW, vis - WINDOW)
        out_parts[m, e, place, 0:have, :] = own_out[:, at : at + WINDOW]
    qkv_copy.wait()
    for p in range(8):
        count = min(PIECE, own_qkv.shape[1] - p * PIECE)
        weight[p, e, own_rows, 0:count] = own_qkv[:, p * PIECE : p * PIECE + count]
    pl.semaphore_wait(barrier, PEERS + 2)

    mine = 4 * m + pos

    def side(core):
        return pl.ds(4 * core, 4)

    for which, core in ((0, other), (1, m)):
        view = weight.at[side(core), e, own_rows]
        remote(view, view, own_sem.at[0, which], own_sem.at[1, which], to_mate)

    def send_z(plane, which, arrival):
        view = weight.at[mine, plane, mate_rows if which else own_rows]
        device = to_behind if arrival % 2 else to_ahead
        remote(view, view, z_send.at[arrival, which], z_recv.at[arrival, which], device)

    send_z(e, 0, 0)
    send_z(e, 0, 1)
    view = out_parts.at[m, e]
    remote(view, view, oo_sem.at[0], oo_sem.at[1], to_mate)

    def send_dest(step, carry):
        peer = lax.rem(q + step, PEERS)
        remote(dest_tile, every.at[q], dest_sem.at[0], dest_sem.at[1], {"seq": peer})
        return carry

    lax.fori_loop(1, PEERS, send_dest, 0)
    done(weight.at[side(m), e, mate_rows], own_sem.at[1, 0])
    send_z(e, 1, 0)
    send_z(e, 1, 1)
    kv_there = kv_ref.at[kv_rows]

    def send_out(plane, arrival):
        view = out_parts.at[m, plane, pos]
        device = to_behind if arrival % 2 else to_ahead
        remote(view, view, o_send.at[arrival], o_recv.at[arrival], device)

    def plane_of(arrival):
        hops = arrival // 2 + 1
        if arrival % 2 == 0:
            return lax.rem(e - d * hops + PLANES, PLANES)
        return lax.rem(e + d * hops + PLANES, PLANES)

    def piece(k, place):
        return weight.at[4 * m + place, plane_of(k)]

    def part(k, place, which):
        return weight.at[4 * m + place, plane_of(k), pl.ds(which * half_rows, half_rows)]

    width = VHEADS * VHEAD

    def norm_jobs():
        x_copy.wait()
        for t in range(tokens // 64):
            rows = slice(t * 64, t * 64 + 64)
            values = x_ref[t // 2, t % 2 * 64 : t % 2 * 64 + 64, :].astype(f32)
            center = values - jnp.mean(values, axis=-1, keepdims=True)
            spread = jnp.mean(center * center, axis=-1, keepdims=True)
            result = (center * lax.rsqrt(spread + EPS) * gain).astype(bf16)
            for plane in range(PLANES):
                normed[plane, rows, :] = result[:, plane * ROWS : (plane + 1) * ROWS]
            yield

    def table_jobs():
        wait_all(every, dest_sem.at[1])
        tab_tile[...] = yield from color_tables(every[...].reshape(PEERS * 8, 128), q)
        tab_copy.start()
        tab_out.start()

    def add_plane(plane, mode, p):
        count = min(PIECE, 3 * width - p * PIECE)
        cols = slice(p * PIECE, p * PIECE + count)
        found = dot_nn(normed[plane], weight[p, plane, :, 0:count])
        if mode == 0:
            summed[:, cols] = found
        elif mode == 1:
            summed[:, cols] += found
        else:
            total = (summed[:, cols] + found).astype(bf16)
            mixed[:, :, cols] = total.reshape(PAIRS, span, count)

    def plane_jobs(k):
        if k < 0:
            done(weight.at[side(other), e, mate_rows], own_sem.at[1, 1])
            plane = e
        else:
            same = k ^ 1 if k < ARRIVALS - 1 else k
            done(weight.at[side(m), e], m_recv.at[same])
            plane = plane_of(k)
        mode = 0 if k < 0 else 1 if k < ARRIVALS - 1 else 2
        for p in range(8):
            add_plane(plane, mode, p)
            if p % 3 == 2:
                yield
        yield

    def query_jobs():
        q_copy.wait()
        for copy in late:
            copy.wait()
        for g in range(KVHEADS):
            block = q_ref[:, g * SHARED * HEAD : (g + 1) * SHARED * HEAD]
            for hh in range(SHARED):
                x = block[:, hh * HEAD : (hh + 1) * HEAD].astype(f32)
                inv = lax.rsqrt(jnp.mean(x * x, axis=-1, keepdims=True) + EPS)
                y = (x * inv * qg_ref[...]).astype(bf16)
                for s in range(CAP):
                    qn[g, s, hh * LEN : (hh + 1) * LEN, :] = y[s * LEN : (s + 1) * LEN, :]
            yield

    def out_jobs(k):
        if k < 0:
            plane = e
            done(out_parts.at[m, e], oo_sem.at[1])
        else:
            plane = plane_of(k)
            done(out_parts.at[m, e], mo_recv.at[k ^ 1 if k < ARRIVALS - 1 else k])
        both = []
        for core in range(2):
            parts = [out_parts[core, plane, place, 0:have, :] for place in range(4)]
            parts[3] = parts[3][:, 4 * WINDOW - vis :]
            both.append(jnp.concatenate(parts, axis=1).astype(f32))
        rows = pl.ds(pl.multiple_of(2 * have * plane, 2 * have), 2 * have)
        out_ref[rows, :] = jnp.concatenate(both, axis=0).astype(bf16)
        yield

    queue = [norm_jobs(), table_jobs(), plane_jobs(-1), query_jobs()]

    def pump(steps):
        while queue and steps > 0:
            try:
                next(queue[0])
                steps -= 1
            except StopIteration:
                queue.pop(0)

    send_out(e, 0)
    send_out(e, 1)
    remote(kv_hbm, kv_there, kv_sem.at[0], kv_sem.at[1], to_mate)
    pump(2)
    hops = ((0, 1), (2, 3), (4, 5), (6,))
    for t in range(len(hops) + 2):
        if t < len(hops):
            for which in range(2):
                for k in hops[t]:
                    rows = mate_rows if which else own_rows
                    done(weight.at[mine, plane_of(k), rows], z_recv.at[k, which])
                    if k + 2 < ARRIVALS:
                        send_z(plane_of(k), which, k + 2)
            for k in hops[t]:
                view = piece(k, pos)
                remote(view, view, r_send.at[k, 0], r_recv.at[k, 0], to_right)
                remote(view, view, r_send.at[k, 1], r_recv.at[k, 1], to_left)
            for k in hops[t]:
                view = out_parts.at[m, plane_of(k), pos]
                done(view, o_recv.at[k])
                if k + 2 < ARRIVALS:
                    send_out(plane_of(k), k + 2)
                remote(view, view, ro_send.at[k, 0], ro_recv.at[k, 0], to_right)
                remote(view, view, ro_send.at[k, 1], ro_recv.at[k, 1], to_left)
        pump(2)
        if 0 <= t - 1 < len(hops):
            for k in hops[t - 1]:
                view = part(k, left, 0)
                done(piece(k, left), r_recv.at[k, 0])
                remote(view, view, r_send.at[k, 2], r_recv.at[k, 2], to_right)
                view = part(k, right, 1)
                done(piece(k, right), r_recv.at[k, 1])
                remote(view, view, r_send.at[k, 3], r_recv.at[k, 3], to_left)
            for k in hops[t - 1]:
                from_left = out_parts.at[m, plane_of(k), left]
                from_right = out_parts.at[m, plane_of(k), right]
                done(from_left, ro_recv.at[k, 0])
                done(from_right, ro_recv.at[k, 1])
                if k % 2 == 0:
                    remote(from_left, from_left, ro_send.at[k, 2], ro_recv.at[k, 2], to_right)
                else:
                    remote(from_right, from_right, ro_send.at[k, 2], ro_recv.at[k, 2], to_left)
        pump(2)
        if 0 <= t - 2 < len(hops):
            for k in hops[t - 2]:
                done(part(k, far, 0), r_recv.at[k, 2])
                done(part(k, far, 1), r_recv.at[k, 3])
                view = weight.at[side(m), plane_of(k)]
                remote(view, view, m_send.at[k], m_recv.at[k], to_mate)
            for k in hops[t - 2]:
                done(out_parts.at[m, plane_of(k), far], ro_recv.at[k, 2])
                view = out_parts.at[m, plane_of(k)]
                remote(view, view, mo_send.at[k], mo_recv.at[k], to_mate)
        pump(2)
        if t == 1:
            queue.append(out_jobs(-1))
        if 0 <= t - 2 < len(hops):
            queue.extend(plane_jobs(k) for k in hops[t - 2])
        if 0 <= t - 3 < len(hops):
            queue.extend(out_jobs(k) for k in hops[t - 3])
    pump(1000)
    queue.append(out_jobs(ARRIVALS - 1))

    row = lax.broadcasted_iota(jnp.int32, (span, span), 0)
    col = lax.broadcasted_iota(jnp.int32, (span, span), 1)
    near = (row // BLK) == (col // BLK)

    def window(head):
        first, last = head * VHEAD // 128, ((head + 1) * VHEAD - 1) // 128
        return first, last, first * 128, (last - first + 1) * 128

    def attend_pair(c):
        pair = tab_ref[0, c] & 3
        allowed = near | (image_ref[2 * pair] == image_ref[2 * pair + 1])
        insides, scores = [], []
        for head in range(VHEADS):
            _, _, base, cut = window(head)
            lanes = lax.broadcasted_iota(jnp.int32, (span, cut), 1) + base
            inside = (lanes >= head * VHEAD) & (lanes < (head + 1) * VHEAD)
            query = jnp.where(inside, mixed[pair, :, base : base + cut], jnp.zeros((), bf16))
            key = mixed[pair, :, width + base : width + base + cut]
            insides.append(inside)
            scores.append(dot_nt(key, query))
        weights = [
            softmax_over_rows(found, allowed, 1.0 / math.sqrt(VHEAD)).astype(bf16)
            for found in scores
        ]
        tiles = [None] * (width // 128)
        for head in range(VHEADS):
            first, last, base, cut = window(head)
            value = mixed[pair, :, 2 * width + base : 2 * width + base + cut]
            result = dot_tn(weights[head], value)
            for t in range(first, last + 1):
                at = (t - first) * 128
                found = result[:, at : at + 128]
                if tiles[t] is not None:
                    found = jnp.where(insides[head][:, at : at + 128], found, tiles[t])
                tiles[t] = found
        att[c] = jnp.concatenate(tiles, axis=1).astype(bf16)

    half = KVHEADS * HEAD
    tab_copy.wait()
    for a in range(2):
        pairs = (2 * a, 2 * a + 1)

        def attend_pairs(c, carry):
            attend_pair(c)
            return carry

        lax.fori_loop(pairs[0], pairs[1] + 1, attend_pairs, 0)
        if a == 0:
            pump(1000)
        attended = jnp.concatenate([att[c] for c in pairs], axis=0)

        def project(t, carry):
            cols = pl.ds(pl.multiple_of(t * 256, 256), 256)
            tokens_in = jnp.concatenate(
                [x_ref[tab_ref[0, c] & 3, :, cols] for c in pairs], axis=0
            )
            total = tokens_in.astype(f32) + dot_nn(attended, out_ref[:, cols])
            hidden[a, :, cols] = total.astype(bf16)
            return carry

        lax.fori_loop(0, vis // 256, project, 0)
        if a == 0:
            kv_copy.wait()
            done(kv_there, kv_sem.at[1])
        for b in range(GROUPS):
            for t in range(GROUP):
                at = (b * GROUP + t) * HEAD
                both = jnp.concatenate(
                    [kv_ref[:, at : at + HEAD], kv_ref[:, half + at : half + at + HEAD]], axis=1
                )
                pay[a][b][:, :, t * 2 * HEAD : (t + 1) * 2 * HEAD] = (
                    dot_nn(hidden[a], both).astype(bf16).reshape(PEERS, BLK // 4, 2 * HEAD)
                )
            exchange(pay[a][b], got1[a][b], q, f_send.at[0, a, b], f_recv.at[0, a, b])

    og_copy.wait()

    def shuffle(got, out, table):
        def body(index, carry):
            out[index] = got[tab_ref[table, index] & 15]
            return carry

        lax.fori_loop(0, PEERS, body, 0)

    def relay(a, b):
        wait_all(got1[a][b], f_recv.at[0, a, b])
        shuffle(got1[a][b], out2[a][b], 6 if a else 2)
        exchange(out2[a][b], got2[b].at[pl.ds(a * PEERS, PEERS)], q, f_send.at[1, a, b], f_recv.at[1, a, b])

    def give_back(h):
        wait_all(got3[h], recv_sem.at[0, h])
        shuffle(got3[h], out4[h], 3)
        exchange(out4[h], back_hbm.at[h], q, send_sem.at[1, h], recv_sem.at[1, h], own_back.at[h])

    def one(h, gi, s):
        g = h * PER + gi
        at = pl.multiple_of(gi * 2 * HEAD, 2 * HEAD)
        group = h * PER // GROUP
        from_col = pl.multiple_of((h * PER % GROUP + gi) * 2 * HEAD, 2 * HEAD)
        yield
        blocks, masks = [], []
        seen = seen_rows[pl.ds(s, 1), :]
        for kb in range(CAP):
            index = tab_ref[4, s * CAP + kb]
            start = 4 * (jnp.maximum(index, 0) & 7)
            block = got2[group][pl.ds(start, 4), :, pl.ds(from_col, 2 * HEAD)]
            blocks.append(
                jnp.where(index >= 0, block, jnp.zeros((), bf16)).reshape(BLK, 2 * HEAD)
            )
            masks.append(jnp.broadcast_to(kimg_ref[s, kb] < seen, (BLK, SHARED * LEN)))
        keyval = jnp.concatenate(blocks, axis=0)
        allowed = jnp.concatenate(masks, axis=0)
        keys = keyval[:, :HEAD].astype(f32)
        values = keyval[:, HEAD:]
        inv = lax.rsqrt(jnp.mean(keys * keys, axis=-1, keepdims=True) + EPS)
        kn = (keys * inv * kg_ref[...]).astype(bf16)
        yield
        queries = qn[g, s]
        rows = pl.ds(pl.multiple_of(s * LEN, LEN), LEN)
        cols = pl.ds(pl.multiple_of(g * SHARED * HEAD, SHARED * HEAD), SHARED * HEAD)
        grad_row = og_ref[rows, cols]
        grads = jnp.concatenate(
            [grad_row[:, hh * HEAD : (hh + 1) * HEAD] for hh in range(SHARED)], axis=0
        )
        scale = 1.0 / math.sqrt(HEAD)
        scores = dot_nt(kn, queries)
        grad_dot = dot_nt(values, grads)
        yield
        weights = softmax_over_rows(scores, allowed, scale)
        rounded = weights.astype(bf16)
        yield
        attended = dot_tn(rounded, values).astype(bf16)
        att_ref[rows, cols] = jnp.concatenate(
            [attended[hh * LEN : (hh + 1) * LEN, :] for hh in range(SHARED)], axis=1
        )
        grad_values = dot_nn(rounded, grads)
        yield
        delta = jnp.sum(weights * grad_dot, axis=0, keepdims=True)
        grad_scores = (weights * (grad_dot - delta) * scale).astype(bf16)
        yield
        gained = dot_nn(grad_scores, queries) * kg_ref[...]
        yield
        mean = jnp.mean(keys * gained, axis=-1, keepdims=True)
        grad_keys = inv * (gained - keys * inv * inv * mean)
        result = jnp.concatenate([grad_keys, grad_values], axis=1).astype(bf16)
        gkv[pl.ds(s * CAP, CAP), :, pl.ds(at, 2 * HEAD)] = result.reshape(CAP, BLK, 2 * HEAD)

    def attend(h):
        if h * PER % GROUP == 0:
            for a in range(2):
                wait_all(got2[h * PER // GROUP], f_recv.at[1, a, h * PER // GROUP])

        def body(step, carry):
            gi, s = step // (CAP // 2), lax.rem(step, CAP // 2) * 2
            both = [one(h, gi, s), one(h, gi, s + 1)]
            while both:
                both = [steps for steps in both if next(steps, both) is not both]
            return carry

        lax.fori_loop(0, PER * CAP // 2, body, 0)

        def pack(cb, carry):
            block = gkv[tab_ref[5, cb] & 15]
            out3[h][pl.ds(2 * cb, 2)] = block.reshape(2, BLK // 2, WIDE)
            return carry

        lax.fori_loop(0, 2 * PAIRS, pack, 0)
        exchange(out3[h], got3[h], q, send_sem.at[0, h], recv_sem.at[0, h])
        cols = slice(h * PER * SHARED * HEAD, (h + 1) * PER * SHARED * HEAD)
        pltpu.make_async_copy(att_ref.at[:, cols], att_hbm.at[:, cols], att_sem.at[h]).start()

    for a in range(2):
        for b in range(GROUPS):
            relay(a, b)
    for h in range(PIECES):
        attend(h)
        if h > 0:
            give_back(h - 1)
    give_back(PIECES - 1)
    for h in range(PIECES):
        wait_all(back_hbm.at[h], recv_sem.at[1, h])

    tab_out.wait()
    for h in range(PIECES):
        cols = slice(h * PER * SHARED * HEAD, (h + 1) * PER * SHARED * HEAD)
        pltpu.make_async_copy(att_ref.at[:, cols], att_hbm.at[:, cols], att_sem.at[h]).wait()
        pltpu.make_async_copy(out4[h].at[q], back_hbm.at[h, q], own_back.at[h]).wait()
        for phase in range(2):
            wait_all(got3[h], send_sem.at[phase, h])
    for a in range(2):
        for b in range(GROUPS):
            for phase in range(2):
                wait_all(got1[a][b], f_send.at[phase, a, b])
    wait_all(every, dest_sem.at[0])
    for which in range(2):
        done(weight.at[side(m), e, own_rows], own_sem.at[0, which])
    done(kv_there, kv_sem.at[0])
    done(out_parts.at[m, e], oo_sem.at[0])
    for k in range(ARRIVALS):
        for which in range(2):
            done(weight.at[mine, e, own_rows], z_send.at[k, which])
        done(out_parts.at[m, e, pos], o_send.at[k])
        done(out_parts.at[m, e], mo_send.at[k])
        for way in range(3):
            done(out_parts.at[m, e, pos], ro_send.at[k, way])
        for way in range(4):
            done(piece(k, pos) if way < 2 else part(k, pos, 0), r_send.at[k, way])
        done(weight.at[side(m), e], m_send.at[k])


def place_kernel(tab_hbm, att_hbm, back_hbm, att_out, kvg_out, tab_ref, att, back, kvg, sems):
    parts = 4
    rows = att.shape[0] // parts
    att_in, back_in, att_back, kvg_back = [], [], [], []
    for t in range(parts):
        view = pl.ds(t * rows, rows)
        att_in.append(pltpu.make_async_copy(att_hbm.at[view], att.at[view], sems.at[0, t]))
        att_back.append(pltpu.make_async_copy(att.at[view], att_out.at[view], sems.at[1, t]))
    for h in range(PIECES):
        back_in.append(pltpu.make_async_copy(back_hbm.at[h], back.at[h], sems.at[2, h]))
    for j in range(PAIRS):
        view = pl.ds(2 * j, 2)
        kvg_back.append(pltpu.make_async_copy(kvg.at[view], kvg_out.at[view], sems.at[3, j]))
    tab_in = pltpu.make_async_copy(tab_hbm, tab_ref, sems.at[4, 0])
    for copy in [tab_in] + back_in + att_in:
        copy.start()
    for copy in [tab_in] + back_in:
        copy.wait()
    half = KVHEADS * HEAD
    for j in range(PAIRS):
        color = tab_ref[1, j] & 3
        for g in range(KVHEADS):
            at = g % PER * 2 * HEAD
            block = back[g // PER, pl.ds(4 * color, 4), :, at : at + 2 * HEAD]
            block = block.reshape(2, BLK, 2 * HEAD)
            kvg[2 * j : 2 * j + 2, :, g * HEAD : (g + 1) * HEAD] = block[:, :, :HEAD]
            kvg[2 * j : 2 * j + 2, :, half + g * HEAD : half + (g + 1) * HEAD] = block[:, :, HEAD:]
        kvg_back[j].start()
    for coming, going in zip(att_in, att_back):
        coming.wait()
        going.start()
    for copy in kvg_back + att_back:
        copy.wait()


HBM = pl.BlockSpec(memory_space=pltpu.HBM)
LIMIT = 62 * 1024 * 1024


def local(
    images,
    vit_gain,
    vit_qkv,
    vit_out,
    kv_weight,
    queries,
    q_gain,
    k_gain,
    out_grad,
    block_image,
    block_dest,
    key_image,
    text_seen,
):
    enc_blocks, block_len, vis = images.shape
    tokens = enc_blocks * block_len
    buffers = [pltpu.VMEM((PEERS, BLK // 2, WIDE), bf16)] * PIECES
    chunks = [[pltpu.VMEM((PEERS, BLK // 4, GWIDE), bf16)] * GROUPS] * 2
    dma = pltpu.SemaphoreType.DMA
    attended, back, tables = pl.pallas_call(
        kernel,
        out_shape=(
            jax.ShapeDtypeStruct(queries.shape, bf16),
            jax.ShapeDtypeStruct((PIECES, PEERS, BLK // 2, WIDE), bf16),
            jax.ShapeDtypeStruct((8, 128), jnp.int32),
        ),
        in_specs=[HBM] * 13,
        out_specs=(HBM, HBM, HBM),
        scratch_shapes=[
            pltpu.SMEM(block_image.shape, jnp.int32),
            pltpu.SMEM(block_dest.shape, jnp.int32),
            pltpu.SMEM(key_image.shape, jnp.int32),
            pltpu.VMEM((1, CAP * LEN), jnp.int32),
            pltpu.VMEM((vis // 128, 128), f32),
            pltpu.VMEM((1, HEAD), f32),
            pltpu.VMEM((1, HEAD), f32),
            pltpu.VMEM((PAIRS, 2 * BLK, vis), bf16),
            pltpu.VMEM(vit_out.shape, bf16),
            pltpu.VMEM(vit_qkv.shape, bf16),
            pltpu.VMEM(queries.shape, bf16),
            pltpu.VMEM(queries.shape, bf16),
            pltpu.VMEM(queries.shape, bf16),
            pltpu.VMEM((8, 128), jnp.int32),
            pltpu.VMEM((PEERS, 8, 128), jnp.int32),
            pltpu.VMEM((8, 128), jnp.int32),
            pltpu.SMEM((8, 128), jnp.int32),
            pltpu.VMEM((8, SHARED * LEN), jnp.int32),
            pltpu.VMEM((8, PLANES, ROWS, PIECE), bf16),
            pltpu.VMEM((2, PLANES, 4, 48, WINDOW), bf16),
            pltpu.VMEM((VHEADS * VHEAD, vis), bf16),
            pltpu.VMEM((vis, 2 * KVHEADS * HEAD), bf16),
            pltpu.VMEM((PLANES, tokens, ROWS), bf16),
            pltpu.VMEM((tokens, 3 * VHEADS * VHEAD), f32),
            pltpu.VMEM((PAIRS, 2 * BLK, 3 * VHEADS * VHEAD), bf16),
            pltpu.VMEM((PAIRS, 2 * BLK, VHEADS * VHEAD), bf16),
            pltpu.VMEM((2, 4 * BLK, vis), bf16),
            chunks,
            pltpu.VMEM((KVHEADS, CAP, SHARED * LEN, HEAD), bf16),
            pltpu.VMEM((CAP * CAP, BLK, WIDE), bf16),
            chunks,
            chunks,
            [pltpu.VMEM((2 * PEERS, BLK // 4, GWIDE), bf16)] * GROUPS,
            buffers,
            buffers,
            buffers,
            dma((15,)),
            dma((2,)),
            dma((2, 2)),
            dma((2,)),
        ]
        + [dma((ARRIVALS, 2))] * 2
        + [dma((ARRIVALS,))] * 2
        + [dma((ARRIVALS, 4))] * 2
        + [dma((ARRIVALS,))] * 2
        + [dma((ARRIVALS, 3))] * 2
        + [dma((ARRIVALS,))] * 2
        + [dma((2,)), dma((PIECES,)), dma((PIECES,))]
        + [dma((2, 2, GROUPS))] * 2
        + [dma((2, PIECES))] * 2,
        compiler_params=pltpu.CompilerParams(
            collective_id=0, has_side_effects=True, vmem_limit_bytes=LIMIT
        ),
    )(
        block_image,
        block_dest,
        key_image,
        text_seen.reshape(1, -1),
        vit_gain.reshape(-1, 128),
        q_gain.reshape(1, HEAD),
        k_gain.reshape(1, HEAD),
        images.reshape(PAIRS, 2 * BLK, vis),
        vit_qkv,
        vit_out,
        kv_weight,
        queries,
        out_grad,
    )
    attended, kv_grad = pl.pallas_call(
        place_kernel,
        out_shape=(
            jax.ShapeDtypeStruct(queries.shape, bf16),
            jax.ShapeDtypeStruct((enc_blocks, block_len, 2 * KVHEADS * HEAD), bf16),
        ),
        in_specs=[HBM, HBM, HBM],
        out_specs=(HBM, HBM),
        scratch_shapes=[
            pltpu.SMEM((8, 128), jnp.int32),
            pltpu.VMEM(queries.shape, bf16),
            pltpu.VMEM((PIECES, PEERS, BLK // 2, WIDE), bf16),
            pltpu.VMEM((enc_blocks, block_len, 2 * KVHEADS * HEAD), bf16),
            dma((5, 4)),
        ],
        compiler_params=pltpu.CompilerParams(vmem_limit_bytes=LIMIT),
    )(tables, attended, back)
    return attended, kv_grad


def solution(mesh):
    everywhere = ("enc", "seq", "mp")
    placed = (
        P(everywhere, None, None),
        P(),
        P(("enc", "mp"), None),
        P(("enc", "mp"), None),
        P("mp", None),
        P(everywhere, None),
        P(),
        P(),
        P(everywhere, None),
        P(everywhere),
        P(everywhere),
        P(everywhere, None),
        P(everywhere),
    )
    return jax.shard_map(
        local,
        mesh=mesh,
        in_specs=placed,
        out_specs=(P(everywhere, None), P(everywhere, None, None)),
        check_vma=False,
    )
```

```python
import math

import jax
import jax.numpy as jnp
from jax import lax
from jax.experimental import pallas as pl
from jax.experimental.pallas import tpu as pltpu
from jax.sharding import PartitionSpec as P

VHEADS = 8
VHEAD = 80
HEAD = 128
KVHEADS = 4
SHARED = 8
BLK = 64
LEN = 32
CAP = 4
PEERS = 16
PAIRS = 4
PIECES = 2
PER = KVHEADS // PIECES
WIDE = PER * 2 * HEAD
GROUPS = 2
GROUP = KVHEADS // GROUPS
GWIDE = GROUP * 2 * HEAD
EPS = 1e-05
MESH = pl.DeviceIdType.MESH
f32 = jnp.float32
bf16 = jnp.bfloat16


def dot_nn(left, right):
    return jnp.dot(left, right, preferred_element_type=f32)


def dot_nt(left, right):
    return lax.dot_general(left, right, (((1,), (1,)), ((), ())), preferred_element_type=f32)


def dot_tn(left, right):
    return lax.dot_general(left, right, (((0,), (0,)), ((), ())), preferred_element_type=f32)


def exchange(source, target, me, send_sem, recv_sem, own_sem=None):
    def body(step, carry):
        peer = lax.rem(me + step, PEERS)
        pltpu.make_async_remote_copy(
            src_ref=source.at[peer],
            dst_ref=target.at[me],
            send_sem=send_sem,
            recv_sem=recv_sem,
            device_id={"seq": peer},
            device_id_type=MESH,
        ).start()
        return carry

    lax.fori_loop(1, PEERS, body, 0)
    if own_sem is None:
        target[me] = source[me]
    else:
        pltpu.make_async_copy(source.at[me], target.at[me], own_sem).start()


def wait_all(buffer, sem):
    view = buffer.at[pl.ds(0, PEERS - 1)]
    pltpu.make_async_copy(view, view, sem).wait()


def split_colors(src_partner, dst_partner, doublings):
    n = src_partner.shape[0]
    row = lax.broadcasted_iota(jnp.int32, (n, n), 0)
    col = lax.broadcasted_iota(jnp.int32, (n, n), 1)
    src_b = jnp.where(src_partner, 1.0, 0.0).astype(bf16)
    dst_b = jnp.where(dst_partner, 1.0, 0.0).astype(bf16)
    power = dot_nn(src_b, dst_b).astype(bf16)
    total = jnp.where(row == col, 1.0, 0.0) + power.astype(f32)
    yield
    for _ in range(doublings - 1):
        power = dot_nn(power, power).astype(bf16)
        total = total + dot_nn(total.astype(bf16), power)
        yield
    orbit = total > 0.5
    lead_c = jnp.min(jnp.where(orbit, col, n), axis=1, keepdims=True)
    lead_r = jnp.min(jnp.where(orbit, row, n), axis=0, keepdims=True)
    other_c = jnp.sum(jnp.where(src_partner, lead_r, 0), axis=1, keepdims=True)
    other_r = jnp.sum(jnp.where(src_partner, lead_c, 0), axis=0, keepdims=True)
    return (lead_c < other_c).astype(jnp.int32), (lead_r < other_r).astype(jnp.int32)


def color_tables(dest, me):
    n = dest.shape[0]
    row = lax.broadcasted_iota(jnp.int32, (n, n), 0)
    col = lax.broadcasted_iota(jnp.int32, (n, n), 1)
    dest_t = jnp.transpose(dest.astype(f32)).astype(jnp.int32)
    owner_c, owner_r = dest >> 4, dest_t >> 4
    parity_same = (row & 1) == (col & 1)
    src_same = ((row >> 3) == (col >> 3)) & parity_same
    dst_same = (owner_c == owner_r) & parity_same
    rank_c = jnp.sum(jnp.where(dst_same & (col < row), 1, 0), axis=1, keepdims=True)
    rank_r = jnp.sum(jnp.where(dst_same & (row < col), 1, 0), axis=0, keepdims=True)
    src_partner = col == (row ^ 2)
    dst_partner = dst_same & (rank_r == (rank_c ^ 1))
    yield
    one_c, one_r = yield from split_colors(src_partner, dst_partner, 5)
    yield
    alike = (one_c == one_r) & (row != col)
    two_c, _ = yield from split_colors(src_same & alike, dst_same & alike, 4)
    yield
    color = jnp.broadcast_to(2 * one_c + two_c, (n, n))
    src = row >> 3
    pair = (row & 7) >> 1
    half = row & 1
    even = half == 0
    mine = src == me
    turn, turn2 = me // 4, me // 8

    def pick(mask, value):
        return jnp.sum(jnp.where(mask, value, 0), axis=0, keepdims=True)

    rows = [
        pick(mine & even & (color == col), pair),
        pick(mine & even & (pair == col), color),
        pick(even & (color == turn2) & (owner_c == col), src),
        pick(even & (color == turn) & (src == col), owner_c),
        pick((owner_c == me) & ((dest & 15) == col), 2 * color + half + 1) - 1,
        pick((owner_c == me) & (2 * color + half == col), dest & 15),
        pick(even & (color == 2 + turn2) & (owner_c == col), src),
    ]
    rows += [jnp.zeros_like(rows[0])]
    return jnp.concatenate(rows, axis=0)


PLANES = 8
ROWS = 160
PIECE = 256
ARRIVALS = PLANES - 1
WINDOW = 384
LOG2E = 1.4426950408889634


def softmax_over_rows(scores, allowed, scale):
    masked = jnp.where(allowed, scores, -jnp.inf)
    top = jnp.max(masked, axis=0, keepdims=True)
    terms = jnp.exp2((masked - top) * (scale * LOG2E))
    return terms * (1.0 / jnp.sum(terms, axis=0, keepdims=True))


def kernel(
    image_hbm,
    dest_hbm,
    kimg_hbm,
    seen_hbm,
    gain_hbm,
    qg_hbm,
    kg_hbm,
    x_hbm,
    qkv_hbm,
    out_hbm,
    kv_hbm,
    q_hbm,
    og_hbm,
    att_hbm,
    back_hbm,
    tab_hbm,
    image_ref,
    dest_ref,
    kimg_ref,
    seen_ref,
    gain_ref,
    qg_ref,
    kg_ref,
    x_ref,
    own_out,
    own_qkv,
    q_ref,
    og_ref,
    att_ref,
    dest_tile,
    every,
    tab_tile,
    tab_ref,
    seen_rows,
    weight,
    out_parts,
    out_ref,
    kv_ref,
    normed,
    summed,
    mixed,
    att,
    hidden,
    pay,
    qn,
    gkv,
    got1,
    out2,
    got2,
    out3,
    got3,
    out4,
    local_sem,
    dest_sem,
    own_sem,
    kv_sem,
    z_send,
    z_recv,
    o_send,
    o_recv,
    r_send,
    r_recv,
    m_send,
    m_recv,
    ro_send,
    ro_recv,
    mo_send,
    mo_recv,
    oo_sem,
    att_sem,
    own_back,
    f_send,
    f_recv,
    send_sem,
    recv_sem,
):
    pairs_here, span, vis = x_ref.shape
    tokens = pairs_here * span
    e, q, m = lax.axis_index("enc"), lax.axis_index("seq"), lax.axis_index("mp")
    other = 1 - m
    d = 1 - 2 * m
    stride = 1 + 3 * m
    pos = lax.rem(q // stride, 4)
    ring = q - pos * stride
    left, right, far = lax.rem(pos + 3, 4), lax.rem(pos + 1, 4), lax.rem(pos + 2, 4)
    ahead, behind = lax.rem(e + d + PLANES, PLANES), lax.rem(e - d + PLANES, PLANES)
    to_left, to_right = {"seq": ring + left * stride}, {"seq": ring + right * stride}
    to_ahead, to_behind, to_mate = {"enc": ahead}, {"enc": behind}, {"mp": other}

    def remote(source, target, send, recv, device):
        pltpu.make_async_remote_copy(
            src_ref=source,
            dst_ref=target,
            send_sem=send,
            recv_sem=recv,
            device_id=device,
            device_id_type=MESH,
        ).start()

    def done(view, sem):
        pltpu.make_async_copy(view, view, sem).wait()

    half_rows = ROWS // 2
    own_rows = pl.ds(pl.multiple_of(m * half_rows, half_rows), half_rows)
    mate_rows = pl.ds(pl.multiple_of(other * half_rows, half_rows), half_rows)
    kv_half = kv_hbm.shape[0]
    kv_rows = pl.ds(pl.multiple_of(m * kv_half, kv_half), kv_half)
    copies = [
        pltpu.make_async_copy(source, target, local_sem.at[index])
        for index, (source, target) in enumerate(
            (
                (qkv_hbm, own_qkv),
                (x_hbm, x_ref),
                (out_hbm, own_out),
                (kv_hbm, kv_ref.at[kv_rows]),
                (q_hbm, q_ref),
                (og_hbm, og_ref),
                (tab_tile, tab_ref),
                (tab_tile, tab_hbm),
                (dest_hbm, dest_ref),
                (seen_hbm, seen_ref),
                (gain_hbm, gain_ref),
                (image_hbm, image_ref),
                (kimg_hbm, kimg_ref),
                (qg_hbm, qg_ref),
                (kg_hbm, kg_ref),
            )
        )
    ]
    qkv_copy, x_copy, out_copy, kv_copy, q_copy, og_copy, tab_copy, tab_out = copies[:8]
    dest_copy, seen_copy, gain_copy = copies[8:11]
    late = copies[11:]
    for copy in [qkv_copy] + copies[8:] + copies[1:6]:
        copy.start()

    barrier = pltpu.get_barrier_semaphore()

    def hello(step, carry):
        pl.semaphore_signal(
            barrier, inc=1, device_id={"seq": lax.rem(q + step, PEERS)}, device_id_type=MESH
        )
        return carry

    lax.fori_loop(1, PEERS, hello, 0)
    for device in (to_ahead, to_behind, to_mate):
        pl.semaphore_signal(barrier, inc=1, device_id=device, device_id_type=MESH)

    sub = lax.broadcasted_iota(jnp.int32, (8, 128), 0)
    lane = lax.broadcasted_iota(jnp.int32, (8, 128), 1)
    tile = jnp.zeros((8, 128), jnp.int32)
    for copy in (dest_copy, seen_copy, gain_copy):
        copy.wait()
    for block in range(8):
        tile = jnp.where(sub == block, dest_ref[block], tile)
    dest_tile[...] = tile
    every[q] = tile
    spread = jnp.where(lane // LEN == sub, seen_ref[...].astype(f32), 0.0).astype(bf16)
    wide = (128, SHARED * LEN)
    place = lax.rem(lax.broadcasted_iota(jnp.int32, wide, 0), LEN) == lax.rem(
        lax.broadcasted_iota(jnp.int32, wide, 1), LEN
    )
    seen_rows[...] = dot_nn(spread, jnp.where(place, 1.0, 0.0).astype(bf16)).astype(jnp.int32)
    gain = jnp.concatenate([gain_ref[t : t + 1, :] for t in range(vis // 128)], axis=1)
    out_copy.wait()
    have = own_out.shape[0]
    for place in range(4):
        at = min(place * WINDOW, vis - WINDOW)
        out_parts[m, e, place, 0:have, :] = own_out[:, at : at + WINDOW]
    qkv_copy.wait()
    for p in range(8):
        count = min(PIECE, own_qkv.shape[1] - p * PIECE)
        weight[p, e, own_rows, 0:count] = own_qkv[:, p * PIECE : p * PIECE + count]
    pl.semaphore_wait(barrier, PEERS + 2)

    mine = 4 * m + pos

    def side(core):
        return pl.ds(4 * core, 4)

    for which, core in ((0, other), (1, m)):
        view = weight.at[side(core), e, own_rows]
        remote(view, view, own_sem.at[0, which], own_sem.at[1, which], to_mate)

    def send_z(plane, which, arrival):
        view = weight.at[mine, plane, mate_rows if which else own_rows]
        device = to_behind if arrival % 2 else to_ahead
        remote(view, view, z_send.at[arrival, which], z_recv.at[arrival, which], device)

    send_z(e, 0, 0)
    send_z(e, 0, 1)
    view = out_parts.at[m, e]
    remote(view, view, oo_sem.at[0], oo_sem.at[1], to_mate)

    def send_dest(step, carry):
        peer = lax.rem(q + step, PEERS)
        remote(dest_tile, every.at[q], dest_sem.at[0], dest_sem.at[1], {"seq": peer})
        return carry

    lax.fori_loop(1, PEERS, send_dest, 0)
    done(weight.at[side(m), e, mate_rows], own_sem.at[1, 0])
    send_z(e, 1, 0)
    send_z(e, 1, 1)
    kv_there = kv_ref.at[kv_rows]

    def send_out(plane, arrival):
        view = out_parts.at[m, plane, pos]
        device = to_behind if arrival % 2 else to_ahead
        remote(view, view, o_send.at[arrival], o_recv.at[arrival], device)

    def plane_of(arrival):
        hops = arrival // 2 + 1
        if arrival % 2 == 0:
            return lax.rem(e - d * hops + PLANES, PLANES)
        return lax.rem(e + d * hops + PLANES, PLANES)

    def piece(k, place):
        return weight.at[4 * m + place, plane_of(k)]

    def part(k, place, which):
        return weight.at[4 * m + place, plane_of(k), pl.ds(which * half_rows, half_rows)]

    width = VHEADS * VHEAD

    def norm_jobs():
        x_copy.wait()
        for t in range(tokens // 64):
            rows = slice(t * 64, t * 64 + 64)
            values = x_ref[t // 2, t % 2 * 64 : t % 2 * 64 + 64, :].astype(f32)
            center = values - jnp.mean(values, axis=-1, keepdims=True)
            spread = jnp.mean(center * center, axis=-1, keepdims=True)
            result = (center * lax.rsqrt(spread + EPS) * gain).astype(bf16)
            for plane in range(PLANES):
                normed[plane, rows, :] = result[:, plane * ROWS : (plane + 1) * ROWS]
            yield

    def table_jobs():
        wait_all(every, dest_sem.at[1])
        tab_tile[...] = yield from color_tables(every[...].reshape(PEERS * 8, 128), q)
        tab_copy.start()
        tab_out.start()

    def add_plane(plane, mode, p):
        count = min(PIECE, 3 * width - p * PIECE)
        cols = slice(p * PIECE, p * PIECE + count)
        found = dot_nn(normed[plane], weight[p, plane, :, 0:count])
        if mode == 0:
            summed[:, cols] = found
        elif mode == 1:
            summed[:, cols] += found
        else:
            total = (summed[:, cols] + found).astype(bf16)
            mixed[:, :, cols] = total.reshape(PAIRS, span, count)

    def plane_jobs(k):
        if k < 0:
            done(weight.at[side(other), e, mate_rows], own_sem.at[1, 1])
            plane = e
        else:
            same = k ^ 1 if k < ARRIVALS - 1 else k
            done(weight.at[side(m), e], m_recv.at[same])
            plane = plane_of(k)
        mode = 0 if k < 0 else 1 if k < ARRIVALS - 1 else 2
        for p in range(8):
            add_plane(plane, mode, p)
            if p % 3 == 2:
                yield
        yield

    def query_jobs():
        q_copy.wait()
        for copy in late:
            copy.wait()
        for g in range(KVHEADS):
            block = q_ref[:, g * SHARED * HEAD : (g + 1) * SHARED * HEAD]
            for hh in range(SHARED):
                x = block[:, hh * HEAD : (hh + 1) * HEAD].astype(f32)
                inv = lax.rsqrt(jnp.mean(x * x, axis=-1, keepdims=True) + EPS)
                y = (x * inv * qg_ref[...]).astype(bf16)
                for s in range(CAP):
                    qn[g, s, hh * LEN : (hh + 1) * LEN, :] = y[s * LEN : (s + 1) * LEN, :]
            yield

    def out_jobs(k):
        if k < 0:
            plane = e
            done(out_parts.at[m, e], oo_sem.at[1])
        else:
            plane = plane_of(k)
            done(out_parts.at[m, e], mo_recv.at[k ^ 1 if k < ARRIVALS - 1 else k])
        both = []
        for core in range(2):
            parts = [out_parts[core, plane, place, 0:have, :] for place in range(4)]
            parts[3] = parts[3][:, 4 * WINDOW - vis :]
            both.append(jnp.concatenate(parts, axis=1).astype(f32))
        rows = pl.ds(pl.multiple_of(2 * have * plane, 2 * have), 2 * have)
        out_ref[rows, :] = jnp.concatenate(both, axis=0).astype(bf16)
        yield

    queue = [norm_jobs(), table_jobs(), plane_jobs(-1), query_jobs()]

    def pump(steps):
        while queue and steps > 0:
            try:
                next(queue[0])
                steps -= 1
            except StopIteration:
                queue.pop(0)

    send_out(e, 0)
    send_out(e, 1)
    remote(kv_hbm, kv_there, kv_sem.at[0], kv_sem.at[1], to_mate)
    pump(2)
    hops = ((0, 1), (2, 3), (4, 5), (6,))
    for t in range(len(hops) + 2):
        if t < len(hops):
            for which in range(2):
                for k in hops[t]:
                    rows = mate_rows if which else own_rows
                    done(weight.at[mine, plane_of(k), rows], z_recv.at[k, which])
                    if k + 2 < ARRIVALS:
                        send_z(plane_of(k), which, k + 2)
            for k in hops[t]:
                view = piece(k, pos)
                remote(view, view, r_send.at[k, 0], r_recv.at[k, 0], to_right)
                remote(view, view, r_send.at[k, 1], r_recv.at[k, 1], to_left)
            for k in hops[t]:
                view = out_parts.at[m, plane_of(k), pos]
                done(view, o_recv.at[k])
                if k + 2 < ARRIVALS:
                    send_out(plane_of(k), k + 2)
                remote(view, view, ro_send.at[k, 0], ro_recv.at[k, 0], to_right)
                remote(view, view, ro_send.at[k, 1], ro_recv.at[k, 1], to_left)
        pump(2)
        if 0 <= t - 1 < len(hops):
            for k in hops[t - 1]:
                view = part(k, left, 0)
                done(piece(k, left), r_recv.at[k, 0])
                remote(view, view, r_send.at[k, 2], r_recv.at[k, 2], to_right)
                view = part(k, right, 1)
                done(piece(k, right), r_recv.at[k, 1])
                remote(view, view, r_send.at[k, 3], r_recv.at[k, 3], to_left)
            for k in hops[t - 1]:
                from_left = out_parts.at[m, plane_of(k), left]
                from_right = out_parts.at[m, plane_of(k), right]
                done(from_left, ro_recv.at[k, 0])
                done(from_right, ro_recv.at[k, 1])
                if k % 2 == 0:
                    remote(from_left, from_left, ro_send.at[k, 2], ro_recv.at[k, 2], to_right)
                else:
                    remote(from_right, from_right, ro_send.at[k, 2], ro_recv.at[k, 2], to_left)
        pump(2)
        if 0 <= t - 2 < len(hops):
            for k in hops[t - 2]:
                done(part(k, far, 0), r_recv.at[k, 2])
                done(part(k, far, 1), r_recv.at[k, 3])
                view = weight.at[side(m), plane_of(k)]
                remote(view, view, m_send.at[k], m_recv.at[k], to_mate)
            for k in hops[t - 2]:
                done(out_parts.at[m, plane_of(k), far], ro_recv.at[k, 2])
                view = out_parts.at[m, plane_of(k)]
                remote(view, view, mo_send.at[k], mo_recv.at[k], to_mate)
        pump(2)
        if t == 1:
            queue.append(out_jobs(-1))
        if 0 <= t - 2 < len(hops):
            queue.extend(plane_jobs(k) for k in hops[t - 2])
        if 0 <= t - 3 < len(hops):
            queue.extend(out_jobs(k) for k in hops[t - 3])
    pump(1000)
    queue.append(out_jobs(ARRIVALS - 1))

    row = lax.broadcasted_iota(jnp.int32, (span, span), 0)
    col = lax.broadcasted_iota(jnp.int32, (span, span), 1)
    near = (row // BLK) == (col // BLK)

    def window(head):
        first, last = head * VHEAD // 128, ((head + 1) * VHEAD - 1) // 128
        return first, last, first * 128, (last - first + 1) * 128

    def attend_pair(c):
        pair = tab_ref[0, c] & 3
        allowed = near | (image_ref[2 * pair] == image_ref[2 * pair + 1])
        insides, scores = [], []
        for head in range(VHEADS):
            _, _, base, cut = window(head)
            lanes = lax.broadcasted_iota(jnp.int32, (span, cut), 1) + base
            inside = (lanes >= head * VHEAD) & (lanes < (head + 1) * VHEAD)
            query = jnp.where(inside, mixed[pair, :, base : base + cut], jnp.zeros((), bf16))
            key = mixed[pair, :, width + base : width + base + cut]
            insides.append(inside)
            scores.append(dot_nt(key, query))
        weights = [
            softmax_over_rows(found, allowed, 1.0 / math.sqrt(VHEAD)).astype(bf16)
            for found in scores
        ]
        tiles = [None] * (width // 128)
        for head in range(VHEADS):
            first, last, base, cut = window(head)
            value = mixed[pair, :, 2 * width + base : 2 * width + base + cut]
            result = dot_tn(weights[head], value)
            for t in range(first, last + 1):
                at = (t - first) * 128
                found = result[:, at : at + 128]
                if tiles[t] is not None:
                    found = jnp.where(insides[head][:, at : at + 128], found, tiles[t])
                tiles[t] = found
        att[c] = jnp.concatenate(tiles, axis=1).astype(bf16)

    half = KVHEADS * HEAD
    tab_copy.wait()
    for a in range(2):
        pairs = (2 * a, 2 * a + 1)

        def attend_pairs(c, carry):
            attend_pair(c)
            return carry

        lax.fori_loop(pairs[0], pairs[1] + 1, attend_pairs, 0)
        if a == 0:
            pump(1000)
        attended = jnp.concatenate([att[c] for c in pairs], axis=0)

        def project(t, carry):
            cols = pl.ds(pl.multiple_of(t * 256, 256), 256)
            tokens_in = jnp.concatenate(
                [x_ref[tab_ref[0, c] & 3, :, cols] for c in pairs], axis=0
            )
            total = tokens_in.astype(f32) + dot_nn(attended, out_ref[:, cols])
            hidden[a, :, cols] = total.astype(bf16)
            return carry

        lax.fori_loop(0, vis // 256, project, 0)
        if a == 0:
            kv_copy.wait()
            done(kv_there, kv_sem.at[1])
        for b in range(GROUPS):
            for t in range(GROUP):
                at = (b * GROUP + t) * HEAD
                both = jnp.concatenate(
                    [kv_ref[:, at : at + HEAD], kv_ref[:, half + at : half + at + HEAD]], axis=1
                )
                pay[a][b][:, :, t * 2 * HEAD : (t + 1) * 2 * HEAD] = (
                    dot_nn(hidden[a], both).astype(bf16).reshape(PEERS, BLK // 4, 2 * HEAD)
                )
            exchange(pay[a][b], got1[a][b], q, f_send.at[0, a, b], f_recv.at[0, a, b])

    og_copy.wait()

    def shuffle(got, out, table):
        def body(index, carry):
            out[index] = got[tab_ref[table, index] & 15]
            return carry

        lax.fori_loop(0, PEERS, body, 0)

    def relay(a, b):
        wait_all(got1[a][b], f_recv.at[0, a, b])
        shuffle(got1[a][b], out2[a][b], 6 if a else 2)
        exchange(out2[a][b], got2[b].at[pl.ds(a * PEERS, PEERS)], q, f_send.at[1, a, b], f_recv.at[1, a, b])

    def give_back(h):
        wait_all(got3[h], recv_sem.at[0, h])
        shuffle(got3[h], out4[h], 3)
        exchange(out4[h], back_hbm.at[h], q, send_sem.at[1, h], recv_sem.at[1, h], own_back.at[h])

    def one(h, gi, s):
        g = h * PER + gi
        at = pl.multiple_of(gi * 2 * HEAD, 2 * HEAD)
        group = h * PER // GROUP
        from_col = pl.multiple_of((h * PER % GROUP + gi) * 2 * HEAD, 2 * HEAD)
        yield
        blocks, masks = [], []
        seen = seen_rows[pl.ds(s, 1), :]
        for kb in range(CAP):
            index = tab_ref[4, s * CAP + kb]
            start = 4 * (jnp.maximum(index, 0) & 7)
            block = got2[group][pl.ds(start, 4), :, pl.ds(from_col, 2 * HEAD)]
            blocks.append(
                jnp.where(index >= 0, block, jnp.zeros((), bf16)).reshape(BLK, 2 * HEAD)
            )
            masks.append(jnp.broadcast_to(kimg_ref[s, kb] < seen, (BLK, SHARED * LEN)))
        keyval = jnp.concatenate(blocks, axis=0)
        allowed = jnp.concatenate(masks, axis=0)
        keys = keyval[:, :HEAD].astype(f32)
        values = keyval[:, HEAD:]
        inv = lax.rsqrt(jnp.mean(keys * keys, axis=-1, keepdims=True) + EPS)
        kn = (keys * inv * kg_ref[...]).astype(bf16)
        yield
        queries = qn[g, s]
        rows = pl.ds(pl.multiple_of(s * LEN, LEN), LEN)
        cols = pl.ds(pl.multiple_of(g * SHARED * HEAD, SHARED * HEAD), SHARED * HEAD)
        grad_row = og_ref[rows, cols]
        grads = jnp.concatenate(
            [grad_row[:, hh * HEAD : (hh + 1) * HEAD] for hh in range(SHARED)], axis=0
        )
        scale = 1.0 / math.sqrt(HEAD)
        scores = dot_nt(kn, queries)
        grad_dot = dot_nt(values, grads)
        yield
        weights = softmax_over_rows(scores, allowed, scale)
        rounded = weights.astype(bf16)
        yield
        attended = dot_tn(rounded, values).astype(bf16)
        att_ref[rows, cols] = jnp.concatenate(
            [attended[hh * LEN : (hh + 1) * LEN, :] for hh in range(SHARED)], axis=1
        )
        grad_values = dot_nn(rounded, grads)
        yield
        delta = jnp.sum(weights * grad_dot, axis=0, keepdims=True)
        grad_scores = (weights * (grad_dot - delta) * scale).astype(bf16)
        yield
        gained = dot_nn(grad_scores, queries) * kg_ref[...]
        yield
        mean = jnp.mean(keys * gained, axis=-1, keepdims=True)
        grad_keys = inv * (gained - keys * inv * inv * mean)
        result = jnp.concatenate([grad_keys, grad_values], axis=1).astype(bf16)
        gkv[pl.ds(s * CAP, CAP), :, pl.ds(at, 2 * HEAD)] = result.reshape(CAP, BLK, 2 * HEAD)

    def attend(h):
        if h * PER % GROUP == 0:
            for a in range(2):
                wait_all(got2[h * PER // GROUP], f_recv.at[1, a, h * PER // GROUP])

        def body(gi, carry):
            running = [one(h, gi, s) for s in range(CAP)]
            while running:
                running = [steps for steps in running if next(steps, running) is not running]
            return carry

        lax.fori_loop(0, PER, body, 0)

        def pack(cb, carry):
            block = gkv[tab_ref[5, cb] & 15]
            out3[h][pl.ds(2 * cb, 2)] = block.reshape(2, BLK // 2, WIDE)
            return carry

        lax.fori_loop(0, 2 * PAIRS, pack, 0)
        exchange(out3[h], got3[h], q, send_sem.at[0, h], recv_sem.at[0, h])
        cols = slice(h * PER * SHARED * HEAD, (h + 1) * PER * SHARED * HEAD)
        pltpu.make_async_copy(att_ref.at[:, cols], att_hbm.at[:, cols], att_sem.at[h]).start()

    for a in range(2):
        for b in range(GROUPS):
            relay(a, b)
    for h in range(PIECES):
        attend(h)
        if h > 0:
            give_back(h - 1)
    give_back(PIECES - 1)
    for h in range(PIECES):
        wait_all(back_hbm.at[h], recv_sem.at[1, h])

    tab_out.wait()
    for h in range(PIECES):
        cols = slice(h * PER * SHARED * HEAD, (h + 1) * PER * SHARED * HEAD)
        pltpu.make_async_copy(att_ref.at[:, cols], att_hbm.at[:, cols], att_sem.at[h]).wait()
        pltpu.make_async_copy(out4[h].at[q], back_hbm.at[h, q], own_back.at[h]).wait()
        for phase in range(2):
            wait_all(got3[h], send_sem.at[phase, h])
    for a in range(2):
        for b in range(GROUPS):
            for phase in range(2):
                wait_all(got1[a][b], f_send.at[phase, a, b])
    wait_all(every, dest_sem.at[0])
    for which in range(2):
        done(weight.at[side(m), e, own_rows], own_sem.at[0, which])
    done(kv_there, kv_sem.at[0])
    done(out_parts.at[m, e], oo_sem.at[0])
    for k in range(ARRIVALS):
        for which in range(2):
            done(weight.at[mine, e, own_rows], z_send.at[k, which])
        done(out_parts.at[m, e, pos], o_send.at[k])
        done(out_parts.at[m, e], mo_send.at[k])
        for way in range(3):
            done(out_parts.at[m, e, pos], ro_send.at[k, way])
        for way in range(4):
            done(piece(k, pos) if way < 2 else part(k, pos, 0), r_send.at[k, way])
        done(weight.at[side(m), e], m_send.at[k])


def place_kernel(tab_hbm, att_hbm, back_hbm, att_out, kvg_out, tab_ref, att, back, kvg, sems):
    parts = 4
    rows = att.shape[0] // parts
    att_in, back_in, att_back, kvg_back = [], [], [], []
    for t in range(parts):
        view = pl.ds(t * rows, rows)
        att_in.append(pltpu.make_async_copy(att_hbm.at[view], att.at[view], sems.at[0, t]))
        att_back.append(pltpu.make_async_copy(att.at[view], att_out.at[view], sems.at[1, t]))
    for h in range(PIECES):
        back_in.append(pltpu.make_async_copy(back_hbm.at[h], back.at[h], sems.at[2, h]))
    for j in range(PAIRS):
        view = pl.ds(2 * j, 2)
        kvg_back.append(pltpu.make_async_copy(kvg.at[view], kvg_out.at[view], sems.at[3, j]))
    tab_in = pltpu.make_async_copy(tab_hbm, tab_ref, sems.at[4, 0])
    for copy in [tab_in] + back_in + att_in:
        copy.start()
    for copy in [tab_in] + back_in:
        copy.wait()
    half = KVHEADS * HEAD
    for j in range(PAIRS):
        color = tab_ref[1, j] & 3
        for g in range(KVHEADS):
            at = g % PER * 2 * HEAD
            block = back[g // PER, pl.ds(4 * color, 4), :, at : at + 2 * HEAD]
            block = block.reshape(2, BLK, 2 * HEAD)
            kvg[2 * j : 2 * j + 2, :, g * HEAD : (g + 1) * HEAD] = block[:, :, :HEAD]
            kvg[2 * j : 2 * j + 2, :, half + g * HEAD : half + (g + 1) * HEAD] = block[:, :, HEAD:]
        kvg_back[j].start()
    for coming, going in zip(att_in, att_back):
        coming.wait()
        going.start()
    for copy in kvg_back + att_back:
        copy.wait()


HBM = pl.BlockSpec(memory_space=pltpu.HBM)
LIMIT = 62 * 1024 * 1024


def local(
    images,
    vit_gain,
    vit_qkv,
    vit_out,
    kv_weight,
    queries,
    q_gain,
    k_gain,
    out_grad,
    block_image,
    block_dest,
    key_image,
    text_seen,
):
    enc_blocks, block_len, vis = images.shape
    tokens = enc_blocks * block_len
    buffers = [pltpu.VMEM((PEERS, BLK // 2, WIDE), bf16)] * PIECES
    chunks = [[pltpu.VMEM((PEERS, BLK // 4, GWIDE), bf16)] * GROUPS] * 2
    dma = pltpu.SemaphoreType.DMA
    attended, back, tables = pl.pallas_call(
        kernel,
        out_shape=(
            jax.ShapeDtypeStruct(queries.shape, bf16),
            jax.ShapeDtypeStruct((PIECES, PEERS, BLK // 2, WIDE), bf16),
            jax.ShapeDtypeStruct((8, 128), jnp.int32),
        ),
        in_specs=[HBM] * 13,
        out_specs=(HBM, HBM, HBM),
        scratch_shapes=[
            pltpu.SMEM(block_image.shape, jnp.int32),
            pltpu.SMEM(block_dest.shape, jnp.int32),
            pltpu.SMEM(key_image.shape, jnp.int32),
            pltpu.VMEM((1, CAP * LEN), jnp.int32),
            pltpu.VMEM((vis // 128, 128), f32),
            pltpu.VMEM((1, HEAD), f32),
            pltpu.VMEM((1, HEAD), f32),
            pltpu.VMEM((PAIRS, 2 * BLK, vis), bf16),
            pltpu.VMEM(vit_out.shape, bf16),
            pltpu.VMEM(vit_qkv.shape, bf16),
            pltpu.VMEM(queries.shape, bf16),
            pltpu.VMEM(queries.shape, bf16),
            pltpu.VMEM(queries.shape, bf16),
            pltpu.VMEM((8, 128), jnp.int32),
            pltpu.VMEM((PEERS, 8, 128), jnp.int32),
            pltpu.VMEM((8, 128), jnp.int32),
            pltpu.SMEM((8, 128), jnp.int32),
            pltpu.VMEM((8, SHARED * LEN), jnp.int32),
            pltpu.VMEM((8, PLANES, ROWS, PIECE), bf16),
            pltpu.VMEM((2, PLANES, 4, 48, WINDOW), bf16),
            pltpu.VMEM((VHEADS * VHEAD, vis), bf16),
            pltpu.VMEM((vis, 2 * KVHEADS * HEAD), bf16),
            pltpu.VMEM((PLANES, tokens, ROWS), bf16),
            pltpu.VMEM((tokens, 3 * VHEADS * VHEAD), f32),
            pltpu.VMEM((PAIRS, 2 * BLK, 3 * VHEADS * VHEAD), bf16),
            pltpu.VMEM((PAIRS, 2 * BLK, VHEADS * VHEAD), bf16),
            pltpu.VMEM((2, 4 * BLK, vis), bf16),
            chunks,
            pltpu.VMEM((KVHEADS, CAP, SHARED * LEN, HEAD), bf16),
            pltpu.VMEM((CAP * CAP, BLK, WIDE), bf16),
            chunks,
            chunks,
            [pltpu.VMEM((2 * PEERS, BLK // 4, GWIDE), bf16)] * GROUPS,
            buffers,
            buffers,
            buffers,
            dma((15,)),
            dma((2,)),
            dma((2, 2)),
            dma((2,)),
        ]
        + [dma((ARRIVALS, 2))] * 2
        + [dma((ARRIVALS,))] * 2
        + [dma((ARRIVALS, 4))] * 2
        + [dma((ARRIVALS,))] * 2
        + [dma((ARRIVALS, 3))] * 2
        + [dma((ARRIVALS,))] * 2
        + [dma((2,)), dma((PIECES,)), dma((PIECES,))]
        + [dma((2, 2, GROUPS))] * 2
        + [dma((2, PIECES))] * 2,
        compiler_params=pltpu.CompilerParams(
            collective_id=0, has_side_effects=True, vmem_limit_bytes=LIMIT
        ),
    )(
        block_image,
        block_dest,
        key_image,
        text_seen.reshape(1, -1),
        vit_gain.reshape(-1, 128),
        q_gain.reshape(1, HEAD),
        k_gain.reshape(1, HEAD),
        images.reshape(PAIRS, 2 * BLK, vis),
        vit_qkv,
        vit_out,
        kv_weight,
        queries,
        out_grad,
    )
    attended, kv_grad = pl.pallas_call(
        place_kernel,
        out_shape=(
            jax.ShapeDtypeStruct(queries.shape, bf16),
            jax.ShapeDtypeStruct((enc_blocks, block_len, 2 * KVHEADS * HEAD), bf16),
        ),
        in_specs=[HBM, HBM, HBM],
        out_specs=(HBM, HBM),
        scratch_shapes=[
            pltpu.SMEM((8, 128), jnp.int32),
            pltpu.VMEM(queries.shape, bf16),
            pltpu.VMEM((PIECES, PEERS, BLK // 2, WIDE), bf16),
            pltpu.VMEM((enc_blocks, block_len, 2 * KVHEADS * HEAD), bf16),
            dma((5, 4)),
        ],
        compiler_params=pltpu.CompilerParams(vmem_limit_bytes=LIMIT),
    )(tables, attended, back)
    return attended, kv_grad


def solution(mesh):
    everywhere = ("enc", "seq", "mp")
    placed = (
        P(everywhere, None, None),
        P(),
        P(("enc", "mp"), None),
        P(("enc", "mp"), None),
        P("mp", None),
        P(everywhere, None),
        P(),
        P(),
        P(everywhere, None),
        P(everywhere),
        P(everywhere),
        P(everywhere, None),
        P(everywhere),
    )
    return jax.shard_map(
        local,
        mesh=mesh,
        in_specs=placed,
        out_specs=(P(everywhere, None), P(everywhere, None, None)),
        check_vma=False,
    )
```

```python
import math

import jax
import jax.numpy as jnp
from jax import lax
from jax.experimental import pallas as pl
from jax.experimental.pallas import tpu as pltpu
from jax.sharding import PartitionSpec as P

VHEADS = 8
VHEAD = 80
HEAD = 128
KVHEADS = 4
SHARED = 8
BLK = 64
LEN = 32
CAP = 4
PEERS = 16
PAIRS = 4
PIECES = 2
PER = KVHEADS // PIECES
WIDE = PER * 2 * HEAD
GROUPS = 2
GROUP = KVHEADS // GROUPS
GWIDE = GROUP * 2 * HEAD
EPS = 1e-05
MESH = pl.DeviceIdType.MESH
f32 = jnp.float32
bf16 = jnp.bfloat16


def dot_nn(left, right):
    return jnp.dot(left, right, preferred_element_type=f32)


def dot_nt(left, right):
    return lax.dot_general(left, right, (((1,), (1,)), ((), ())), preferred_element_type=f32)


def dot_tn(left, right):
    return lax.dot_general(left, right, (((0,), (0,)), ((), ())), preferred_element_type=f32)


def exchange(source, target, me, send_sem, recv_sem, own_sem=None):
    def body(step, carry):
        peer = lax.rem(me + step, PEERS)
        pltpu.make_async_remote_copy(
            src_ref=source.at[peer],
            dst_ref=target.at[me],
            send_sem=send_sem,
            recv_sem=recv_sem,
            device_id={"seq": peer},
            device_id_type=MESH,
        ).start()
        return carry

    lax.fori_loop(1, PEERS, body, 0)
    if own_sem is None:
        target[me] = source[me]
    else:
        pltpu.make_async_copy(source.at[me], target.at[me], own_sem).start()


def wait_all(buffer, sem):
    view = buffer.at[pl.ds(0, PEERS - 1)]
    pltpu.make_async_copy(view, view, sem).wait()


def split_colors(src_partner, dst_partner, doublings):
    n = src_partner.shape[0]
    row = lax.broadcasted_iota(jnp.int32, (n, n), 0)
    col = lax.broadcasted_iota(jnp.int32, (n, n), 1)
    src_b = jnp.where(src_partner, 1.0, 0.0).astype(bf16)
    dst_b = jnp.where(dst_partner, 1.0, 0.0).astype(bf16)
    power = dot_nn(src_b, dst_b).astype(bf16)
    total = jnp.where(row == col, 1.0, 0.0) + power.astype(f32)
    yield
    for _ in range(doublings - 1):
        power = dot_nn(power, power).astype(bf16)
        total = total + dot_nn(total.astype(bf16), power)
        yield
    orbit = total > 0.5
    lead_c = jnp.min(jnp.where(orbit, col, n), axis=1, keepdims=True)
    lead_r = jnp.min(jnp.where(orbit, row, n), axis=0, keepdims=True)
    other_c = jnp.sum(jnp.where(src_partner, lead_r, 0), axis=1, keepdims=True)
    other_r = jnp.sum(jnp.where(src_partner, lead_c, 0), axis=0, keepdims=True)
    return (lead_c < other_c).astype(jnp.int32), (lead_r < other_r).astype(jnp.int32)


def color_tables(dest, me):
    n = dest.shape[0]
    row = lax.broadcasted_iota(jnp.int32, (n, n), 0)
    col = lax.broadcasted_iota(jnp.int32, (n, n), 1)
    dest_t = jnp.transpose(dest.astype(f32)).astype(jnp.int32)
    owner_c, owner_r = dest >> 4, dest_t >> 4
    parity_same = (row & 1) == (col & 1)
    src_same = ((row >> 3) == (col >> 3)) & parity_same
    dst_same = (owner_c == owner_r) & parity_same
    rank_c = jnp.sum(jnp.where(dst_same & (col < row), 1, 0), axis=1, keepdims=True)
    rank_r = jnp.sum(jnp.where(dst_same & (row < col), 1, 0), axis=0, keepdims=True)
    src_partner = col == (row ^ 2)
    dst_partner = dst_same & (rank_r == (rank_c ^ 1))
    yield
    one_c, one_r = yield from split_colors(src_partner, dst_partner, 5)
    yield
    alike = (one_c == one_r) & (row != col)
    two_c, _ = yield from split_colors(src_same & alike, dst_same & alike, 4)
    yield
    color = jnp.broadcast_to(2 * one_c + two_c, (n, n))
    src = row >> 3
    pair = (row & 7) >> 1
    half = row & 1
    even = half == 0
    mine = src == me
    turn, turn2 = me // 4, me // 8

    def pick(mask, value):
        return jnp.sum(jnp.where(mask, value, 0), axis=0, keepdims=True)

    rows = [
        pick(mine & even & (color == col), pair),
        pick(mine & even & (pair == col), color),
        pick(even & (color == turn2) & (owner_c == col), src),
        pick(even & (color == turn) & (src == col), owner_c),
        pick((owner_c == me) & ((dest & 15) == col), 2 * color + half + 1) - 1,
        pick((owner_c == me) & (2 * color + half == col), dest & 15),
        pick(even & (color == 2 + turn2) & (owner_c == col), src),
    ]
    rows += [jnp.zeros_like(rows[0])]
    return jnp.concatenate(rows, axis=0)


PLANES = 8
ROWS = 160
PIECE = 256
ARRIVALS = PLANES - 1
WINDOW = 384
LOG2E = 1.4426950408889634


def softmax_over_rows(scores, allowed, scale):
    masked = jnp.where(allowed, scores, -jnp.inf)
    top = jnp.max(masked, axis=0, keepdims=True)
    terms = jnp.exp2((masked - top) * (scale * LOG2E))
    return terms * (1.0 / jnp.sum(terms, axis=0, keepdims=True))


def kernel(
    image_hbm,
    dest_hbm,
    kimg_hbm,
    seen_hbm,
    gain_hbm,
    qg_hbm,
    kg_hbm,
    x_hbm,
    qkv_hbm,
    out_hbm,
    kv_hbm,
    q_hbm,
    og_hbm,
    att_hbm,
    back_hbm,
    tab_hbm,
    image_ref,
    dest_ref,
    kimg_ref,
    seen_ref,
    gain_ref,
    qg_ref,
    kg_ref,
    x_ref,
    own_out,
    own_qkv,
    q_ref,
    og_ref,
    att_ref,
    dest_tile,
    every,
    tab_tile,
    tab_ref,
    seen_rows,
    weight,
    out_parts,
    out_ref,
    kv_ref,
    normed,
    summed,
    mixed,
    att,
    hidden,
    pay,
    qn,
    gkv,
    got1,
    out2,
    got2,
    out3,
    got3,
    out4,
    local_sem,
    dest_sem,
    own_sem,
    kv_sem,
    z_send,
    z_recv,
    o_send,
    o_recv,
    r_send,
    r_recv,
    m_send,
    m_recv,
    ro_send,
    ro_recv,
    mo_send,
    mo_recv,
    oo_sem,
    att_sem,
    own_back,
    f_send,
    f_recv,
    send_sem,
    recv_sem,
):
    pairs_here, span, vis = x_ref.shape
    tokens = pairs_here * span
    e, q, m = lax.axis_index("enc"), lax.axis_index("seq"), lax.axis_index("mp")
    other = 1 - m
    d = 1 - 2 * m
    stride = 1 + 3 * m
    pos = lax.rem(q // stride, 4)
    ring = q - pos * stride
    left, right, far = lax.rem(pos + 3, 4), lax.rem(pos + 1, 4), lax.rem(pos + 2, 4)
    ahead, behind = lax.rem(e + d + PLANES, PLANES), lax.rem(e - d + PLANES, PLANES)
    to_left, to_right = {"seq": ring + left * stride}, {"seq": ring + right * stride}
    to_ahead, to_behind, to_mate = {"enc": ahead}, {"enc": behind}, {"mp": other}

    def remote(source, target, send, recv, device):
        pltpu.make_async_remote_copy(
            src_ref=source,
            dst_ref=target,
            send_sem=send,
            recv_sem=recv,
            device_id=device,
            device_id_type=MESH,
        ).start()

    def done(view, sem):
        pltpu.make_async_copy(view, view, sem).wait()

    half_rows = ROWS // 2
    own_rows = pl.ds(pl.multiple_of(m * half_rows, half_rows), half_rows)
    mate_rows = pl.ds(pl.multiple_of(other * half_rows, half_rows), half_rows)
    kv_half = kv_hbm.shape[0]
    kv_rows = pl.ds(pl.multiple_of(m * kv_half, kv_half), kv_half)
    copies = [
        pltpu.make_async_copy(source, target, local_sem.at[index])
        for index, (source, target) in enumerate(
            (
                (qkv_hbm, own_qkv),
                (x_hbm, x_ref),
                (out_hbm, own_out),
                (kv_hbm, kv_ref.at[kv_rows]),
                (q_hbm, q_ref),
                (og_hbm, og_ref),
                (tab_tile, tab_ref),
                (tab_tile, tab_hbm),
                (dest_hbm, dest_ref),
                (seen_hbm, seen_ref),
                (gain_hbm, gain_ref),
                (image_hbm, image_ref),
                (kimg_hbm, kimg_ref),
                (qg_hbm, qg_ref),
                (kg_hbm, kg_ref),
            )
        )
    ]
    qkv_copy, x_copy, out_copy, kv_copy, q_copy, og_copy, tab_copy, tab_out = copies[:8]
    dest_copy, seen_copy, gain_copy = copies[8:11]
    late = copies[11:]
    for copy in [qkv_copy] + copies[8:] + copies[1:6]:
        copy.start()

    barrier = pltpu.get_barrier_semaphore()

    def hello(step, carry):
        pl.semaphore_signal(
            barrier, inc=1, device_id={"seq": lax.rem(q + step, PEERS)}, device_id_type=MESH
        )
        return carry

    lax.fori_loop(1, PEERS, hello, 0)
    for device in (to_ahead, to_behind, to_mate):
        pl.semaphore_signal(barrier, inc=1, device_id=device, device_id_type=MESH)

    sub = lax.broadcasted_iota(jnp.int32, (8, 128), 0)
    lane = lax.broadcasted_iota(jnp.int32, (8, 128), 1)
    tile = jnp.zeros((8, 128), jnp.int32)
    for copy in (dest_copy, seen_copy, gain_copy):
        copy.wait()
    for block in range(8):
        tile = jnp.where(sub == block, dest_ref[block], tile)
    dest_tile[...] = tile
    every[q] = tile
    spread = jnp.where(lane // LEN == sub, seen_ref[...].astype(f32), 0.0).astype(bf16)
    wide = (128, SHARED * LEN)
    place = lax.rem(lax.broadcasted_iota(jnp.int32, wide, 0), LEN) == lax.rem(
        lax.broadcasted_iota(jnp.int32, wide, 1), LEN
    )
    seen_rows[...] = dot_nn(spread, jnp.where(place, 1.0, 0.0).astype(bf16)).astype(jnp.int32)
    gain = jnp.concatenate([gain_ref[t : t + 1, :] for t in range(vis // 128)], axis=1)
    out_copy.wait()
    have = own_out.shape[0]
    for place in range(4):
        at = min(place * WINDOW, vis - WINDOW)
        out_parts[m, e, place, 0:have, :] = own_out[:, at : at + WINDOW]
    qkv_copy.wait()
    for p in range(8):
        count = min(PIECE, own_qkv.shape[1] - p * PIECE)
        weight[p, e, own_rows, 0:count] = own_qkv[:, p * PIECE : p * PIECE + count]
    pl.semaphore_wait(barrier, PEERS + 2)

    mine = 4 * m + pos

    def side(core):
        return pl.ds(4 * core, 4)

    for which, core in ((0, other), (1, m)):
        view = weight.at[side(core), e, own_rows]
        remote(view, view, own_sem.at[0, which], own_sem.at[1, which], to_mate)

    def send_z(plane, which, arrival):
        view = weight.at[mine, plane, mate_rows if which else own_rows]
        device = to_behind if arrival % 2 else to_ahead
        remote(view, view, z_send.at[arrival, which], z_recv.at[arrival, which], device)

    send_z(e, 0, 0)
    send_z(e, 0, 1)
    view = out_parts.at[m, e]
    remote(view, view, oo_sem.at[0], oo_sem.at[1], to_mate)

    def send_dest(step, carry):
        peer = lax.rem(q + step, PEERS)
        remote(dest_tile, every.at[q], dest_sem.at[0], dest_sem.at[1], {"seq": peer})
        return carry

    lax.fori_loop(1, PEERS, send_dest, 0)
    done(weight.at[side(m), e, mate_rows], own_sem.at[1, 0])
    send_z(e, 1, 0)
    send_z(e, 1, 1)
    kv_there = kv_ref.at[kv_rows]

    def send_out(plane, arrival):
        view = out_parts.at[m, plane, pos]
        device = to_behind if arrival % 2 else to_ahead
        remote(view, view, o_send.at[arrival], o_recv.at[arrival], device)

    def plane_of(arrival):
        hops = arrival // 2 + 1
        if arrival % 2 == 0:
            return lax.rem(e - d * hops + PLANES, PLANES)
        return lax.rem(e + d * hops + PLANES, PLANES)

    def piece(k, place):
        return weight.at[4 * m + place, plane_of(k)]

    def part(k, place, which):
        return weight.at[4 * m + place, plane_of(k), pl.ds(which * half_rows, half_rows)]

    width = VHEADS * VHEAD

    def norm_jobs():
        x_copy.wait()
        for t in range(tokens // 64):
            rows = slice(t * 64, t * 64 + 64)
            values = x_ref[t // 2, t % 2 * 64 : t % 2 * 64 + 64, :].astype(f32)
            center = values - jnp.mean(values, axis=-1, keepdims=True)
            spread = jnp.mean(center * center, axis=-1, keepdims=True)
            result = (center * lax.rsqrt(spread + EPS) * gain).astype(bf16)
            for plane in range(PLANES):
                normed[plane, rows, :] = result[:, plane * ROWS : (plane + 1) * ROWS]
            yield

    def table_jobs():
        wait_all(every, dest_sem.at[1])
        tab_tile[...] = yield from color_tables(every[...].reshape(PEERS * 8, 128), q)
        tab_copy.start()
        tab_out.start()

    def add_plane(plane, mode, p):
        count = min(PIECE, 3 * width - p * PIECE)
        cols = slice(p * PIECE, p * PIECE + count)
        found = dot_nn(normed[plane], weight[p, plane, :, 0:count])
        if mode == 0:
            summed[:, cols] = found
        elif mode == 1:
            summed[:, cols] += found
        else:
            total = (summed[:, cols] + found).astype(bf16)
            mixed[:, :, cols] = total.reshape(PAIRS, span, count)

    def plane_jobs(k):
        if k < 0:
            done(weight.at[side(other), e, mate_rows], own_sem.at[1, 1])
            plane = e
        else:
            same = k ^ 1 if k < ARRIVALS - 1 else k
            done(weight.at[side(m), e], m_recv.at[same])
            plane = plane_of(k)
        mode = 0 if k < 0 else 1 if k < ARRIVALS - 1 else 2
        for p in range(8):
            add_plane(plane, mode, p)
            if p % 3 == 2:
                yield
        yield

    def query_jobs():
        q_copy.wait()
        for copy in late:
            copy.wait()
        for g in range(KVHEADS):
            block = q_ref[:, g * SHARED * HEAD : (g + 1) * SHARED * HEAD]
            for hh in range(SHARED):
                x = block[:, hh * HEAD : (hh + 1) * HEAD].astype(f32)
                inv = lax.rsqrt(jnp.mean(x * x, axis=-1, keepdims=True) + EPS)
                y = (x * inv * qg_ref[...]).astype(bf16)
                for s in range(CAP):
                    qn[g, s, hh * LEN : (hh + 1) * LEN, :] = y[s * LEN : (s + 1) * LEN, :]
            yield

    def out_jobs(k):
        if k < 0:
            plane = e
            done(out_parts.at[m, e], oo_sem.at[1])
        else:
            plane = plane_of(k)
            done(out_parts.at[m, e], mo_recv.at[k ^ 1 if k < ARRIVALS - 1 else k])
        both = []
        for core in range(2):
            parts = [out_parts[core, plane, place, 0:have, :] for place in range(4)]
            parts[3] = parts[3][:, 4 * WINDOW - vis :]
            both.append(jnp.concatenate(parts, axis=1).astype(f32))
        rows = pl.ds(pl.multiple_of(2 * have * plane, 2 * have), 2 * have)
        out_ref[rows, :] = jnp.concatenate(both, axis=0).astype(bf16)
        yield

    queue = [norm_jobs(), table_jobs(), plane_jobs(-1), query_jobs()]

    def pump(steps):
        while queue and steps > 0:
            try:
                next(queue[0])
                steps -= 1
            except StopIteration:
                queue.pop(0)

    send_out(e, 0)
    send_out(e, 1)
    remote(kv_hbm, kv_there, kv_sem.at[0], kv_sem.at[1], to_mate)
    pump(2)
    hops = ((0, 1), (2, 3), (4, 5), (6,))
    for t in range(len(hops) + 2):
        if t < len(hops):
            for which in range(2):
                for k in hops[t]:
                    rows = mate_rows if which else own_rows
                    done(weight.at[mine, plane_of(k), rows], z_recv.at[k, which])
                    if k + 2 < ARRIVALS:
                        send_z(plane_of(k), which, k + 2)
            for k in hops[t]:
                view = piece(k, pos)
                remote(view, view, r_send.at[k, 0], r_recv.at[k, 0], to_right)
                remote(view, view, r_send.at[k, 1], r_recv.at[k, 1], to_left)
            for k in hops[t]:
                view = out_parts.at[m, plane_of(k), pos]
                done(view, o_recv.at[k])
                if k + 2 < ARRIVALS:
                    send_out(plane_of(k), k + 2)
                remote(view, view, ro_send.at[k, 0], ro_recv.at[k, 0], to_right)
                remote(view, view, ro_send.at[k, 1], ro_recv.at[k, 1], to_left)
        pump(2)
        if 0 <= t - 1 < len(hops):
            for k in hops[t - 1]:
                view = part(k, left, 0)
                done(piece(k, left), r_recv.at[k, 0])
                remote(view, view, r_send.at[k, 2], r_recv.at[k, 2], to_right)
                view = part(k, right, 1)
                done(piece(k, right), r_recv.at[k, 1])
                remote(view, view, r_send.at[k, 3], r_recv.at[k, 3], to_left)
            for k in hops[t - 1]:
                from_left = out_parts.at[m, plane_of(k), left]
                from_right = out_parts.at[m, plane_of(k), right]
                done(from_left, ro_recv.at[k, 0])
                done(from_right, ro_recv.at[k, 1])
                if k % 2 == 0:
                    remote(from_left, from_left, ro_send.at[k, 2], ro_recv.at[k, 2], to_right)
                else:
                    remote(from_right, from_right, ro_send.at[k, 2], ro_recv.at[k, 2], to_left)
        pump(2)
        if 0 <= t - 2 < len(hops):
            for k in hops[t - 2]:
                done(part(k, far, 0), r_recv.at[k, 2])
                done(part(k, far, 1), r_recv.at[k, 3])
                view = weight.at[side(m), plane_of(k)]
                remote(view, view, m_send.at[k], m_recv.at[k], to_mate)
            for k in hops[t - 2]:
                done(out_parts.at[m, plane_of(k), far], ro_recv.at[k, 2])
                view = out_parts.at[m, plane_of(k)]
                remote(view, view, mo_send.at[k], mo_recv.at[k], to_mate)
        pump(2)
        if t == 1:
            queue.append(out_jobs(-1))
        if 0 <= t - 2 < len(hops):
            queue.extend(plane_jobs(k) for k in hops[t - 2])
        if 0 <= t - 3 < len(hops):
            queue.extend(out_jobs(k) for k in hops[t - 3])
    pump(1000)
    queue.append(out_jobs(ARRIVALS - 1))

    row = lax.broadcasted_iota(jnp.int32, (span, span), 0)
    col = lax.broadcasted_iota(jnp.int32, (span, span), 1)
    near = (row // BLK) == (col // BLK)

    def window(head):
        first, last = head * VHEAD // 128, ((head + 1) * VHEAD - 1) // 128
        return first, last, first * 128, (last - first + 1) * 128

    def attend_pair(c):
        pair = tab_ref[0, c] & 3
        allowed = near | (image_ref[2 * pair] == image_ref[2 * pair + 1])
        insides, scores = [], []
        for head in range(VHEADS):
            _, _, base, cut = window(head)
            lanes = lax.broadcasted_iota(jnp.int32, (span, cut), 1) + base
            inside = (lanes >= head * VHEAD) & (lanes < (head + 1) * VHEAD)
            query = jnp.where(inside, mixed[pair, :, base : base + cut], jnp.zeros((), bf16))
            key = mixed[pair, :, width + base : width + base + cut]
            insides.append(inside)
            scores.append(dot_nt(key, query))
        weights = [
            softmax_over_rows(found, allowed, 1.0 / math.sqrt(VHEAD)).astype(bf16)
            for found in scores
        ]
        tiles = [None] * (width // 128)
        for head in range(VHEADS):
            first, last, base, cut = window(head)
            value = mixed[pair, :, 2 * width + base : 2 * width + base + cut]
            result = dot_tn(weights[head], value)
            for t in range(first, last + 1):
                at = (t - first) * 128
                found = result[:, at : at + 128]
                if tiles[t] is not None:
                    found = jnp.where(insides[head][:, at : at + 128], found, tiles[t])
                tiles[t] = found
        att[c] = jnp.concatenate(tiles, axis=1).astype(bf16)

    half = KVHEADS * HEAD
    tab_copy.wait()
    for a in range(2):
        pairs = (2 * a, 2 * a + 1)

        def attend_pairs(c, carry):
            attend_pair(c)
            return carry

        lax.fori_loop(pairs[0], pairs[1] + 1, attend_pairs, 0)
        if a == 0:
            pump(1000)
        attended = jnp.concatenate([att[c] for c in pairs], axis=0)

        def project(t, carry):
            cols = pl.ds(pl.multiple_of(t * 256, 256), 256)
            tokens_in = jnp.concatenate(
                [x_ref[tab_ref[0, c] & 3, :, cols] for c in pairs], axis=0
            )
            total = tokens_in.astype(f32) + dot_nn(attended, out_ref[:, cols])
            hidden[a, :, cols] = total.astype(bf16)
            return carry

        lax.fori_loop(0, vis // 256, project, 0)
        if a == 0:
            kv_copy.wait()
            done(kv_there, kv_sem.at[1])
        for b in range(GROUPS):
            for t in range(GROUP):
                at = (b * GROUP + t) * HEAD
                both = jnp.concatenate(
                    [kv_ref[:, at : at + HEAD], kv_ref[:, half + at : half + at + HEAD]], axis=1
                )
                pay[a][b][:, :, t * 2 * HEAD : (t + 1) * 2 * HEAD] = (
                    dot_nn(hidden[a], both).astype(bf16).reshape(PEERS, BLK // 4, 2 * HEAD)
                )
            exchange(pay[a][b], got1[a][b], q, f_send.at[0, a, b], f_recv.at[0, a, b])

    og_copy.wait()

    def shuffle(got, out, table):
        def body(index, carry):
            out[index] = got[tab_ref[table, index] & 15]
            return carry

        lax.fori_loop(0, PEERS, body, 0)

    def relay(a, b):
        wait_all(got1[a][b], f_recv.at[0, a, b])
        shuffle(got1[a][b], out2[a][b], 6 if a else 2)
        exchange(out2[a][b], got2[b].at[pl.ds(a * PEERS, PEERS)], q, f_send.at[1, a, b], f_recv.at[1, a, b])

    def give_back(h):
        wait_all(got3[h], recv_sem.at[0, h])
        shuffle(got3[h], out4[h], 3)
        exchange(out4[h], back_hbm.at[h], q, send_sem.at[1, h], recv_sem.at[1, h], own_back.at[h])

    def one(h, gi, s):
        g = h * PER + gi
        at = pl.multiple_of(gi * 2 * HEAD, 2 * HEAD)
        group = h * PER // GROUP
        from_col = pl.multiple_of((h * PER % GROUP + gi) * 2 * HEAD, 2 * HEAD)
        yield
        blocks, masks = [], []
        seen = seen_rows[pl.ds(s, 1), :]
        for kb in range(CAP):
            index = tab_ref[4, s * CAP + kb]
            start = 4 * (jnp.maximum(index, 0) & 7)
            block = got2[group][pl.ds(start, 4), :, pl.ds(from_col, 2 * HEAD)]
            blocks.append(
                jnp.where(index >= 0, block, jnp.zeros((), bf16)).reshape(BLK, 2 * HEAD)
            )
            masks.append(jnp.broadcast_to(kimg_ref[s, kb] < seen, (BLK, SHARED * LEN)))
        keyval = jnp.concatenate(blocks, axis=0)
        allowed = jnp.concatenate(masks, axis=0)
        keys = keyval[:, :HEAD].astype(f32)
        values = keyval[:, HEAD:]
        inv = lax.rsqrt(jnp.mean(keys * keys, axis=-1, keepdims=True) + EPS)
        kn = (keys * inv * kg_ref[...]).astype(bf16)
        yield
        queries = qn[g, s]
        rows = pl.ds(pl.multiple_of(s * LEN, LEN), LEN)
        cols = pl.ds(pl.multiple_of(g * SHARED * HEAD, SHARED * HEAD), SHARED * HEAD)
        grad_row = og_ref[rows, cols]
        grads = jnp.concatenate(
            [grad_row[:, hh * HEAD : (hh + 1) * HEAD] for hh in range(SHARED)], axis=0
        )
        scale = 1.0 / math.sqrt(HEAD)
        scores = dot_nt(kn, queries)
        grad_dot = dot_nt(values, grads)
        yield
        weights = softmax_over_rows(scores, allowed, scale)
        rounded = weights.astype(bf16)
        yield
        attended = dot_tn(rounded, values).astype(bf16)
        att_ref[rows, cols] = jnp.concatenate(
            [attended[hh * LEN : (hh + 1) * LEN, :] for hh in range(SHARED)], axis=1
        )
        grad_values = dot_nn(rounded, grads)
        yield
        delta = jnp.sum(weights * grad_dot, axis=0, keepdims=True)
        grad_scores = (weights * (grad_dot - delta) * scale).astype(bf16)
        yield
        gained = dot_nn(grad_scores, queries) * kg_ref[...]
        yield
        mean = jnp.mean(keys * gained, axis=-1, keepdims=True)
        grad_keys = inv * (gained - keys * inv * inv * mean)
        result = jnp.concatenate([grad_keys, grad_values], axis=1).astype(bf16)
        gkv[pl.ds(s * CAP, CAP), :, pl.ds(at, 2 * HEAD)] = result.reshape(CAP, BLK, 2 * HEAD)

    def attend(h):
        if h * PER % GROUP == 0:
            for a in range(2):
                wait_all(got2[h * PER // GROUP], f_recv.at[1, a, h * PER // GROUP])

        def body(gi, carry):
            running = [one(h, gi, s) for s in range(CAP)]
            while running:
                running = [steps for steps in running if next(steps, running) is not running]
            return carry

        lax.fori_loop(0, PER, body, 0)

        def pack(cb, carry):
            block = gkv[tab_ref[5, cb] & 15]
            out3[h][pl.ds(2 * cb, 2)] = block.reshape(2, BLK // 2, WIDE)
            return carry

        lax.fori_loop(0, 2 * PAIRS, pack, 0)
        exchange(out3[h], got3[h], q, send_sem.at[0, h], recv_sem.at[0, h])
        cols = slice(h * PER * SHARED * HEAD, (h + 1) * PER * SHARED * HEAD)
        pltpu.make_async_copy(att_ref.at[:, cols], att_hbm.at[:, cols], att_sem.at[h]).start()

    for b in range(GROUPS):
        for a in range(2):
            relay(a, b)
    for h in range(PIECES):
        attend(h)
        if h > 0:
            give_back(h - 1)
    give_back(PIECES - 1)
    for h in range(PIECES):
        wait_all(back_hbm.at[h], recv_sem.at[1, h])

    tab_out.wait()
    for h in range(PIECES):
        cols = slice(h * PER * SHARED * HEAD, (h + 1) * PER * SHARED * HEAD)
        pltpu.make_async_copy(att_ref.at[:, cols], att_hbm.at[:, cols], att_sem.at[h]).wait()
        pltpu.make_async_copy(out4[h].at[q], back_hbm.at[h, q], own_back.at[h]).wait()
        for phase in range(2):
            wait_all(got3[h], send_sem.at[phase, h])
    for a in range(2):
        for b in range(GROUPS):
            for phase in range(2):
                wait_all(got1[a][b], f_send.at[phase, a, b])
    wait_all(every, dest_sem.at[0])
    for which in range(2):
        done(weight.at[side(m), e, own_rows], own_sem.at[0, which])
    done(kv_there, kv_sem.at[0])
    done(out_parts.at[m, e], oo_sem.at[0])
    for k in range(ARRIVALS):
        for which in range(2):
            done(weight.at[mine, e, own_rows], z_send.at[k, which])
        done(out_parts.at[m, e, pos], o_send.at[k])
        done(out_parts.at[m, e], mo_send.at[k])
        for way in range(3):
            done(out_parts.at[m, e, pos], ro_send.at[k, way])
        for way in range(4):
            done(piece(k, pos) if way < 2 else part(k, pos, 0), r_send.at[k, way])
        done(weight.at[side(m), e], m_send.at[k])


def place_kernel(tab_hbm, att_hbm, back_hbm, att_out, kvg_out, tab_ref, att, back, kvg, sems):
    parts = 4
    rows = att.shape[0] // parts
    att_in, back_in, att_back, kvg_back = [], [], [], []
    for t in range(parts):
        view = pl.ds(t * rows, rows)
        att_in.append(pltpu.make_async_copy(att_hbm.at[view], att.at[view], sems.at[0, t]))
        att_back.append(pltpu.make_async_copy(att.at[view], att_out.at[view], sems.at[1, t]))
    for h in range(PIECES):
        back_in.append(pltpu.make_async_copy(back_hbm.at[h], back.at[h], sems.at[2, h]))
    for j in range(PAIRS):
        view = pl.ds(2 * j, 2)
        kvg_back.append(pltpu.make_async_copy(kvg.at[view], kvg_out.at[view], sems.at[3, j]))
    tab_in = pltpu.make_async_copy(tab_hbm, tab_ref, sems.at[4, 0])
    for copy in [tab_in] + back_in + att_in:
        copy.start()
    for copy in [tab_in] + back_in:
        copy.wait()
    half = KVHEADS * HEAD
    for j in range(PAIRS):
        color = tab_ref[1, j] & 3
        for g in range(KVHEADS):
            at = g % PER * 2 * HEAD
            block = back[g // PER, pl.ds(4 * color, 4), :, at : at + 2 * HEAD]
            block = block.reshape(2, BLK, 2 * HEAD)
            kvg[2 * j : 2 * j + 2, :, g * HEAD : (g + 1) * HEAD] = block[:, :, :HEAD]
            kvg[2 * j : 2 * j + 2, :, half + g * HEAD : half + (g + 1) * HEAD] = block[:, :, HEAD:]
        kvg_back[j].start()
    for coming, going in zip(att_in, att_back):
        coming.wait()
        going.start()
    for copy in kvg_back + att_back:
        copy.wait()


HBM = pl.BlockSpec(memory_space=pltpu.HBM)
LIMIT = 62 * 1024 * 1024


def local(
    images,
    vit_gain,
    vit_qkv,
    vit_out,
    kv_weight,
    queries,
    q_gain,
    k_gain,
    out_grad,
    block_image,
    block_dest,
    key_image,
    text_seen,
):
    enc_blocks, block_len, vis = images.shape
    tokens = enc_blocks * block_len
    buffers = [pltpu.VMEM((PEERS, BLK // 2, WIDE), bf16)] * PIECES
    chunks = [[pltpu.VMEM((PEERS, BLK // 4, GWIDE), bf16)] * GROUPS] * 2
    dma = pltpu.SemaphoreType.DMA
    attended, back, tables = pl.pallas_call(
        kernel,
        out_shape=(
            jax.ShapeDtypeStruct(queries.shape, bf16),
            jax.ShapeDtypeStruct((PIECES, PEERS, BLK // 2, WIDE), bf16),
            jax.ShapeDtypeStruct((8, 128), jnp.int32),
        ),
        in_specs=[HBM] * 13,
        out_specs=(HBM, HBM, HBM),
        scratch_shapes=[
            pltpu.SMEM(block_image.shape, jnp.int32),
            pltpu.SMEM(block_dest.shape, jnp.int32),
            pltpu.SMEM(key_image.shape, jnp.int32),
            pltpu.VMEM((1, CAP * LEN), jnp.int32),
            pltpu.VMEM((vis // 128, 128), f32),
            pltpu.VMEM((1, HEAD), f32),
            pltpu.VMEM((1, HEAD), f32),
            pltpu.VMEM((PAIRS, 2 * BLK, vis), bf16),
            pltpu.VMEM(vit_out.shape, bf16),
            pltpu.VMEM(vit_qkv.shape, bf16),
            pltpu.VMEM(queries.shape, bf16),
            pltpu.VMEM(queries.shape, bf16),
            pltpu.VMEM(queries.shape, bf16),
            pltpu.VMEM((8, 128), jnp.int32),
            pltpu.VMEM((PEERS, 8, 128), jnp.int32),
            pltpu.VMEM((8, 128), jnp.int32),
            pltpu.SMEM((8, 128), jnp.int32),
            pltpu.VMEM((8, SHARED * LEN), jnp.int32),
            pltpu.VMEM((8, PLANES, ROWS, PIECE), bf16),
            pltpu.VMEM((2, PLANES, 4, 48, WINDOW), bf16),
            pltpu.VMEM((VHEADS * VHEAD, vis), bf16),
            pltpu.VMEM((vis, 2 * KVHEADS * HEAD), bf16),
            pltpu.VMEM((PLANES, tokens, ROWS), bf16),
            pltpu.VMEM((tokens, 3 * VHEADS * VHEAD), f32),
            pltpu.VMEM((PAIRS, 2 * BLK, 3 * VHEADS * VHEAD), bf16),
            pltpu.VMEM((PAIRS, 2 * BLK, VHEADS * VHEAD), bf16),
            pltpu.VMEM((2, 4 * BLK, vis), bf16),
            chunks,
            pltpu.VMEM((KVHEADS, CAP, SHARED * LEN, HEAD), bf16),
            pltpu.VMEM((CAP * CAP, BLK, WIDE), bf16),
            chunks,
            chunks,
            [pltpu.VMEM((2 * PEERS, BLK // 4, GWIDE), bf16)] * GROUPS,
            buffers,
            buffers,
            buffers,
            dma((15,)),
            dma((2,)),
            dma((2, 2)),
            dma((2,)),
        ]
        + [dma((ARRIVALS, 2))] * 2
        + [dma((ARRIVALS,))] * 2
        + [dma((ARRIVALS, 4))] * 2
        + [dma((ARRIVALS,))] * 2
        + [dma((ARRIVALS, 3))] * 2
        + [dma((ARRIVALS,))] * 2
        + [dma((2,)), dma((PIECES,)), dma((PIECES,))]
        + [dma((2, 2, GROUPS))] * 2
        + [dma((2, PIECES))] * 2,
        compiler_params=pltpu.CompilerParams(
            collective_id=0, has_side_effects=True, vmem_limit_bytes=LIMIT
        ),
    )(
        block_image,
        block_dest,
        key_image,
        text_seen.reshape(1, -1),
        vit_gain.reshape(-1, 128),
        q_gain.reshape(1, HEAD),
        k_gain.reshape(1, HEAD),
        images.reshape(PAIRS, 2 * BLK, vis),
        vit_qkv,
        vit_out,
        kv_weight,
        queries,
        out_grad,
    )
    attended, kv_grad = pl.pallas_call(
        place_kernel,
        out_shape=(
            jax.ShapeDtypeStruct(queries.shape, bf16),
            jax.ShapeDtypeStruct((enc_blocks, block_len, 2 * KVHEADS * HEAD), bf16),
        ),
        in_specs=[HBM, HBM, HBM],
        out_specs=(HBM, HBM),
        scratch_shapes=[
            pltpu.SMEM((8, 128), jnp.int32),
            pltpu.VMEM(queries.shape, bf16),
            pltpu.VMEM((PIECES, PEERS, BLK // 2, WIDE), bf16),
            pltpu.VMEM((enc_blocks, block_len, 2 * KVHEADS * HEAD), bf16),
            dma((5, 4)),
        ],
        compiler_params=pltpu.CompilerParams(vmem_limit_bytes=LIMIT),
    )(tables, attended, back)
    return attended, kv_grad


def solution(mesh):
    everywhere = ("enc", "seq", "mp")
    placed = (
        P(everywhere, None, None),
        P(),
        P(("enc", "mp"), None),
        P(("enc", "mp"), None),
        P("mp", None),
        P(everywhere, None),
        P(),
        P(),
        P(everywhere, None),
        P(everywhere),
        P(everywhere),
        P(everywhere, None),
        P(everywhere),
    )
    return jax.shard_map(
        local,
        mesh=mesh,
        in_specs=placed,
        out_specs=(P(everywhere, None), P(everywhere, None, None)),
        check_vma=False,
    )
```
